512 devices in a mesh: gx: 4 (over y_hi), gy: 8 (over z), gz: 16 (over x, y_lo, core).
Axes of the slice: x: 4, y: 8 (y_hi: 4, y_lo: 2; y = y_hi * 2 + y_lo), z: 8, core: 2. Of those that a mesh axis runs over, the one named last changes fastest.
Arguments:
- fine_source_field: float32 [20, 80, 5120], P('gx', 'gy', 'gz'), may hold values from -6 to 6
- scaling: float32 [4, 16, 1024], P('gx', 'gy', 'gz'), may hold values from 0.5 to 2
- block_fine: float32 [125, 125], replicated, may hold values from -5 to 16, as said below
- block_mid: float32 [27, 27], replicated, may hold values from -5 to 32, as said below
- block_coarse: float32 [8, 8], replicated, may hold values from -1 to 4, as said below
Outputs:
- solution: float32 [20, 80, 5120], P('gx', 'gy', 'gz')
The draws below stay inside these ranges and needn't reach their ends.
Inputs may be any that keep to these rules, and one draw needn't show every extreme that they name: `block_fine`: symmetric positive definite. `block_mid`: symmetric positive definite. `block_coarse`: symmetric positive definite.
All inputs are finite; a program needn't handle non-finite values.
Results may differ from the reference program's by a relative error of at most 0.0001.
Values sent between devices are 32-bit elements; how exact they have to be, the bound alone decides.
No kernel may reach another device: no remote copies, remote signals or barrier semaphores. Data moves between devices by JAX's collectives and lax.ppermute only.
A program may use at most 64 MiB of HBM per device.

```python
import math
import jax
import jax.numpy as jnp
import numpy as np
from jax import lax

FINE_NODES_AXIS = 5
NM = 3
NC = 2
NU = 3
CSWEEPS = 4
ELEMENTS_X = 4
ELEMENTS_Y = 16
ELEMENTS_Z = 1024


def gll_nodes(points):
    if points == 5:
        nodes = np.array([-1.0, -math.sqrt(3.0 / 7.0), 0.0, math.sqrt(3.0 / 7.0), 1.0])
        quadrature_weight = np.array([0.1, 49.0 / 90.0, 32.0 / 45.0, 49.0 / 90.0, 0.1])
        return (nodes, quadrature_weight)
    if points == 3:
        return (np.array([-1.0, 0.0, 1.0]), np.array([1.0 / 3.0, 4.0 / 3.0, 1.0 / 3.0]))
    return (np.array([-1.0, 1.0]), np.array([1.0, 1.0]))


def derivative(nodes):
    count = nodes.shape[0]
    table = np.zeros((count, count))
    for column in range(count):
        for other in range(count):
            if other != column:
                term = np.full(count, 1.0 / (nodes[column] - nodes[other]))
                for third in range(count):
                    if third != column and third != other:
                        term = term * (nodes - nodes[third]) / (nodes[column] - nodes[third])
                table[:, column] += term
    return table


def stiffness_tables(points):
    nodes, quadrature_weight = gll_nodes(points)
    slope = derivative(nodes)
    mass = np.eye(points) * quadrature_weight[None, :]
    line = np.dot(slope.T, np.dot(mass, slope))
    first = np.kron(np.kron(line, mass), mass)
    second = np.kron(np.kron(mass, line), mass)
    third = np.kron(np.kron(mass, mass), line)
    volume = np.kron(np.kron(quadrature_weight, quadrature_weight), quadrature_weight)
    return (first, second, third, volume)


def element_block(key, points):
    coef_key, shift_key, node_key = jax.random.split(key, 3)
    coefs = jnp.exp(jax.random.uniform(coef_key, (3,), jnp.float32, math.log(0.5), math.log(2.0)))
    shift = jnp.exp(jax.random.uniform(shift_key, (), jnp.float32, math.log(0.05), math.log(0.3)))
    rough = jax.random.uniform(node_key, (points ** 3,), jnp.float32, 0.5, 1.5)
    first, second, third, volume = stiffness_tables(points)
    block = coefs[0] * jnp.asarray(first, jnp.float32)
    block = block + coefs[1] * jnp.asarray(second, jnp.float32)
    block = block + coefs[2] * jnp.asarray(third, jnp.float32)
    added = shift * rough * jnp.asarray(volume, jnp.float32)
    return block + jnp.eye(points ** 3, dtype=jnp.float32) * added[None, :]


def draw_block_fine(key, part):
    key = jax.random.fold_in(key, 11)
    return element_block(key, FINE_NODES_AXIS)


def draw_block_mid(key, part):
    key = jax.random.fold_in(key, 23)
    return element_block(key, NM)


def draw_block_coarse(key, part):
    key = jax.random.fold_in(key, 37)
    return element_block(key, NC)


def level_of(stream_key, extent, cuts, low, top_value):
    gain, own = 1.0, jax.random.fold_in(stream_key, 6)
    for position, parts in cuts:
        heights = jnp.exp(jax.random.uniform(jax.random.fold_in(own, position), (parts,), jnp.float32, low / len(cuts), top_value / len(cuts)))
        gain = gain * jnp.repeat(heights, extent[position] // parts).reshape([-1 if axis == position else 1 for axis in range(len(extent))])
    return gain


def centred(stream_key, extent, width, most, cuts=(), held_as=jnp.bfloat16):
    values = jax.random.normal(stream_key, extent, jnp.float32) * width
    if len(cuts) > 0:
        values = level_of(stream_key, extent, cuts, -0.22, 0.18) * values
    return jnp.clip(values, min=-most, max=most).astype(held_as)


def setup_inputs(seed: int = 0) -> dict:
    key_of = jax.random.split(jax.random.key(seed), 6)
    fine_source_field = centred(key_of[0], (FINE_NODES_AXIS * ELEMENTS_X, FINE_NODES_AXIS * ELEMENTS_Y, FINE_NODES_AXIS * ELEMENTS_Z), 1.0, 6.0, ((0, 4), (1, 8), (2, 16)), jnp.float32)
    scaling = jnp.clip(jnp.exp(math.log(2.0) - 1.3862944 * jax.random.uniform(key_of[1], (ELEMENTS_X, ELEMENTS_Y, ELEMENTS_Z), jnp.float32) ** level_of(key_of[1], (ELEMENTS_X, ELEMENTS_Y, ELEMENTS_Z), ((0, 4), (1, 8), (2, 16)), -0.2, 0.2)), 0.5, 2.0)
    block_fine = draw_block_fine(jax.random.fold_in(key_of[5], 71), 0)
    block_mid = draw_block_mid(jax.random.fold_in(key_of[5], 71), 0)
    block_coarse = draw_block_coarse(jax.random.fold_in(key_of[5], 71), 0)
    return {"fine_source_field": fine_source_field, "scaling": scaling, "block_fine": block_fine, "block_mid": block_mid, "block_coarse": block_coarse}


penalty = 0.5
relax = 0.7

def gll_points(points):
    if points == 5:
        return np.array([-1.0, -math.sqrt(3.0 / 7.0), 0.0, math.sqrt(3.0 / 7.0), 1.0])
    if points == 3:
        return np.array([-1.0, 0.0, 1.0])
    return np.array([-1.0, 1.0])

def lagrange(fine_points, coarse_points):
    fine_nodes = gll_points(fine_points)
    coarse_nodes = gll_points(coarse_points)
    table = np.ones((fine_points, coarse_points))
    for column in range(coarse_points):
        for other in range(coarse_points):
            if other != column:
                table[:, column] *= (fine_nodes - coarse_nodes[other]) / (coarse_nodes[column] - coarse_nodes[other])
    return table

def along(values, table, dimension):
    out_points, in_points = table.shape
    moved = jnp.moveaxis(values, dimension, 0)
    elements = moved.shape[0] // in_points
    grouped = moved.reshape(elements, in_points, -1)
    mapped = jnp.einsum('oi,eir->eor', table, grouped, precision=lax.Precision.HIGHEST)
    mapped = mapped.reshape((elements * out_points,) + moved.shape[1:])
    return jnp.moveaxis(mapped, 0, dimension)

def prolong(values, fine_points, coarse_points):
    table = jnp.asarray(lagrange(fine_points, coarse_points), jnp.float32)
    for dimension in range(3):
        values = along(values, table, dimension)
    return values

def restrict(values, fine_points, coarse_points):
    table = jnp.asarray(lagrange(fine_points, coarse_points).T, jnp.float32)
    for dimension in range(3):
        values = along(values, table, dimension)
    return values

def expand(scaling, points):
    return jnp.repeat(jnp.repeat(jnp.repeat(scaling, points, 0), points, 1), points, 2)

def blocks(values, matrix, points):
    sizes = values.shape
    count_x, count_y, count_z = (sizes[0] // points, sizes[1] // points, sizes[2] // points)
    grid = values.reshape(count_x, points, count_y, points, count_z, points)
    grid = grid.transpose(1, 3, 5, 0, 2, 4).reshape(points ** 3, -1)
    result = jnp.dot(matrix.astype(jnp.float32), grid.astype(jnp.float32), precision=lax.Precision.HIGHEST, preferred_element_type=jnp.float32)
    result = result.reshape(points, points, points, count_x, count_y, count_z)
    return result.transpose(3, 0, 4, 1, 5, 2).reshape(sizes)

def neighbour(padded, sizes, dimension, offset):
    starts = [1, 1, 1]
    starts[dimension] = offset
    return lax.slice(padded, starts, [starts[place] + sizes[place] for place in range(3)])

def jumps(values, padded, points):
    total = jnp.zeros_like(values)
    for dimension in range(3):
        length = values.shape[dimension]
        local = jnp.arange(length) % points
        form = [1, 1, 1]
        form[dimension] = length
        first = (local == 0).astype(values.dtype).reshape(form)
        last = (local == points - 1).astype(values.dtype).reshape(form)
        before = neighbour(padded, values.shape, dimension, 0)
        after = neighbour(padded, values.shape, dimension, 2)
        total = total + first * (values - before) + last * (values - after)
    return total

def operate(values, scale, matrix, points, pad_fn):
    scaled = scale * values
    padded = pad_fn(scaled)
    return scale * (blocks(scaled, matrix, points) + penalty * jumps(scaled, padded, points))

def smoother_inverse(matrix, points):
    edge = ((jnp.arange(points) == 0) | (jnp.arange(points) == points - 1)).astype(matrix.dtype)
    counted = (edge[:, None, None] + edge[None, :, None] + edge[None, None, :]).reshape(points ** 3)
    identity_mat = jnp.eye(points ** 3, dtype=matrix.dtype)
    full = matrix + penalty * identity_mat * counted[None, :]
    lower = jnp.linalg.cholesky(full)
    half = lax.linalg.triangular_solve(lower, identity_mat, left_side=True, lower=True)
    return jnp.dot(half.T, half, precision=lax.Precision.HIGHEST)

def sweeps(guess, rhs, scale, matrix, inverse, points, count, pad_fn, cold):
    current = guess
    for step in range(count):
        if cold and step == 0:
            remainder = rhs
        else:
            remainder = rhs - operate(current, scale, matrix, points, pad_fn)
        current = current + relax * blocks(remainder, inverse, points) / (scale * scale)
    return current

def zero_pad(values):
    return jnp.pad(values, 1)

def reference(fine_source_field, scaling, block_fine, block_mid, block_coarse):
    scale_fine = expand(scaling, FINE_NODES_AXIS)
    scale_mid = expand(scaling, NM)
    scale_coarse = expand(scaling, NC)
    inverse_fine = smoother_inverse(block_fine, FINE_NODES_AXIS)
    inverse_mid = smoother_inverse(block_mid, NM)
    coarsest_inverse = smoother_inverse(block_coarse, NC)
    fine_iter = sweeps(jnp.zeros_like(fine_source_field), fine_source_field, scale_fine, block_fine, inverse_fine, FINE_NODES_AXIS, NU, zero_pad, True)
    fine_rest = fine_source_field - operate(fine_iter, scale_fine, block_fine, FINE_NODES_AXIS, zero_pad)
    mid_rhs = restrict(fine_rest, FINE_NODES_AXIS, NM)
    mid_iter = sweeps(jnp.zeros_like(mid_rhs), mid_rhs, scale_mid, block_mid, inverse_mid, NM, NU, zero_pad, True)
    mid_rest = mid_rhs - operate(mid_iter, scale_mid, block_mid, NM, zero_pad)
    coarse_rhs = restrict(mid_rest, NM, NC)
    coarse_iter = sweeps(jnp.zeros_like(coarse_rhs), coarse_rhs, scale_coarse, block_coarse, coarsest_inverse, NC, CSWEEPS, zero_pad, True)
    mid_iter = mid_iter + prolong(coarse_iter, NM, NC)
    mid_iter = sweeps(mid_iter, mid_rhs, scale_mid, block_mid, inverse_mid, NM, NU, zero_pad, False)
    fine_iter = fine_iter + prolong(mid_iter, FINE_NODES_AXIS, NM)
    return sweeps(fine_iter, fine_source_field, scale_fine, block_fine, inverse_fine, FINE_NODES_AXIS, NU, zero_pad, False)
```

```python
import math

import jax
import jax.numpy as jnp
import numpy as np
from jax import lax
from jax.experimental import pallas as pl
from jax.experimental.pallas import tpu as pltpu
from jax.sharding import PartitionSpec as P

FINE = 5
MID = 3
COARSE = 2
CSWEEPS = 4
RADIUS = 15
WINDOW = 32
EX = 4
EY = 16
ROWS = WINDOW * EY
LANES = 128

f32 = jnp.float32
bf16 = jnp.bfloat16
HIGHEST = lax.Precision.HIGHEST
MIB = 1 << 20


def gll_points(points):
    if points == 5:
        return np.array([-1.0, -math.sqrt(3.0 / 7.0), 0.0, math.sqrt(3.0 / 7.0), 1.0])
    if points == 3:
        return np.array([-1.0, 0.0, 1.0])
    return np.array([-1.0, 1.0])


def lagrange(fine_points, coarse_points):
    fine_nodes = gll_points(fine_points)
    coarse_nodes = gll_points(coarse_points)
    table = np.ones((fine_points, coarse_points))
    for column in range(coarse_points):
        for other in range(coarse_points):
            if other != column:
                table[:, column] *= (fine_nodes - coarse_nodes[other]) / (
                    coarse_nodes[column] - coarse_nodes[other]
                )
    return table


def halves(table):
    table = np.asarray(table, np.float32)
    hi = table.astype(jnp.bfloat16)
    lo = (table - hi.astype(np.float32)).astype(jnp.bfloat16)
    return np.block([[hi, lo], [hi, np.zeros_like(lo)]])


def transfer_tables():
    fine_mid = np.kron(np.kron(lagrange(5, 3), lagrange(5, 3)), lagrange(5, 3))
    mid_coarse = np.kron(np.kron(lagrange(3, 2), lagrange(3, 2)), lagrange(3, 2))
    down, up = [], []
    for place in range(EX):
        table = np.zeros((LANES, LANES))
        table[:125, place * 32 : place * 32 + 27] = fine_mid
        down.append(halves(table))
        up.append(halves(table.T))
    middle = np.zeros((LANES, LANES))
    for place in range(EX):
        middle[place * 32 : place * 32 + 27, place * 32 : place * 32 + 8] = mid_coarse
    return np.stack(down), np.stack(up), halves(middle), halves(middle.T)


def spread_tables(count_z):
    tables = []
    for y in range(2):
        table = np.zeros((FINE * count_z, FINE * LANES), np.float32)
        for z in range(count_z):
            for k in range(FINE):
                table[z * FINE + k, k * LANES + y * count_z + z] = 1.0
        tables.append(table)
    return tables


def three_way(values):
    one = values.astype(bf16)
    rest = values - one.astype(f32)
    two = rest.astype(bf16)
    three = (rest - two.astype(f32)).astype(bf16)
    return jnp.concatenate([one, two, three], axis=0)


def pack_body(field_ref, scale_ref, table_ref, out_ref, above, below, nodes):
    for i in range(FINE):
        above[i * FINE : (i + 1) * FINE, :] = field_ref[i, 0:FINE, :]
        below[i * FINE : (i + 1) * FINE, :] = field_ref[i, FINE : 2 * FINE, :]
    spread = jnp.dot(three_way(above[...]), table_ref[0], preferred_element_type=f32)
    spread = spread + jnp.dot(three_way(below[...]), table_ref[1], preferred_element_type=f32)
    spread = spread[0:32] + spread[32:64] + spread[64:96]
    nodes[...] = jnp.zeros((LANES, LANES), f32)
    for k in range(FINE):
        nodes[pl.ds(k, FINE * FINE, stride=FINE), :] = spread[
            0 : FINE * FINE, k * LANES : (k + 1) * LANES
        ]
    out_ref[...] = (nodes[...] / scale_ref[...]).T


def pack(field, scale_row, tables):
    return pl.pallas_call(
        pack_body,
        out_shape=jax.ShapeDtypeStruct((LANES, LANES), f32),
        scratch_shapes=[
            pltpu.VMEM((32, field.shape[2]), f32),
            pltpu.VMEM((32, field.shape[2]), f32),
            pltpu.VMEM((LANES, LANES), f32),
        ],
        compiler_params=pltpu.CompilerParams(vmem_limit_bytes=8 * MIB),
        name="pack",
    )(field, scale_row, tables)


def unpack_body(back_ref, scale_ref, table_ref, out_ref, nodes):
    half = back_ref.shape[0] // 2
    upper = back_ref[pl.ds(0, half, stride=2), :]
    lower = back_ref[pl.ds(1, half, stride=2), :]
    nodes[...] = jnp.concatenate([upper, lower], axis=0).T / scale_ref[...]
    grouped = [nodes[pl.ds(k, FINE * FINE, stride=FINE), :] for k in range(FINE)]
    grouped = jnp.concatenate(grouped, axis=1)
    grouped = jnp.concatenate([grouped, jnp.zeros((7, FINE * LANES), f32)], axis=0)
    split = three_way(grouped)
    for y in range(2):
        lines = jnp.dot(split, table_ref[y], preferred_element_type=f32)
        lines = lines[0:32] + lines[32:64] + lines[64:96]
        for i in range(FINE):
            out_ref[i, y * FINE : (y + 1) * FINE, :] = lines[i * FINE : (i + 1) * FINE]


def unpack(back, scale_row, tables, shape):
    return pl.pallas_call(
        unpack_body,
        out_shape=jax.ShapeDtypeStruct(shape, f32),
        scratch_shapes=[pltpu.VMEM((LANES, LANES), f32)],
        compiler_params=pltpu.CompilerParams(vmem_limit_bytes=8 * MIB),
        name="unpack",
    )(back, scale_row, tables)


def window_body(own_ref, before_ref, after_ref, out_ref, line, *, count_z, parts):
    for y in range(2):
        line[y, 0:16, :] = before_ref[y]
        line[y, 16 : 16 + count_z, :] = own_ref[y * count_z : (y + 1) * count_z, :]
        line[y, 16 + count_z : 32 + count_z, :] = after_ref[y]
    for part in range(parts):
        for y in range(2):
            start = 16 + 2 * part - RADIUS
            out_ref[part, y * WINDOW : (y + 1) * WINDOW, :] = line[y, start : start + WINDOW, :]


def window(own, before, after, parts):
    count_z = own.shape[0] // 2

    def body(*refs):
        window_body(*refs, count_z=count_z, parts=parts)

    return pl.pallas_call(
        body,
        out_shape=jax.ShapeDtypeStruct((parts, 2 * WINDOW, LANES), f32),
        scratch_shapes=[pltpu.VMEM((2, count_z + 32, LANES), f32)],
        compiler_params=pltpu.CompilerParams(vmem_limit_bytes=8 * MIB),
        name="window",
    )(own, before, after)


def iota(shape, dimension):
    return lax.broadcasted_iota(jnp.int32, shape, dimension)


def shifted_block(ref, pad, points):
    nodes = points**3
    pad[...] = jnp.zeros((LANES, LANES), f32)
    pad[0:nodes, 0:nodes] = ref[...]
    lane, row = iota((LANES, LANES), 1), iota((LANES, LANES), 0)
    count = jnp.zeros((LANES, LANES), f32)
    for stride in (points * points, points, 1):
        index = (lane // stride) % points
        count = count + jnp.where((index == 0) | (index == points - 1), 0.5, 0.0)
    diagonal = jnp.where(lane < nodes, count, 1.0)
    return pad[...] + jnp.where(lane == row, diagonal, 0.0)


def invert(matrix, panels):
    lane, row = iota((LANES, LANES), 1), iota((LANES, LANES), 0)
    lane16, row16 = iota((16, LANES), 1), iota((16, LANES), 0)
    for panel in range(panels):
        top = panel * 16
        rows = matrix[top : top + 16, :]
        for step in range(16):
            pivot = top + step
            column = rows[:, pivot : pivot + 1]
            scale = 1.0 / rows[step : step + 1, pivot : pivot + 1]
            scaled = jnp.where(lane16[0:1] == pivot, scale, rows[step : step + 1, :] * scale)
            others = jnp.where(lane16 == pivot, 0.0, rows) - column * scaled
            rows = jnp.where(row16 == step, scaled, others)
        stacked = jnp.concatenate([rows] * 8, axis=0)
        inside = (lane >= top) & (lane < top + 16)
        update = jnp.dot(
            jnp.where(inside, matrix, 0.0), stacked, precision=HIGHEST, preferred_element_type=f32
        )
        matrix = jnp.where(
            (row >= top) & (row < top + 16), stacked, jnp.where(inside, 0.0, matrix) - update
        )
    return matrix


def repeated(matrix):
    lane, row = iota((LANES, LANES), 1), iota((LANES, LANES), 0)
    pick = jnp.where((row % 32 == lane) & (lane < 32), 1.0, 0.0)
    put = jnp.where((lane % 32 == row) & (row < 32), 1.0, 0.0)
    tall = jnp.dot(pick, matrix, precision=HIGHEST, preferred_element_type=f32)
    wide = jnp.dot(tall, put, precision=HIGHEST, preferred_element_type=f32)
    return jnp.where(row // 32 == lane // 32, wide, 0.0)


def inverses_body(fine_ref, mid_ref, coarse_ref, fine_out, mid_out, coarse_out, pad):
    coarse = invert(shifted_block(coarse_ref, pad, COARSE), 1)
    mid = invert(shifted_block(mid_ref, pad, MID), 2)
    fine = invert(shifted_block(fine_ref, pad, FINE), 8)
    fine_out[...] = 0.35 * fine
    mid_out[...] = 0.35 * repeated(mid)
    coarse_out[...] = 0.35 * repeated(coarse)


def inverses(block_fine, block_mid, block_coarse):
    square = jax.ShapeDtypeStruct((LANES, LANES), f32)
    return pl.pallas_call(
        inverses_body,
        out_shape=(square, square, square),
        scratch_shapes=[pltpu.VMEM((LANES, LANES), f32)],
        compiler_params=pltpu.CompilerParams(vmem_limit_bytes=8 * MIB),
        cost_estimate=pl.CostEstimate(
            flops=2_000_000_000, bytes_accessed=20_000_000, transcendentals=0
        ),
        name="inverses",
    )(block_fine, block_mid, block_coarse)


def two_way(values):
    hi = values.astype(bf16)
    lo = (values - hi.astype(f32)).astype(bf16)
    return jnp.concatenate([hi, lo], axis=1)


def two_way_table(table):
    hi = table.astype(bf16)
    lo = (table - hi.astype(f32)).astype(bf16)
    return jnp.concatenate(
        [jnp.concatenate([hi, lo], axis=1), jnp.concatenate([hi, jnp.zeros_like(lo)], axis=1)],
        axis=0,
    )


def times(values, table):
    result = jnp.dot(two_way(values), table, preferred_element_type=f32)
    return result[:, 0:LANES] + result[:, LANES : 2 * LANES]


class Faces:
    def __init__(self, points, in_lanes):
        nodes = points**3
        lane, row = iota((EY, LANES), 1), iota((EY, LANES), 0)
        local = lane % 32 if in_lanes else lane
        place = lane // 32
        self.turns = []
        for dimension, stride in enumerate((points * points, points, 1)):
            index = (local // stride) % points
            first = (index == 0) & (local < nodes)
            last = (index == points - 1) & (local < nodes)
            reach = (points - 1) * stride
            if dimension == 0 and in_lanes:
                first, last = first & (place > 0), last & (place < EX - 1)
                reach = reach - 32
            if dimension == 1:
                first, last = first & (row > 0), last & (row < EY - 1)
            self.turns.append((first[None], last[None], (-reach) % LANES, reach % LANES))

    def gather(self, pairs):
        total = None
        for (before, after), (first, last, down, up) in zip(pairs, self.turns):
            part = 0.0
            if after is not None:
                slabs = after.shape[0] // EY
                turned = pltpu.roll(after, up, 1).reshape(slabs, EY, LANES)
                part = jnp.where(last, turned, part)
            if before is not None:
                slabs = before.shape[0] // EY
                turned = pltpu.roll(before, down, 1).reshape(slabs, EY, LANES)
                part = jnp.where(first, turned, part)
            total = part if total is None else total + part
        return total.reshape(-1, LANES)


CHUNK = 8


def cuts(start, stop):
    count = -(-(stop - start) // CHUNK)
    edges = [start + (stop - start) * piece // count for piece in range(count + 1)]
    return list(zip(edges[:-1], edges[1:]))


def cycle_body(
    bounds_ref,
    recv_ref,
    fine_ref,
    mid_ref,
    coarse_ref,
    down_ref,
    up_ref,
    low_ref,
    high_ref,
    out_ref,
    start,
    ping,
    pong,
    left,
    mid_start,
    mid_ping,
    mid_pong,
    mid_left,
    mask,
):
    fine_faces = Faces(FINE, False)
    mid_faces = Faces(MID, True)
    coarse_faces = Faces(COARSE, True)
    fine_table = two_way_table(fine_ref[...])
    mid_table = two_way_table(mid_ref[...])
    coarse_table = two_way_table(coarse_ref[...])

    slab = iota((ROWS, LANES), 0) // EY
    mask[...] = jnp.where((slab >= bounds_ref[0]) & (slab < bounds_ref[1]), 1.0, 0.0)

    def at(x, a, b, offset=0):
        return slice(x * ROWS + a * EY + offset, x * ROWS + b * EY + offset)

    def fine_gather(ref, x, a, b):
        return fine_faces.gather(
            (
                (
                    ref[at(x - 1, a, b), :] if x > 0 else None,
                    ref[at(x + 1, a, b), :] if x < EX - 1 else None,
                ),
                (ref[at(x, a, b, -1), :], ref[at(x, a, b, 1), :]),
                (ref[at(x, a - 1, b - 1), :], ref[at(x, a + 1, b + 1), :]),
            )
        )

    def fine_sweep(source, target, a, b, keep):
        for x in range(EX):
            for c, d in cuts(a, b):
                rows = at(x, c, d)
                faces = fine_gather(source, x, c, d)
                if keep is not None:
                    left[rows, :] = left[rows, :] + keep * faces
                moved = 0.3 * source[rows, :] + start[rows, :] + times(faces, fine_table)
                target[rows, :] = moved * mask[at(0, c, d), :]

    for x in range(EX):
        for c, d in cuts(0, WINDOW):
            values = jnp.concatenate(
                [recv_ref[pl.ds(x * ROWS + z, EY, stride=WINDOW), :] for z in range(c, d)], axis=0
            )
            rows = at(x, c, d)
            left[rows, :] = 0.027 * values
            start[rows, :] = 2.0 * times(values, fine_table)

    fine_sweep(start, ping, 1, 31, -0.105)
    fine_sweep(ping, pong, 2, 30, -0.35)

    def mid_gather(faces, ref, a, b):
        here = ref[at(0, a, b), :]
        return faces.gather(
            (
                (here, here),
                (ref[at(0, a, b, -1), :], ref[at(0, a, b, 1), :]),
                (ref[at(0, a - 1, b - 1), :], ref[at(0, a + 1, b + 1), :]),
            )
        )

    for c, d in cuts(3, 29):
        total = None
        for x in range(EX):
            rest = left[at(x, c, d), :] + 0.5 * fine_gather(pong, x, c, d)
            part = times(rest, down_ref[x])
            total = part if total is None else total + part
        rows = at(0, c, d)
        total = total * mask[rows, :]
        mid_left[rows, :] = 0.027 * total
        mid_start[rows, :] = 2.0 * times(total, mid_table)

    def mid_sweep(faces, table, base, source, target, a, b, keep=None):
        for c, d in cuts(a, b):
            rows = at(0, c, d)
            values = mid_gather(faces, source, c, d)
            if keep is not None:
                mid_left[rows, :] = mid_left[rows, :] + keep * values
            moved = 0.3 * source[rows, :] + base[rows, :] + times(values, table)
            target[rows, :] = moved * mask[rows, :]

    mid_sweep(mid_faces, mid_table, mid_start, mid_start, mid_ping, 4, 28, -0.105)
    mid_sweep(mid_faces, mid_table, mid_start, mid_ping, mid_pong, 5, 27, -0.35)

    base = ping.at[0:ROWS]
    even = ping.at[ROWS : 2 * ROWS]
    odd = ping.at[2 * ROWS : 3 * ROWS]
    for c, d in cuts(6, 26):
        rows = at(0, c, d)
        rest = mid_left[rows, :] + 0.5 * mid_gather(mid_faces, mid_pong, c, d)
        low = times(rest * mask[rows, :], low_ref[...])
        base[rows, :] = 2.0 * times(low, coarse_table)
    mid_sweep(coarse_faces, coarse_table, base, base, even, 7, 25)
    mid_sweep(coarse_faces, coarse_table, base, even, odd, 8, 24)
    mid_sweep(coarse_faces, coarse_table, base, odd, even, 9, 23)

    for c, d in cuts(9, 23):
        rows = at(0, c, d)
        mid_pong[rows, :] = mid_pong[rows, :] + times(even[rows, :], high_ref[...])
    mid_sweep(mid_faces, mid_table, mid_start, mid_pong, mid_ping, 10, 22)
    mid_sweep(mid_faces, mid_table, mid_start, mid_ping, mid_pong, 11, 21)
    mid_sweep(mid_faces, mid_table, mid_start, mid_pong, mid_ping, 12, 20)

    lifted = two_way(mid_ping[at(0, 12, 20), :])
    for x in range(EX):
        rows = at(x, 12, 20)
        added = jnp.dot(lifted, up_ref[x], preferred_element_type=f32)
        added = added[:, 0:LANES] + added[:, LANES : 2 * LANES]
        pong[rows, :] = pong[rows, :] + added
    fine_sweep(pong, ping, 13, 19, None)
    fine_sweep(ping, pong, 14, 18, None)
    fine_sweep(pong, ping, 15, 17, None)

    for x in range(EX):
        for z in range(2):
            for y in range(2):
                values = ping[pl.ds(x * ROWS + (15 + z) * EY + y, 8, stride=2), :]
                out_ref[pl.ds(x * 32 + z * 2 + y, 8, stride=4), :] = values


def cycle(bounds, recv, fine, mid, coarse, down, up, low, high):
    big = pltpu.VMEM((EX * ROWS, LANES), f32)
    small = pltpu.VMEM((ROWS, LANES), f32)
    vmem = pl.BlockSpec(memory_space=pltpu.VMEM)
    return pl.pallas_call(
        cycle_body,
        out_shape=jax.ShapeDtypeStruct((LANES, LANES), f32),
        in_specs=[pl.BlockSpec(memory_space=pltpu.SMEM)] + [vmem] * 8,
        out_specs=vmem,
        scratch_shapes=[big, big, big, big, small, small, small, small, small],
        compiler_params=pltpu.CompilerParams(vmem_limit_bytes=32 * MIB),
        name="cycle",
    )(bounds, recv, fine, mid, coarse, down, up, low, high)


def per_device(fine_source_field, scaling, block_fine, block_mid, block_coarse):
    count_z = scaling.shape[2]
    parts = lax.axis_size("gx") * lax.axis_size("gy")
    groups = lax.axis_size("gz")
    down, up, low, high = transfer_tables()
    tables = np.stack(spread_tables(count_z)).astype(jnp.bfloat16)
    back_tables = np.ascontiguousarray(tables.transpose(0, 2, 1))
    scale_row = scaling.reshape(1, 2 * count_z)

    own = pack(fine_source_field, scale_row, tables)
    lines = own.reshape(2, count_z, LANES)
    before = lax.ppermute(lines[:, count_z - 16 :], "gz", [(i, i + 1) for i in range(groups - 1)])
    after = lax.ppermute(lines[:, :16], "gz", [(i + 1, i) for i in range(groups - 1)])
    chunks = window(own, before, after, parts)
    recv = lax.all_to_all(chunks, ("gx", "gy"), 0, 0, tiled=True)
    fine, mid, coarse = inverses(block_fine, block_mid, block_coarse)

    part = lax.axis_index("gx") * lax.axis_size("gy") + lax.axis_index("gy")
    first = lax.axis_index("gz") * count_z + 2 * part - RADIUS
    bounds = jnp.stack([jnp.maximum(0, -first), jnp.minimum(WINDOW, groups * count_z - first)])
    result = cycle(
        bounds.astype(jnp.int32),
        recv.reshape(EX * ROWS, LANES),
        fine,
        mid,
        coarse,
        down,
        up,
        low,
        high,
    )
    back = lax.all_to_all(result.reshape(parts, 4, LANES), ("gx", "gy"), 0, 0, tiled=True)
    return unpack(back.reshape(LANES, LANES), scale_row, back_tables, fine_source_field.shape)


def solution(mesh):
    in_specs = (P("gx", "gy", "gz"), P("gx", "gy", "gz"), P(), P(), P())
    out_specs = P("gx", "gy", "gz")
    return jax.shard_map(
        per_device, mesh=mesh, in_specs=in_specs, out_specs=out_specs, check_vma=False
    )
```

```python
import math

import jax
import jax.numpy as jnp
import numpy as np
from jax import lax
from jax.experimental import pallas as pl
from jax.experimental.pallas import tpu as pltpu
from jax.sharding import PartitionSpec as P

FINE = 5
MID = 3
COARSE = 2
CSWEEPS = 4
RADIUS = 15
HALO = 16
OWN = 4
WINDOW = OWN + 2 * RADIUS
EX = 4
EY = 16
HALF = EY // 2
LANES = 128

f32 = jnp.float32
bf16 = jnp.bfloat16
HIGHEST = lax.Precision.HIGHEST
MIB = 1 << 20


def gll_points(points):
    if points == 5:
        return np.array([-1.0, -math.sqrt(3.0 / 7.0), 0.0, math.sqrt(3.0 / 7.0), 1.0])
    if points == 3:
        return np.array([-1.0, 0.0, 1.0])
    return np.array([-1.0, 1.0])


def lagrange(fine_points, coarse_points):
    fine_nodes = gll_points(fine_points)
    coarse_nodes = gll_points(coarse_points)
    table = np.ones((fine_points, coarse_points))
    for column in range(coarse_points):
        for other in range(coarse_points):
            if other != column:
                table[:, column] *= (fine_nodes - coarse_nodes[other]) / (
                    coarse_nodes[column] - coarse_nodes[other]
                )
    return table


def halves(table):
    table = np.asarray(table, np.float32)
    hi = table.astype(jnp.bfloat16)
    lo = (table - hi.astype(np.float32)).astype(jnp.bfloat16)
    return np.block([[hi, lo], [hi, np.zeros_like(lo)]])


def transfer_tables():
    fine_mid = np.kron(np.kron(lagrange(5, 3), lagrange(5, 3)), lagrange(5, 3))
    mid_coarse = np.kron(np.kron(lagrange(3, 2), lagrange(3, 2)), lagrange(3, 2))
    down, up = [], []
    for place in range(EX):
        table = np.zeros((LANES, LANES))
        table[:125, place * 32 : place * 32 + 27] = fine_mid
        down.append(halves(table))
        up.append(halves(table.T))
    middle = np.zeros((LANES, LANES))
    for place in range(EX):
        middle[place * 32 : place * 32 + 27, place * 32 : place * 32 + 8] = mid_coarse
    return np.stack(down), np.stack(up), halves(middle), halves(middle.T)


def iota(shape, dimension):
    return lax.broadcasted_iota(jnp.int32, shape, dimension)


def three_way(values):
    one = values.astype(bf16)
    rest = values - one.astype(f32)
    two = rest.astype(bf16)
    three = (rest - two.astype(f32)).astype(bf16)
    return jnp.concatenate([one, two, three], axis=0)


def place_of(lane, y):
    i, j, k = lane // (FINE * FINE), (lane // FINE) % FINE, lane % FINE
    return jnp.where(lane < FINE**3, k * LANES + i * 2 * FINE + y * FINE + j, -1)


def pack_body(core_ref, field_ref, scale_ref, own_ref, edge_ref, lines, turned, *, count_z):
    lines[...] = jnp.zeros_like(lines)
    for i in range(FINE):
        lines[i * 2 * FINE : (i + 1) * 2 * FINE, 0 : count_z * FINE] = field_ref[i]
    for part in range(lines.shape[1] // LANES):
        lanes = slice(part * LANES, (part + 1) * LANES)
        turned[lanes, :] = lines[:, lanes].T
    lane = iota((1, 2 * LANES), 1)
    place = place_of(lane % LANES, lane // LANES)
    table = jnp.where(iota((FINE * LANES, 2 * LANES), 0) == place, 1.0, 0.0).astype(bf16)
    values = [turned[pl.ds(k, count_z, stride=FINE), :] for k in range(FINE)]
    nodes = jnp.dot(
        three_way(jnp.concatenate(values, axis=1)), table, preferred_element_type=f32
    )
    nodes = nodes[0:count_z] + nodes[count_z : 2 * count_z] + nodes[2 * count_z : 3 * count_z]
    scale = scale_ref[0].T
    for y in range(2):
        own_ref[y] = nodes[:, y * LANES : (y + 1) * LANES] / scale[:, y : y + 1]
    start = pl.multiple_of(core_ref[0] * (count_z - HALO), HALO)
    for y in range(2):
        edge_ref[y] = own_ref[y, pl.ds(start, HALO), :]


def pack(core, field, scaling):
    count_z = scaling.shape[2]
    width = -(-count_z * FINE // LANES) * LANES

    def body(*refs):
        pack_body(*refs, count_z=count_z)

    vmem = pl.BlockSpec(memory_space=pltpu.VMEM)
    return pl.pallas_call(
        body,
        out_shape=(
            jax.ShapeDtypeStruct((2, count_z, LANES), f32),
            jax.ShapeDtypeStruct((2, HALO, LANES), f32),
        ),
        in_specs=[pl.BlockSpec(memory_space=pltpu.SMEM), vmem, vmem],
        out_specs=(vmem, vmem),
        scratch_shapes=[pltpu.VMEM((LANES, width), f32), pltpu.VMEM((width, LANES), f32)],
        compiler_params=pltpu.CompilerParams(vmem_limit_bytes=8 * MIB),
        name="pack",
    )(core, field, scaling)


def join_body(core_ref, own_ref, halo_ref, mine_ref, give_ref, *, count_z):
    core = core_ref[0]
    own_at = pl.multiple_of((1 - core) * HALO, HALO)
    halo_at = pl.multiple_of(core * count_z, HALO)
    for ref, y in ((mine_ref, core), (give_ref, 1 - core)):
        ref[pl.ds(own_at, count_z), :] = own_ref[y]
        ref[pl.ds(halo_at, HALO), :] = halo_ref[y]


def join(core, own, halo):
    count_z = own.shape[1]

    def body(*refs):
        join_body(*refs, count_z=count_z)

    vmem = pl.BlockSpec(memory_space=pltpu.VMEM)
    line = jax.ShapeDtypeStruct((count_z + HALO, LANES), f32)
    return pl.pallas_call(
        body,
        out_shape=(line, line),
        in_specs=[pl.BlockSpec(memory_space=pltpu.SMEM), vmem, vmem],
        out_specs=(vmem, vmem),
        compiler_params=pltpu.CompilerParams(vmem_limit_bytes=8 * MIB),
        name="join",
    )(core, own, halo)


def window_body(core_ref, mine_ref, other_ref, out_ref, line, *, parts):
    length = mine_ref.shape[0]
    core = core_ref[0]
    line[pl.ds(pl.multiple_of(core * length, HALO), length), :] = mine_ref[...]
    line[pl.ds(pl.multiple_of((1 - core) * length, HALO), length), :] = other_ref[...]
    for part in range(parts):
        start = HALO - RADIUS + OWN * part
        out_ref[part * WINDOW : (part + 1) * WINDOW, :] = line[start : start + WINDOW, :]


def window(core, mine, other, parts):
    def body(*refs):
        window_body(*refs, parts=parts)

    vmem = pl.BlockSpec(memory_space=pltpu.VMEM)
    return pl.pallas_call(
        body,
        out_shape=jax.ShapeDtypeStruct((parts * WINDOW, LANES), f32),
        in_specs=[pl.BlockSpec(memory_space=pltpu.SMEM), vmem, vmem],
        out_specs=vmem,
        scratch_shapes=[pltpu.VMEM((2 * mine.shape[0], LANES), f32)],
        compiler_params=pltpu.CompilerParams(vmem_limit_bytes=8 * MIB),
        name="window",
    )(core, mine, other)


def unpack_body(core_ref, back_ref, scale_ref, out_ref, turned, *, count_z):
    scale = scale_ref[0].T
    base = core_ref[0] * (2 * count_z)
    rows = [
        back_ref[pl.ds(base + y, count_z, stride=2), :] / scale[:, y : y + 1] for y in range(2)
    ]
    table = jnp.concatenate(
        [
            jnp.where(
                iota((LANES, FINE * LANES), 1) == place_of(iota((LANES, 1), 0), y), 1.0, 0.0
            )
            for y in range(2)
        ],
        axis=0,
    ).astype(bf16)
    spread = jnp.dot(
        three_way(jnp.concatenate(rows, axis=1)), table, preferred_element_type=f32
    )
    spread = spread[0:count_z] + spread[count_z : 2 * count_z] + spread[2 * count_z : 3 * count_z]
    for k in range(FINE):
        turned[pl.ds(k, count_z, stride=FINE), :] = spread[:, k * LANES : (k + 1) * LANES]
    lines = [
        turned[part * LANES : (part + 1) * LANES, :].T for part in range(turned.shape[0] // LANES)
    ]
    lines = jnp.concatenate(lines, axis=1)
    for i in range(FINE):
        out_ref[i] = lines[i * 2 * FINE : (i + 1) * 2 * FINE, 0 : count_z * FINE]


def unpack(core, back, scaling, shape):
    count_z = scaling.shape[2]
    width = -(-count_z * FINE // LANES) * LANES

    def body(*refs):
        unpack_body(*refs, count_z=count_z)

    vmem = pl.BlockSpec(memory_space=pltpu.VMEM)
    return pl.pallas_call(
        body,
        out_shape=jax.ShapeDtypeStruct(shape, f32),
        in_specs=[pl.BlockSpec(memory_space=pltpu.SMEM), vmem, vmem],
        out_specs=vmem,
        scratch_shapes=[pltpu.VMEM((width, LANES), f32)],
        compiler_params=pltpu.CompilerParams(vmem_limit_bytes=8 * MIB),
        name="unpack",
    )(core, back, scaling)


def shifted_block(ref, pad, points):
    nodes = points**3
    pad[...] = jnp.zeros((LANES, LANES), f32)
    pad[0:nodes, 0:nodes] = ref[...]
    lane, row = iota((LANES, LANES), 1), iota((LANES, LANES), 0)
    count = jnp.zeros((LANES, LANES), f32)
    for stride in (points * points, points, 1):
        index = (lane // stride) % points
        count = count + jnp.where((index == 0) | (index == points - 1), 0.5, 0.0)
    diagonal = jnp.where(lane < nodes, count, 1.0)
    return pad[...] + jnp.where(lane == row, diagonal, 0.0)


def invert(matrix, panels):
    lane, row = iota((LANES, LANES), 1), iota((LANES, LANES), 0)
    lane16, row16 = iota((16, LANES), 1), iota((16, LANES), 0)
    for panel in range(panels):
        top = panel * 16
        rows = matrix[top : top + 16, :]
        for step in range(16):
            pivot = top + step
            column = rows[:, pivot : pivot + 1]
            scale = 1.0 / rows[step : step + 1, pivot : pivot + 1]
            scaled = jnp.where(lane16[0:1] == pivot, scale, rows[step : step + 1, :] * scale)
            others = jnp.where(lane16 == pivot, 0.0, rows) - column * scaled
            rows = jnp.where(row16 == step, scaled, others)
        stacked = jnp.concatenate([rows] * 8, axis=0)
        inside = (lane >= top) & (lane < top + 16)
        update = jnp.dot(
            jnp.where(inside, matrix, 0.0), stacked, precision=HIGHEST, preferred_element_type=f32
        )
        matrix = jnp.where(
            (row >= top) & (row < top + 16), stacked, jnp.where(inside, 0.0, matrix) - update
        )
    return matrix


def repeated(matrix):
    lane, row = iota((LANES, LANES), 1), iota((LANES, LANES), 0)
    pick = jnp.where((row % 32 == lane) & (lane < 32), 1.0, 0.0)
    put = jnp.where((lane % 32 == row) & (row < 32), 1.0, 0.0)
    tall = jnp.dot(pick, matrix, precision=HIGHEST, preferred_element_type=f32)
    wide = jnp.dot(tall, put, precision=HIGHEST, preferred_element_type=f32)
    return jnp.where(row // 32 == lane // 32, wide, 0.0)


def inverses_body(fine_ref, mid_ref, coarse_ref, fine_out, mid_out, coarse_out, pad):
    coarse = invert(shifted_block(coarse_ref, pad, COARSE), 1)
    mid = invert(shifted_block(mid_ref, pad, MID), 2)
    fine = invert(shifted_block(fine_ref, pad, FINE), 8)
    fine_out[...] = 0.35 * fine
    mid_out[...] = 0.35 * repeated(mid)
    coarse_out[...] = 0.35 * repeated(coarse)


def inverses(block_fine, block_mid, block_coarse):
    square = jax.ShapeDtypeStruct((LANES, LANES), f32)
    return pl.pallas_call(
        inverses_body,
        out_shape=(square, square, square),
        scratch_shapes=[pltpu.VMEM((LANES, LANES), f32)],
        compiler_params=pltpu.CompilerParams(vmem_limit_bytes=8 * MIB),
        cost_estimate=pl.CostEstimate(
            flops=2_000_000_000, bytes_accessed=20_000_000, transcendentals=0
        ),
        name="inverses",
    )(block_fine, block_mid, block_coarse)


def two_way(values):
    hi = values.astype(bf16)
    lo = (values - hi.astype(f32)).astype(bf16)
    return jnp.concatenate([hi, lo], axis=1)


def two_way_table(table):
    hi = table.astype(bf16)
    lo = (table - hi.astype(f32)).astype(bf16)
    return jnp.concatenate(
        [jnp.concatenate([hi, lo], axis=1), jnp.concatenate([hi, jnp.zeros_like(lo)], axis=1)],
        axis=0,
    )


def times(values, table):
    result = jnp.dot(two_way(values), table, preferred_element_type=f32)
    return result[:, 0:LANES] + result[:, LANES : 2 * LANES]


class Faces:
    def __init__(self, points, in_lanes):
        nodes = points**3
        lane, row = iota((EY, LANES), 1), iota((EY, LANES), 0)
        local = lane % 32 if in_lanes else lane
        place = lane // 32
        self.turns = []
        for dimension, stride in enumerate((points * points, points, 1)):
            index = (local // stride) % points
            first = (index == 0) & (local < nodes)
            last = (index == points - 1) & (local < nodes)
            reach = (points - 1) * stride
            if dimension == 0 and in_lanes:
                first, last = first & (place > 0), last & (place < EX - 1)
                reach = reach - 32
            if dimension == 1:
                first, last = first & (row > 0), last & (row < EY - 1)
            self.turns.append((first[None], last[None], (-reach) % LANES, reach % LANES))

    def gather(self, pairs):
        total = None
        for (before, after), (first, last, down, up) in zip(pairs, self.turns):
            part = 0.0
            if after is not None:
                slabs = after.shape[0] // EY
                turned = pltpu.roll(after, up, 1).reshape(slabs, EY, LANES)
                part = jnp.where(last, turned, part)
            if before is not None:
                slabs = before.shape[0] // EY
                turned = pltpu.roll(before, down, 1).reshape(slabs, EY, LANES)
                part = jnp.where(first, turned, part)
            total = part if total is None else total + part
        return total.reshape(-1, LANES)


CHUNK = 8


def cuts(start, stop):
    count = -(-(stop - start) // CHUNK)
    edges = [start + (stop - start) * piece // count for piece in range(count + 1)]
    return list(zip(edges[:-1], edges[1:]))


def flat(values):
    return values.reshape(-1, LANES)


def beside(ref, rows):
    before = jnp.concatenate([ref[rows, HALF - 1 : EY - 1, :], ref[rows, 0:HALF, :]], axis=1)
    after = jnp.concatenate([ref[rows, HALF:EY, :], ref[rows, 1 : HALF + 1, :]], axis=1)
    return flat(before), flat(after)


def cycle_body(
    bounds_ref,
    mine_ref,
    other_ref,
    fine_ref,
    mid_ref,
    coarse_ref,
    down_ref,
    up_ref,
    low_ref,
    high_ref,
    out_ref,
    start,
    ping,
    pong,
    left,
    mid_start,
    mid_ping,
    mid_pong,
    mid_left,
    mask,
):
    fine_faces = Faces(FINE, False)
    mid_faces = Faces(MID, True)
    coarse_faces = Faces(COARSE, True)
    fine_table = two_way_table(fine_ref[...])
    mid_table = two_way_table(mid_ref[...])
    coarse_table = two_way_table(coarse_ref[...])

    slab = iota((WINDOW, EY, LANES), 0)
    mask[...] = jnp.where((slab >= bounds_ref[0]) & (slab < bounds_ref[1]), 1.0, 0.0)
    even_is_mine = bounds_ref[2] == 0

    def at(x, a, b):
        return slice(x * WINDOW + a, x * WINDOW + b)

    def get(ref, rows):
        return flat(ref[rows, :, :])

    def put(ref, rows, values):
        ref[rows, :, :] = values.reshape(-1, EY, LANES)

    def fine_gather(ref, x, a, b):
        return fine_faces.gather(
            (
                (
                    get(ref, at(x - 1, a, b)) if x > 0 else None,
                    get(ref, at(x + 1, a, b)) if x < EX - 1 else None,
                ),
                beside(ref, at(x, a, b)),
                (get(ref, at(x, a - 1, b - 1)), get(ref, at(x, a + 1, b + 1))),
            )
        )

    def fine_sweep(source, target, a, b, keep):
        for x in range(EX):
            for c, d in cuts(a, b):
                rows = at(x, c, d)
                faces = fine_gather(source, x, c, d)
                if keep is not None:
                    put(left, rows, get(left, rows) + keep * faces)
                moved = 0.3 * get(source, rows) + get(start, rows) + times(faces, fine_table)
                put(target, rows, moved * get(mask, at(0, c, d)))

    for x in range(EX):
        for c, d in cuts(0, WINDOW):
            values = []
            for z in range(c, d):
                place = pl.ds(x * HALF * WINDOW + z, HALF, stride=WINDOW)
                mine, other = mine_ref[place, :], other_ref[place, :]
                values.append(jnp.where(even_is_mine, mine, other))
                values.append(jnp.where(even_is_mine, other, mine))
            values = jnp.concatenate(values, axis=0)
            rows = at(x, c, d)
            put(left, rows, 0.027 * values)
            put(start, rows, 2.0 * times(values, fine_table))

    fine_sweep(start, ping, 1, WINDOW - 1, -0.105)
    fine_sweep(ping, pong, 2, WINDOW - 2, -0.35)

    def mid_gather(faces, ref, a, b):
        here = get(ref, at(0, a, b))
        return faces.gather(
            (
                (here, here),
                beside(ref, at(0, a, b)),
                (get(ref, at(0, a - 1, b - 1)), get(ref, at(0, a + 1, b + 1))),
            )
        )

    for c, d in cuts(3, WINDOW - 3):
        total = None
        for x in range(EX):
            rest = get(left, at(x, c, d)) + 0.5 * fine_gather(pong, x, c, d)
            part = times(rest, down_ref[x])
            total = part if total is None else total + part
        rows = at(0, c, d)
        total = total * get(mask, rows)
        put(mid_left, rows, 0.027 * total)
        put(mid_start, rows, 2.0 * times(total, mid_table))

    def mid_sweep(faces, table, base, source, target, margin, keep=None):
        for c, d in cuts(margin, WINDOW - margin):
            rows = at(0, c, d)
            values = mid_gather(faces, source, c, d)
            if keep is not None:
                put(mid_left, rows, get(mid_left, rows) + keep * values)
            moved = 0.3 * get(source, rows) + get(base, rows) + times(values, table)
            put(target, rows, moved * get(mask, rows))

    mid_sweep(mid_faces, mid_table, mid_start, mid_start, mid_ping, 4, -0.105)
    mid_sweep(mid_faces, mid_table, mid_start, mid_ping, mid_pong, 5, -0.35)

    base = ping.at[0:WINDOW]
    even = ping.at[WINDOW : 2 * WINDOW]
    odd = ping.at[2 * WINDOW : 3 * WINDOW]
    for c, d in cuts(6, WINDOW - 6):
        rows = at(0, c, d)
        rest = get(mid_left, rows) + 0.5 * mid_gather(mid_faces, mid_pong, c, d)
        low = times(rest * get(mask, rows), low_ref[...])
        put(base, rows, 2.0 * times(low, coarse_table))
    mid_sweep(coarse_faces, coarse_table, base, base, even, 7)
    mid_sweep(coarse_faces, coarse_table, base, even, odd, 8)
    mid_sweep(coarse_faces, coarse_table, base, odd, even, 9)

    for c, d in cuts(9, WINDOW - 9):
        rows = at(0, c, d)
        put(mid_pong, rows, get(mid_pong, rows) + times(get(even, rows), high_ref[...]))
    mid_sweep(mid_faces, mid_table, mid_start, mid_pong, mid_ping, 10)
    mid_sweep(mid_faces, mid_table, mid_start, mid_ping, mid_pong, 11)
    mid_sweep(mid_faces, mid_table, mid_start, mid_pong, mid_ping, 12)

    lifted = two_way(get(mid_ping, at(0, 12, WINDOW - 12)))
    for x in range(EX):
        rows = at(x, 12, WINDOW - 12)
        added = jnp.dot(lifted, up_ref[x], preferred_element_type=f32)
        added = added[:, 0:LANES] + added[:, LANES : 2 * LANES]
        put(pong, rows, get(pong, rows) + added)
    fine_sweep(pong, ping, 13, WINDOW - 13, None)
    fine_sweep(ping, pong, 14, WINDOW - 14, None)
    fine_sweep(pong, ping, RADIUS, WINDOW - RADIUS, None)

    for x in range(EX):
        for z in range(OWN):
            for y in range(2):
                values = ping[x * WINDOW + RADIUS + z, y * HALF : (y + 1) * HALF, :]
                first = x * HALF * OWN * 2 + z * 2 + y
                out_ref[pl.ds(first, HALF, stride=2 * OWN), :] = values


def cycle(bounds, mine, other, fine, mid, coarse, down, up, low, high):
    big = pltpu.VMEM((EX * WINDOW, EY, LANES), f32)
    small = pltpu.VMEM((WINDOW, EY, LANES), f32)
    vmem = pl.BlockSpec(memory_space=pltpu.VMEM)
    return pl.pallas_call(
        cycle_body,
        out_shape=jax.ShapeDtypeStruct((EX * HALF * 2 * OWN, LANES), f32),
        in_specs=[pl.BlockSpec(memory_space=pltpu.SMEM)] + [vmem] * 9,
        out_specs=vmem,
        scratch_shapes=[big, big, big, big, small, small, small, small, small],
        compiler_params=pltpu.CompilerParams(vmem_limit_bytes=32 * MIB),
        name="cycle",
    )(bounds, mine, other, fine, mid, coarse, down, up, low, high)


def per_device(fine_source_field, scaling, block_fine, block_mid, block_coarse):
    count_z = scaling.shape[2]
    parts = lax.axis_size("gx") * lax.axis_size("gy")
    groups = lax.axis_size("gz")
    down, up, low, high = transfer_tables()
    group = lax.axis_index("gz")
    core = group % 2
    cores = core.astype(jnp.int32).reshape(1)

    own, edge = pack(cores, fine_source_field, scaling)
    ties = [(i, i + 1) for i in range(1, groups - 1, 2)]
    halo = lax.ppermute(edge, "gz", ties + [(j, i) for i, j in ties])
    pairs = [(i, i ^ 1) for i in range(groups)]
    mine, give = join(cores, own, halo)
    other = lax.ppermute(give, "gz", pairs)
    chunks = window(cores, mine, other, parts)
    recv = lax.all_to_all(
        chunks.reshape(parts, WINDOW, LANES), ("gx", "gy"), 0, 0, tiled=True
    ).reshape(parts * WINDOW, LANES)
    fine, mid, coarse = inverses(block_fine, block_mid, block_coarse)
    other = lax.ppermute(recv, "gz", pairs)

    part = lax.axis_index("gx") * lax.axis_size("gy") + lax.axis_index("gy")
    first = (group - core) * count_z + OWN * part - RADIUS
    bounds = jnp.stack(
        [jnp.maximum(0, -first), jnp.minimum(WINDOW, groups * count_z - first), core]
    )
    result = cycle(
        bounds.astype(jnp.int32), recv, other, fine, mid, coarse, down, up, low, high
    )
    back = lax.all_to_all(
        result.reshape(parts, 2 * OWN, LANES), ("gx", "gy"), 0, 0, tiled=True
    ).reshape(parts * 2 * OWN, LANES)
    return unpack(cores, back, scaling, fine_source_field.shape)


def solution(mesh):
    in_specs = (P("gx", "gy", "gz"), P("gx", "gy", "gz"), P(), P(), P())
    out_specs = P("gx", "gy", "gz")
    return jax.shard_map(
        per_device, mesh=mesh, in_specs=in_specs, out_specs=out_specs, check_vma=False
    )
```

```python
import math

import jax
import jax.numpy as jnp
import numpy as np
from jax import lax
from jax.experimental import pallas as pl
from jax.experimental.pallas import tpu as pltpu
from jax.sharding import PartitionSpec as P

FINE = 5
MID = 3
COARSE = 2
CSWEEPS = 4
RADIUS = 15
HALO = 16
OWN = 4
WINDOW = OWN + 2 * RADIUS
EX = 4
EY = 16
HALF = EY // 2
LANES = 128

f32 = jnp.float32
bf16 = jnp.bfloat16
HIGHEST = lax.Precision.HIGHEST
MIB = 1 << 20


def gll_points(points):
    if points == 5:
        return np.array([-1.0, -math.sqrt(3.0 / 7.0), 0.0, math.sqrt(3.0 / 7.0), 1.0])
    if points == 3:
        return np.array([-1.0, 0.0, 1.0])
    return np.array([-1.0, 1.0])


def lagrange(fine_points, coarse_points):
    fine_nodes = gll_points(fine_points)
    coarse_nodes = gll_points(coarse_points)
    table = np.ones((fine_points, coarse_points))
    for column in range(coarse_points):
        for other in range(coarse_points):
            if other != column:
                table[:, column] *= (fine_nodes - coarse_nodes[other]) / (
                    coarse_nodes[column] - coarse_nodes[other]
                )
    return table


def halves(table):
    table = np.asarray(table, np.float32)
    hi = table.astype(jnp.bfloat16)
    lo = (table - hi.astype(np.float32)).astype(jnp.bfloat16)
    return np.block([[hi, lo], [hi, np.zeros_like(lo)]])


def transfer_tables():
    fine_mid = np.kron(np.kron(lagrange(5, 3), lagrange(5, 3)), lagrange(5, 3))
    mid_coarse = np.kron(np.kron(lagrange(3, 2), lagrange(3, 2)), lagrange(3, 2))
    down, up = [], []
    for place in range(EX):
        table = np.zeros((LANES, LANES))
        table[:125, place * 32 : place * 32 + 27] = fine_mid
        down.append(halves(table))
        up.append(halves(table.T))
    middle = np.zeros((LANES, LANES))
    for place in range(EX):
        middle[place * 32 : place * 32 + 27, place * 32 : place * 32 + 8] = mid_coarse
    return np.stack(down), np.stack(up), halves(middle), halves(middle.T)


def iota(shape, dimension):
    return lax.broadcasted_iota(jnp.int32, shape, dimension)


def three_way(values):
    one = values.astype(bf16)
    rest = values - one.astype(f32)
    two = rest.astype(bf16)
    three = (rest - two.astype(f32)).astype(bf16)
    return jnp.concatenate([one, two, three], axis=0)


def place_of(lane, y):
    i, j, k = lane // (FINE * FINE), (lane // FINE) % FINE, lane % FINE
    return jnp.where(lane < FINE**3, k * LANES + i * 2 * FINE + y * FINE + j, -1)


def pack_body(core_ref, field_ref, scale_ref, own_ref, edge_ref, lines, turned, *, count_z):
    lines[...] = jnp.zeros_like(lines)
    for i in range(FINE):
        lines[i * 2 * FINE : (i + 1) * 2 * FINE, 0 : count_z * FINE] = field_ref[i]
    for part in range(lines.shape[1] // LANES):
        lanes = slice(part * LANES, (part + 1) * LANES)
        turned[lanes, :] = lines[:, lanes].T
    lane = iota((1, 2 * LANES), 1)
    place = place_of(lane % LANES, lane // LANES)
    table = jnp.where(iota((FINE * LANES, 2 * LANES), 0) == place, 1.0, 0.0).astype(bf16)
    values = [turned[pl.ds(k, count_z, stride=FINE), :] for k in range(FINE)]
    nodes = jnp.dot(
        three_way(jnp.concatenate(values, axis=1)), table, preferred_element_type=f32
    )
    nodes = nodes[0:count_z] + nodes[count_z : 2 * count_z] + nodes[2 * count_z : 3 * count_z]
    scale = scale_ref[0].T
    for y in range(2):
        own_ref[y] = nodes[:, y * LANES : (y + 1) * LANES] / scale[:, y : y + 1]
    start = pl.multiple_of(core_ref[0] * (count_z - HALO), HALO)
    for y in range(2):
        edge_ref[y] = own_ref[y, pl.ds(start, HALO), :]


def pack(core, field, scaling):
    count_z = scaling.shape[2]
    width = -(-count_z * FINE // LANES) * LANES

    def body(*refs):
        pack_body(*refs, count_z=count_z)

    vmem = pl.BlockSpec(memory_space=pltpu.VMEM)
    return pl.pallas_call(
        body,
        out_shape=(
            jax.ShapeDtypeStruct((2, count_z, LANES), f32),
            jax.ShapeDtypeStruct((2, HALO, LANES), f32),
        ),
        in_specs=[pl.BlockSpec(memory_space=pltpu.SMEM), vmem, vmem],
        out_specs=(vmem, vmem),
        scratch_shapes=[pltpu.VMEM((LANES, width), f32), pltpu.VMEM((width, LANES), f32)],
        compiler_params=pltpu.CompilerParams(vmem_limit_bytes=8 * MIB),
        name="pack",
    )(core, field, scaling)


def join_body(core_ref, own_ref, halo_ref, mine_ref, give_ref, *, count_z):
    core = core_ref[0]
    own_at = pl.multiple_of((1 - core) * HALO, HALO)
    halo_at = pl.multiple_of(core * count_z, HALO)
    for ref, y in ((mine_ref, core), (give_ref, 1 - core)):
        ref[pl.ds(own_at, count_z), :] = own_ref[y]
        ref[pl.ds(halo_at, HALO), :] = halo_ref[y]


def join(core, own, halo):
    count_z = own.shape[1]

    def body(*refs):
        join_body(*refs, count_z=count_z)

    vmem = pl.BlockSpec(memory_space=pltpu.VMEM)
    line = jax.ShapeDtypeStruct((count_z + HALO, LANES), f32)
    return pl.pallas_call(
        body,
        out_shape=(line, line),
        in_specs=[pl.BlockSpec(memory_space=pltpu.SMEM), vmem, vmem],
        out_specs=(vmem, vmem),
        compiler_params=pltpu.CompilerParams(vmem_limit_bytes=8 * MIB),
        name="join",
    )(core, own, halo)


def window_body(core_ref, mine_ref, other_ref, out_ref, line, *, parts):
    length = mine_ref.shape[0]
    core = core_ref[0]
    line[pl.ds(pl.multiple_of(core * length, HALO), length), :] = mine_ref[...]
    line[pl.ds(pl.multiple_of((1 - core) * length, HALO), length), :] = other_ref[...]
    for part in range(parts):
        start = HALO - RADIUS + OWN * part
        out_ref[part * WINDOW : (part + 1) * WINDOW, :] = line[start : start + WINDOW, :]


def window(core, mine, other, parts):
    def body(*refs):
        window_body(*refs, parts=parts)

    vmem = pl.BlockSpec(memory_space=pltpu.VMEM)
    return pl.pallas_call(
        body,
        out_shape=jax.ShapeDtypeStruct((parts * WINDOW, LANES), f32),
        in_specs=[pl.BlockSpec(memory_space=pltpu.SMEM), vmem, vmem],
        out_specs=vmem,
        scratch_shapes=[pltpu.VMEM((2 * mine.shape[0], LANES), f32)],
        compiler_params=pltpu.CompilerParams(vmem_limit_bytes=8 * MIB),
        name="window",
    )(core, mine, other)


def unpack_body(core_ref, back_ref, scale_ref, out_ref, turned, *, count_z):
    scale = scale_ref[0].T
    base = core_ref[0] * (2 * count_z)
    rows = [
        back_ref[pl.ds(base + y, count_z, stride=2), :] / scale[:, y : y + 1] for y in range(2)
    ]
    table = jnp.concatenate(
        [
            jnp.where(
                iota((LANES, FINE * LANES), 1) == place_of(iota((LANES, 1), 0), y), 1.0, 0.0
            )
            for y in range(2)
        ],
        axis=0,
    ).astype(bf16)
    spread = jnp.dot(
        three_way(jnp.concatenate(rows, axis=1)), table, preferred_element_type=f32
    )
    spread = spread[0:count_z] + spread[count_z : 2 * count_z] + spread[2 * count_z : 3 * count_z]
    for k in range(FINE):
        turned[pl.ds(k, count_z, stride=FINE), :] = spread[:, k * LANES : (k + 1) * LANES]
    lines = [
        turned[part * LANES : (part + 1) * LANES, :].T for part in range(turned.shape[0] // LANES)
    ]
    lines = jnp.concatenate(lines, axis=1)
    for i in range(FINE):
        out_ref[i] = lines[i * 2 * FINE : (i + 1) * 2 * FINE, 0 : count_z * FINE]


def unpack(core, back, scaling, shape):
    count_z = scaling.shape[2]
    width = -(-count_z * FINE // LANES) * LANES

    def body(*refs):
        unpack_body(*refs, count_z=count_z)

    vmem = pl.BlockSpec(memory_space=pltpu.VMEM)
    return pl.pallas_call(
        body,
        out_shape=jax.ShapeDtypeStruct(shape, f32),
        in_specs=[pl.BlockSpec(memory_space=pltpu.SMEM), vmem, vmem],
        out_specs=vmem,
        scratch_shapes=[pltpu.VMEM((width, LANES), f32)],
        compiler_params=pltpu.CompilerParams(vmem_limit_bytes=8 * MIB),
        name="unpack",
    )(core, back, scaling)


def shifted_block(ref, pad, points):
    nodes = points**3
    pad[...] = jnp.zeros((LANES, LANES), f32)
    pad[0:nodes, 0:nodes] = ref[...]
    lane, row = iota((LANES, LANES), 1), iota((LANES, LANES), 0)
    count = jnp.zeros((LANES, LANES), f32)
    for stride in (points * points, points, 1):
        index = (lane // stride) % points
        count = count + jnp.where((index == 0) | (index == points - 1), 0.5, 0.0)
    diagonal = jnp.where(lane < nodes, count, 1.0)
    return pad[...] + jnp.where(lane == row, diagonal, 0.0)


def invert(matrix, panels):
    lane, row = iota((LANES, LANES), 1), iota((LANES, LANES), 0)
    lane16, row16 = iota((16, LANES), 1), iota((16, LANES), 0)
    for panel in range(panels):
        top = panel * 16
        rows = matrix[top : top + 16, :]
        for step in range(16):
            pivot = top + step
            column = rows[:, pivot : pivot + 1]
            scale = 1.0 / rows[step : step + 1, pivot : pivot + 1]
            scaled = jnp.where(lane16[0:1] == pivot, scale, rows[step : step + 1, :] * scale)
            others = jnp.where(lane16 == pivot, 0.0, rows) - column * scaled
            rows = jnp.where(row16 == step, scaled, others)
        stacked = jnp.concatenate([rows] * 8, axis=0)
        inside = (lane >= top) & (lane < top + 16)
        update = jnp.dot(
            jnp.where(inside, matrix, 0.0), stacked, precision=HIGHEST, preferred_element_type=f32
        )
        matrix = jnp.where(
            (row >= top) & (row < top + 16), stacked, jnp.where(inside, 0.0, matrix) - update
        )
    return matrix


def repeated(matrix):
    lane, row = iota((LANES, LANES), 1), iota((LANES, LANES), 0)
    pick = jnp.where((row % 32 == lane) & (lane < 32), 1.0, 0.0)
    put = jnp.where((lane % 32 == row) & (row < 32), 1.0, 0.0)
    tall = jnp.dot(pick, matrix, precision=HIGHEST, preferred_element_type=f32)
    wide = jnp.dot(tall, put, precision=HIGHEST, preferred_element_type=f32)
    return jnp.where(row // 32 == lane // 32, wide, 0.0)


def inverses_body(fine_ref, mid_ref, coarse_ref, fine_out, mid_out, coarse_out, pad):
    coarse = invert(shifted_block(coarse_ref, pad, COARSE), 1)
    mid = invert(shifted_block(mid_ref, pad, MID), 2)
    fine = invert(shifted_block(fine_ref, pad, FINE), 8)
    fine_out[...] = 0.35 * fine
    mid_out[...] = 0.35 * repeated(mid)
    coarse_out[...] = 0.35 * repeated(coarse)


def inverses(block_fine, block_mid, block_coarse):
    square = jax.ShapeDtypeStruct((LANES, LANES), f32)
    return pl.pallas_call(
        inverses_body,
        out_shape=(square, square, square),
        scratch_shapes=[pltpu.VMEM((LANES, LANES), f32)],
        compiler_params=pltpu.CompilerParams(vmem_limit_bytes=8 * MIB),
        cost_estimate=pl.CostEstimate(
            flops=2_000_000_000, bytes_accessed=20_000_000, transcendentals=0
        ),
        name="inverses",
    )(block_fine, block_mid, block_coarse)


def two_way(values):
    hi = values.astype(bf16)
    lo = (values - hi.astype(f32)).astype(bf16)
    return jnp.concatenate([hi, lo], axis=1)


def two_way_table(table):
    hi = table.astype(bf16)
    lo = (table - hi.astype(f32)).astype(bf16)
    return jnp.concatenate(
        [jnp.concatenate([hi, lo], axis=1), jnp.concatenate([hi, jnp.zeros_like(lo)], axis=1)],
        axis=0,
    )


def times(values, table):
    result = jnp.dot(two_way(values), table, preferred_element_type=f32)
    return result[:, 0:LANES] + result[:, LANES : 2 * LANES]


class Faces:
    def __init__(self, points, in_lanes):
        nodes = points**3
        lane, row = iota((EY, LANES), 1), iota((EY, LANES), 0)
        local = lane % 32 if in_lanes else lane
        place = lane // 32
        self.turns = []
        for dimension, stride in enumerate((points * points, points, 1)):
            index = (local // stride) % points
            first = (index == 0) & (local < nodes)
            last = (index == points - 1) & (local < nodes)
            reach = (points - 1) * stride
            if dimension == 0 and in_lanes:
                first, last = first & (place > 0), last & (place < EX - 1)
                reach = reach - 32
            if dimension == 1:
                first, last = first & (row > 0), last & (row < EY - 1)
            self.turns.append((first[None], last[None], (-reach) % LANES, reach % LANES))

    def gather(self, pairs):
        total = None
        for (before, after), (first, last, down, up) in zip(pairs, self.turns):
            part = 0.0
            if after is not None:
                slabs = after.shape[0] // EY
                turned = pltpu.roll(after, up, 1).reshape(slabs, EY, LANES)
                part = jnp.where(last, turned, part)
            if before is not None:
                slabs = before.shape[0] // EY
                turned = pltpu.roll(before, down, 1).reshape(slabs, EY, LANES)
                part = jnp.where(first, turned, part)
            total = part if total is None else total + part
        return total.reshape(-1, LANES)


CHUNK = 8


def cuts(start, stop):
    count = -(-(stop - start) // CHUNK)
    edges = [start + (stop - start) * piece // count for piece in range(count + 1)]
    return list(zip(edges[:-1], edges[1:]))


def flat(values):
    return values.reshape(-1, LANES)


def beside(ref, rows):
    before = jnp.concatenate([ref[rows, HALF - 1 : EY - 1, :], ref[rows, 0:HALF, :]], axis=1)
    after = jnp.concatenate([ref[rows, HALF:EY, :], ref[rows, 1 : HALF + 1, :]], axis=1)
    return flat(before), flat(after)


def cycle_body(
    bounds_ref,
    mine_ref,
    other_ref,
    fine_ref,
    mid_ref,
    coarse_ref,
    down_ref,
    up_ref,
    low_ref,
    high_ref,
    out_ref,
    start,
    ping,
    pong,
    left,
    mid_start,
    mid_ping,
    mid_pong,
    mid_left,
    mask,
):
    fine_faces = Faces(FINE, False)
    mid_faces = Faces(MID, True)
    coarse_faces = Faces(COARSE, True)
    fine_table = two_way_table(fine_ref[...])
    mid_table = two_way_table(mid_ref[...])
    coarse_table = two_way_table(coarse_ref[...])

    slab = iota((WINDOW, EY, LANES), 0)
    mask[...] = jnp.where((slab >= bounds_ref[0]) & (slab < bounds_ref[1]), 1.0, 0.0)
    even_is_mine = bounds_ref[2] == 0

    def at(x, a, b):
        return slice(x * WINDOW + a, x * WINDOW + b)

    def get(ref, rows):
        return flat(ref[rows, :, :])

    def put(ref, rows, values):
        ref[rows, :, :] = values.reshape(-1, EY, LANES)

    def fine_gather(ref, x, a, b):
        return fine_faces.gather(
            (
                (
                    get(ref, at(x - 1, a, b)) if x > 0 else None,
                    get(ref, at(x + 1, a, b)) if x < EX - 1 else None,
                ),
                beside(ref, at(x, a, b)),
                (get(ref, at(x, a - 1, b - 1)), get(ref, at(x, a + 1, b + 1))),
            )
        )

    def fine_sweep(source, target, a, b, keep):
        for x in range(EX):
            for c, d in cuts(a, b):
                rows = at(x, c, d)
                faces = fine_gather(source, x, c, d)
                if keep is not None:
                    put(left, rows, get(left, rows) + keep * faces)
                moved = 0.3 * get(source, rows) + get(start, rows) + times(faces, fine_table)
                put(target, rows, moved * get(mask, at(0, c, d)))

    for x in range(EX):
        for c, d in cuts(0, WINDOW):
            values = []
            for z in range(c, d):
                place = pl.ds(x * HALF * WINDOW + z, HALF, stride=WINDOW)
                mine, other = mine_ref[place, :], other_ref[place, :]
                values.append(jnp.where(even_is_mine, mine, other))
                values.append(jnp.where(even_is_mine, other, mine))
            values = jnp.concatenate(values, axis=0)
            rows = at(x, c, d)
            put(left, rows, 0.027 * values)
            put(start, rows, 2.0 * times(values, fine_table))

    fine_sweep(start, ping, 1, WINDOW - 1, -0.105)
    fine_sweep(ping, pong, 2, WINDOW - 2, -0.35)

    def mid_gather(faces, ref, a, b):
        here = get(ref, at(0, a, b))
        return faces.gather(
            (
                (here, here),
                beside(ref, at(0, a, b)),
                (get(ref, at(0, a - 1, b - 1)), get(ref, at(0, a + 1, b + 1))),
            )
        )

    for c, d in cuts(3, WINDOW - 3):
        total = None
        for x in range(EX):
            rest = get(left, at(x, c, d)) + 0.5 * fine_gather(pong, x, c, d)
            part = times(rest, down_ref[x])
            total = part if total is None else total + part
        rows = at(0, c, d)
        total = total * get(mask, rows)
        put(mid_left, rows, 0.027 * total)
        put(mid_start, rows, 2.0 * times(total, mid_table))

    def mid_sweep(faces, table, base, source, target, margin, keep=None):
        for c, d in cuts(margin, WINDOW - margin):
            rows = at(0, c, d)
            values = mid_gather(faces, source, c, d)
            if keep is not None:
                put(mid_left, rows, get(mid_left, rows) + keep * values)
            moved = 0.3 * get(source, rows) + get(base, rows) + times(values, table)
            put(target, rows, moved * get(mask, rows))

    mid_sweep(mid_faces, mid_table, mid_start, mid_start, mid_ping, 4, -0.105)
    mid_sweep(mid_faces, mid_table, mid_start, mid_ping, mid_pong, 5, -0.35)

    base = ping.at[0:WINDOW]
    even = ping.at[WINDOW : 2 * WINDOW]
    odd = ping.at[2 * WINDOW : 3 * WINDOW]
    for c, d in cuts(6, WINDOW - 6):
        rows = at(0, c, d)
        rest = get(mid_left, rows) + 0.5 * mid_gather(mid_faces, mid_pong, c, d)
        low = times(rest * get(mask, rows), low_ref[...])
        put(base, rows, 2.0 * times(low, coarse_table))
    mid_sweep(coarse_faces, coarse_table, base, base, even, 7)
    mid_sweep(coarse_faces, coarse_table, base, even, odd, 8)
    mid_sweep(coarse_faces, coarse_table, base, odd, even, 9)

    for c, d in cuts(9, WINDOW - 9):
        rows = at(0, c, d)
        put(mid_pong, rows, get(mid_pong, rows) + times(get(even, rows), high_ref[...]))
    mid_sweep(mid_faces, mid_table, mid_start, mid_pong, mid_ping, 10)
    mid_sweep(mid_faces, mid_table, mid_start, mid_ping, mid_pong, 11)
    mid_sweep(mid_faces, mid_table, mid_start, mid_pong, mid_ping, 12)

    lifted = two_way(get(mid_ping, at(0, 12, WINDOW - 12)))
    for x in range(EX):
        rows = at(x, 12, WINDOW - 12)
        added = jnp.dot(lifted, up_ref[x], preferred_element_type=f32)
        added = added[:, 0:LANES] + added[:, LANES : 2 * LANES]
        put(pong, rows, get(pong, rows) + added)
    fine_sweep(pong, ping, 13, WINDOW - 13, None)
    fine_sweep(ping, pong, 14, WINDOW - 14, None)
    fine_sweep(pong, ping, RADIUS, WINDOW - RADIUS, None)

    for x in range(EX):
        for z in range(OWN):
            for y in range(2):
                values = ping[x * WINDOW + RADIUS + z, y * HALF : (y + 1) * HALF, :]
                first = x * HALF * OWN * 2 + z * 2 + y
                out_ref[pl.ds(first, HALF, stride=2 * OWN), :] = values


def cycle(bounds, mine, other, fine, mid, coarse, down, up, low, high):
    big = pltpu.VMEM((EX * WINDOW, EY, LANES), f32)
    small = pltpu.VMEM((WINDOW, EY, LANES), f32)
    vmem = pl.BlockSpec(memory_space=pltpu.VMEM)
    return pl.pallas_call(
        cycle_body,
        out_shape=jax.ShapeDtypeStruct((EX * HALF * 2 * OWN, LANES), f32),
        in_specs=[pl.BlockSpec(memory_space=pltpu.SMEM)] + [vmem] * 9,
        out_specs=vmem,
        scratch_shapes=[big, big, big, big, small, small, small, small, small],
        compiler_params=pltpu.CompilerParams(vmem_limit_bytes=32 * MIB),
        name="cycle",
    )(bounds, mine, other, fine, mid, coarse, down, up, low, high)


def per_device(fine_source_field, scaling, block_fine, block_mid, block_coarse):
    count_z = scaling.shape[2]
    parts = lax.axis_size("gx") * lax.axis_size("gy")
    groups = lax.axis_size("gz")
    down, up, low, high = transfer_tables()
    group = lax.axis_index("gz")
    core = group % 2
    cores = core.astype(jnp.int32).reshape(1)

    own, edge = pack(cores, fine_source_field, scaling)
    ties = [(i, i + 1) for i in range(1, groups - 1, 2)]
    halo = lax.ppermute(edge, "gz", ties + [(j, i) for i, j in ties])
    pairs = [(i, i ^ 1) for i in range(groups)]
    mine, give = join(cores, own, halo)
    other = lax.ppermute(give, "gz", pairs)
    chunks = window(cores, mine, other, parts)
    chunks, *matrices = lax.optimization_barrier((chunks, block_fine, block_mid, block_coarse))
    recv = lax.all_to_all(
        chunks.reshape(parts, WINDOW, LANES), ("gx", "gy"), 0, 0, tiled=True
    ).reshape(parts * WINDOW, LANES)
    recv, fine, mid, coarse = lax.optimization_barrier(
        (recv, *inverses(*matrices))
    )
    other = lax.ppermute(recv, "gz", pairs)

    part = lax.axis_index("gx") * lax.axis_size("gy") + lax.axis_index("gy")
    first = (group - core) * count_z + OWN * part - RADIUS
    bounds = jnp.stack(
        [jnp.maximum(0, -first), jnp.minimum(WINDOW, groups * count_z - first), core]
    )
    result = cycle(
        bounds.astype(jnp.int32), recv, other, fine, mid, coarse, down, up, low, high
    )
    back = lax.all_to_all(
        result.reshape(parts, 2 * OWN, LANES), ("gx", "gy"), 0, 0, tiled=True
    ).reshape(parts * 2 * OWN, LANES)
    return unpack(cores, back, scaling, fine_source_field.shape)


def solution(mesh):
    in_specs = (P("gx", "gy", "gz"), P("gx", "gy", "gz"), P(), P(), P())
    out_specs = P("gx", "gy", "gz")
    return jax.shard_map(
        per_device, mesh=mesh, in_specs=in_specs, out_specs=out_specs, check_vma=False
    )
```

```python
import math

import jax
import jax.numpy as jnp
import numpy as np
from jax import lax
from jax.experimental import pallas as pl
from jax.experimental.pallas import tpu as pltpu
from jax.sharding import PartitionSpec as P

FINE = 5
MID = 3
COARSE = 2
CSWEEPS = 4
RADIUS = 15
HALO = 16
OWN = 4
WINDOW = OWN + 2 * RADIUS
EX = 4
EY = 16
HALF = EY // 2
LANES = 128

f32 = jnp.float32
bf16 = jnp.bfloat16
HIGHEST = lax.Precision.HIGHEST
MIB = 1 << 20


def gll_points(points):
    if points == 5:
        return np.array([-1.0, -math.sqrt(3.0 / 7.0), 0.0, math.sqrt(3.0 / 7.0), 1.0])
    if points == 3:
        return np.array([-1.0, 0.0, 1.0])
    return np.array([-1.0, 1.0])


def lagrange(fine_points, coarse_points):
    fine_nodes = gll_points(fine_points)
    coarse_nodes = gll_points(coarse_points)
    table = np.ones((fine_points, coarse_points))
    for column in range(coarse_points):
        for other in range(coarse_points):
            if other != column:
                table[:, column] *= (fine_nodes - coarse_nodes[other]) / (
                    coarse_nodes[column] - coarse_nodes[other]
                )
    return table


def halves(table):
    table = np.asarray(table, np.float32)
    hi = table.astype(jnp.bfloat16)
    lo = (table - hi.astype(np.float32)).astype(jnp.bfloat16)
    return np.block([[hi, lo], [hi, np.zeros_like(lo)]])


def transfer_tables():
    fine_mid = np.kron(np.kron(lagrange(5, 3), lagrange(5, 3)), lagrange(5, 3))
    mid_coarse = np.kron(np.kron(lagrange(3, 2), lagrange(3, 2)), lagrange(3, 2))
    down, up = [], []
    for place in range(EX):
        table = np.zeros((LANES, LANES))
        table[:125, place * 32 : place * 32 + 27] = fine_mid
        down.append(halves(table))
        up.append(halves(table.T))
    middle = np.zeros((LANES, LANES))
    for place in range(EX):
        middle[place * 32 : place * 32 + 27, place * 32 : place * 32 + 8] = mid_coarse
    low = [halves(0.027 * middle)]
    low += [halves(0.5 * np.dot(move, middle)) for move in exchanges(MID, True)]
    return np.stack(down), np.stack(up), np.stack(low), halves(middle.T)


def iota(shape, dimension):
    return lax.broadcasted_iota(jnp.int32, shape, dimension)


def three_way(values):
    one = values.astype(bf16)
    rest = values - one.astype(f32)
    two = rest.astype(bf16)
    three = (rest - two.astype(f32)).astype(bf16)
    return jnp.concatenate([one, two, three], axis=0)


def place_of(lane, y):
    i, j, k = lane // (FINE * FINE), (lane // FINE) % FINE, lane % FINE
    return jnp.where(lane < FINE**3, k * LANES + i * 2 * FINE + y * FINE + j, -1)


def pack_body(core_ref, field_ref, scale_ref, own_ref, edge_ref, lines, turned, *, count_z):
    lines[...] = jnp.zeros_like(lines)
    for i in range(FINE):
        lines[i * 2 * FINE : (i + 1) * 2 * FINE, 0 : count_z * FINE] = field_ref[i]
    for part in range(lines.shape[1] // LANES):
        lanes = slice(part * LANES, (part + 1) * LANES)
        turned[lanes, :] = lines[:, lanes].T
    lane = iota((1, 2 * LANES), 1)
    place = place_of(lane % LANES, lane // LANES)
    table = jnp.where(iota((FINE * LANES, 2 * LANES), 0) == place, 1.0, 0.0).astype(bf16)
    values = [turned[pl.ds(k, count_z, stride=FINE), :] for k in range(FINE)]
    nodes = jnp.dot(
        three_way(jnp.concatenate(values, axis=1)), table, preferred_element_type=f32
    )
    nodes = nodes[0:count_z] + nodes[count_z : 2 * count_z] + nodes[2 * count_z : 3 * count_z]
    scale = scale_ref[0].T
    for y in range(2):
        own_ref[y] = nodes[:, y * LANES : (y + 1) * LANES] / scale[:, y : y + 1]
    start = pl.multiple_of(core_ref[0] * (count_z - HALO), HALO)
    for y in range(2):
        edge_ref[y] = own_ref[y, pl.ds(start, HALO), :]


def pack(core, field, scaling):
    count_z = scaling.shape[2]
    width = -(-count_z * FINE // LANES) * LANES

    def body(*refs):
        pack_body(*refs, count_z=count_z)

    vmem = pl.BlockSpec(memory_space=pltpu.VMEM)
    return pl.pallas_call(
        body,
        out_shape=(
            jax.ShapeDtypeStruct((2, count_z, LANES), f32),
            jax.ShapeDtypeStruct((2, HALO, LANES), f32),
        ),
        in_specs=[pl.BlockSpec(memory_space=pltpu.SMEM), vmem, vmem],
        out_specs=(vmem, vmem),
        scratch_shapes=[pltpu.VMEM((LANES, width), f32), pltpu.VMEM((width, LANES), f32)],
        compiler_params=pltpu.CompilerParams(vmem_limit_bytes=8 * MIB),
        name="pack",
    )(core, field, scaling)


def join_body(core_ref, own_ref, halo_ref, mine_ref, give_ref, *, count_z):
    core = core_ref[0]
    own_at = pl.multiple_of((1 - core) * HALO, HALO)
    halo_at = pl.multiple_of(core * count_z, HALO)
    for ref, y in ((mine_ref, core), (give_ref, 1 - core)):
        ref[pl.ds(own_at, count_z), :] = own_ref[y]
        ref[pl.ds(halo_at, HALO), :] = halo_ref[y]


def join(core, own, halo):
    count_z = own.shape[1]

    def body(*refs):
        join_body(*refs, count_z=count_z)

    vmem = pl.BlockSpec(memory_space=pltpu.VMEM)
    line = jax.ShapeDtypeStruct((count_z + HALO, LANES), f32)
    return pl.pallas_call(
        body,
        out_shape=(line, line),
        in_specs=[pl.BlockSpec(memory_space=pltpu.SMEM), vmem, vmem],
        out_specs=(vmem, vmem),
        compiler_params=pltpu.CompilerParams(vmem_limit_bytes=8 * MIB),
        name="join",
    )(core, own, halo)


def window_body(core_ref, mine_ref, other_ref, out_ref, line, *, parts):
    length = mine_ref.shape[0]
    core = core_ref[0]
    line[pl.ds(pl.multiple_of(core * length, HALO), length), :] = mine_ref[...]
    line[pl.ds(pl.multiple_of((1 - core) * length, HALO), length), :] = other_ref[...]
    for part in range(parts):
        start = HALO - RADIUS + OWN * part
        out_ref[part * WINDOW : (part + 1) * WINDOW, :] = line[start : start + WINDOW, :]


def window(core, mine, other, parts):
    def body(*refs):
        window_body(*refs, parts=parts)

    vmem = pl.BlockSpec(memory_space=pltpu.VMEM)
    return pl.pallas_call(
        body,
        out_shape=jax.ShapeDtypeStruct((parts * WINDOW, LANES), f32),
        in_specs=[pl.BlockSpec(memory_space=pltpu.SMEM), vmem, vmem],
        out_specs=vmem,
        scratch_shapes=[pltpu.VMEM((2 * mine.shape[0], LANES), f32)],
        compiler_params=pltpu.CompilerParams(vmem_limit_bytes=8 * MIB),
        name="window",
    )(core, mine, other)


def unpack_body(core_ref, back_ref, scale_ref, out_ref, turned, *, count_z):
    scale = scale_ref[0].T
    base = core_ref[0] * (2 * count_z)
    rows = [
        back_ref[pl.ds(base + y, count_z, stride=2), :] / scale[:, y : y + 1] for y in range(2)
    ]
    table = jnp.concatenate(
        [
            jnp.where(
                iota((LANES, FINE * LANES), 1) == place_of(iota((LANES, 1), 0), y), 1.0, 0.0
            )
            for y in range(2)
        ],
        axis=0,
    ).astype(bf16)
    spread = jnp.dot(
        three_way(jnp.concatenate(rows, axis=1)), table, preferred_element_type=f32
    )
    spread = spread[0:count_z] + spread[count_z : 2 * count_z] + spread[2 * count_z : 3 * count_z]
    for k in range(FINE):
        turned[pl.ds(k, count_z, stride=FINE), :] = spread[:, k * LANES : (k + 1) * LANES]
    lines = [
        turned[part * LANES : (part + 1) * LANES, :].T for part in range(turned.shape[0] // LANES)
    ]
    lines = jnp.concatenate(lines, axis=1)
    for i in range(FINE):
        out_ref[i] = lines[i * 2 * FINE : (i + 1) * 2 * FINE, 0 : count_z * FINE]


def unpack(core, back, scaling, shape):
    count_z = scaling.shape[2]
    width = -(-count_z * FINE // LANES) * LANES

    def body(*refs):
        unpack_body(*refs, count_z=count_z)

    vmem = pl.BlockSpec(memory_space=pltpu.VMEM)
    return pl.pallas_call(
        body,
        out_shape=jax.ShapeDtypeStruct(shape, f32),
        in_specs=[pl.BlockSpec(memory_space=pltpu.SMEM), vmem, vmem],
        out_specs=vmem,
        scratch_shapes=[pltpu.VMEM((width, LANES), f32)],
        compiler_params=pltpu.CompilerParams(vmem_limit_bytes=8 * MIB),
        name="unpack",
    )(core, back, scaling)


def shifted_block(ref, pad, points):
    nodes = points**3
    pad[...] = jnp.zeros((LANES, LANES), f32)
    pad[0:nodes, 0:nodes] = ref[...]
    lane, row = iota((LANES, LANES), 1), iota((LANES, LANES), 0)
    count = jnp.zeros((LANES, LANES), f32)
    for stride in (points * points, points, 1):
        index = (lane // stride) % points
        count = count + jnp.where((index == 0) | (index == points - 1), 0.5, 0.0)
    diagonal = jnp.where(lane < nodes, count, 1.0)
    return pad[...] + jnp.where(lane == row, diagonal, 0.0)


def invert(matrix, panels):
    lane, row = iota((LANES, LANES), 1), iota((LANES, LANES), 0)
    lane16, row16 = iota((16, LANES), 1), iota((16, LANES), 0)
    for panel in range(panels):
        top = panel * 16
        rows = matrix[top : top + 16, :]
        for step in range(16):
            pivot = top + step
            column = rows[:, pivot : pivot + 1]
            scale = 1.0 / rows[step : step + 1, pivot : pivot + 1]
            scaled = jnp.where(lane16[0:1] == pivot, scale, rows[step : step + 1, :] * scale)
            others = jnp.where(lane16 == pivot, 0.0, rows) - column * scaled
            rows = jnp.where(row16 == step, scaled, others)
        stacked = jnp.concatenate([rows] * 8, axis=0)
        inside = (lane >= top) & (lane < top + 16)
        update = jnp.dot(
            jnp.where(inside, matrix, 0.0), stacked, precision=HIGHEST, preferred_element_type=f32
        )
        matrix = jnp.where(
            (row >= top) & (row < top + 16), stacked, jnp.where(inside, 0.0, matrix) - update
        )
    return matrix


def repeated(matrix):
    lane, row = iota((LANES, LANES), 1), iota((LANES, LANES), 0)
    pick = jnp.where((row % 32 == lane) & (lane < 32), 1.0, 0.0)
    put = jnp.where((lane % 32 == row) & (row < 32), 1.0, 0.0)
    tall = jnp.dot(pick, matrix, precision=HIGHEST, preferred_element_type=f32)
    wide = jnp.dot(tall, put, precision=HIGHEST, preferred_element_type=f32)
    return jnp.where(row // 32 == lane // 32, wide, 0.0)


def inverses_body(moves_ref, fine_ref, mid_ref, coarse_ref, fine_out, mid_out, coarse_out, pad):
    coarse = invert(shifted_block(coarse_ref, pad, COARSE), 1)
    mid = invert(shifted_block(mid_ref, pad, MID), 2)
    fine = invert(shifted_block(fine_ref, pad, FINE), 8)
    levels = ((fine, fine_out), (repeated(mid), mid_out), (repeated(coarse), coarse_out))
    for level, (inverse, out) in enumerate(levels):
        inverse = 0.35 * inverse
        out[0] = two_way_table(inverse)
        for dimension in range(3):
            moved = jnp.dot(
                moves_ref[3 * level + dimension].astype(f32),
                inverse,
                precision=HIGHEST,
                preferred_element_type=f32,
            )
            out[1 + dimension] = two_way_table(moved)


def inverses(block_fine, block_mid, block_coarse):
    square = jax.ShapeDtypeStruct((4, 2 * LANES, 2 * LANES), bf16)
    moves = exchanges(FINE, False) + exchanges(MID, True) + exchanges(COARSE, True)
    moves = np.stack(moves).astype(jnp.bfloat16)
    return pl.pallas_call(
        inverses_body,
        out_shape=(square, square, square),
        scratch_shapes=[pltpu.VMEM((LANES, LANES), f32)],
        compiler_params=pltpu.CompilerParams(vmem_limit_bytes=8 * MIB),
        cost_estimate=pl.CostEstimate(
            flops=2_000_000_000, bytes_accessed=20_000_000, transcendentals=0
        ),
        name="inverses",
    )(moves, block_fine, block_mid, block_coarse)


def two_way(values):
    hi = values.astype(bf16)
    lo = (values - hi.astype(f32)).astype(bf16)
    return jnp.concatenate([hi, lo], axis=1)


def two_way_table(table):
    hi = table.astype(bf16)
    lo = (table - hi.astype(f32)).astype(bf16)
    return jnp.concatenate(
        [jnp.concatenate([hi, lo], axis=1), jnp.concatenate([hi, jnp.zeros_like(lo)], axis=1)],
        axis=0,
    )


def times(values, *tables):
    values = jnp.concatenate([two_way(value) for value in values], axis=1)
    result = jnp.dot(values, jnp.concatenate(tables, axis=0), preferred_element_type=f32)
    return result[:, 0:LANES] + result[:, LANES : 2 * LANES]


def exchanges(points, in_lanes):
    nodes = points**3
    tables = []
    for dimension, stride in enumerate((points * points, points, 1)):
        table = np.zeros((LANES, LANES), np.float32)
        for place in range(EX if in_lanes else 1):
            for node in range(nodes):
                index = (node // stride) % points
                for end, step in ((0, -1), (points - 1, 1)):
                    if index != end:
                        continue
                    source = place * 32 + node - step * (points - 1) * stride
                    if dimension == 0 and in_lanes:
                        if not 0 <= place + step < EX:
                            continue
                        source += step * 32
                    table[source, place * 32 + node] = 1.0
        tables.append(table)
    return tables


class Faces:
    def __init__(self, points, in_lanes):
        lane, row = iota((EY, LANES), 1), iota((EY, LANES), 0)
        local = lane % 32 if in_lanes else lane
        self.masks = []
        for dimension, stride in enumerate((points * points, points, 1)):
            index = (local // stride) % points
            first, last = index == 0, index == points - 1
            if dimension == 1:
                self.masks.append((last & (row > 0), first & (row < EY - 1)))
            else:
                self.masks.append((last, first))

    def moved(self, dimension, faces):
        reach = (FINE - 1) * FINE ** (2 - dimension)
        lane = iota((1, LANES), 1)
        index = (lane // FINE ** (2 - dimension)) % FINE
        node = lane < FINE**3
        order = jnp.where((index == 0) & node, lane + reach, LANES - 1)
        order = jnp.where((index == FINE - 1) & node, lane - reach, order)
        turned = jnp.take_along_axis(
            faces, jnp.broadcast_to(order, faces.shape), axis=1, mode="promise_in_bounds"
        )
        return jnp.where(order < LANES - 1, turned, 0.0)

    def select(self, dimension, before, after):
        from_before, from_after = self.masks[dimension]
        if before is None:
            before, after = 0.0, flat_slabs(after)
        elif after is None:
            before, after = flat_slabs(before), 0.0
        else:
            before, after = flat_slabs(before), flat_slabs(after)
        if dimension == 1:
            after = jnp.where(from_after[None], after, 0.0)
        return flat(jnp.where(from_before[None], before, after))


def flat_slabs(values):
    return values.reshape(-1, EY, LANES)


CHUNK = 16


def cuts(start, stop):
    count = -(-(stop - start) // CHUNK)
    edges = [start + (stop - start) * piece // count for piece in range(count + 1)]
    return list(zip(edges[:-1], edges[1:]))


def flat(values):
    return values.reshape(-1, LANES)


def beside(ref, rows):
    before = jnp.concatenate([ref[rows, HALF - 1 : EY - 1, :], ref[rows, 0:HALF, :]], axis=1)
    after = jnp.concatenate([ref[rows, HALF:EY, :], ref[rows, 1 : HALF + 1, :]], axis=1)
    return flat(before), flat(after)


def cycle_body(
    bounds_ref,
    mine_ref,
    other_ref,
    fine_ref,
    mid_ref,
    coarse_ref,
    down_ref,
    up_ref,
    low_ref,
    high_ref,
    out_ref,
    start,
    ping,
    pong,
    left,
    left_x,
    left_y,
    left_z,
    mid_start,
    mid_ping,
    mid_pong,
    mid_left,
    mid_left_x,
    mid_left_y,
    mid_left_z,
    mask,
):
    lefts = (left_x, left_y, left_z)
    mid_lefts = (mid_left_x, mid_left_y, mid_left_z)
    fine_faces = Faces(FINE, False)
    mid_faces = Faces(MID, True)
    coarse_faces = Faces(COARSE, True)
    fine_table, *fine_tables = [fine_ref[i] for i in range(4)]
    mid_table, *mid_tables = [mid_ref[i] for i in range(4)]
    coarse_table, *coarse_tables = [coarse_ref[i] for i in range(4)]

    slab = iota((WINDOW, EY, LANES), 0)
    mask[...] = jnp.where((slab >= bounds_ref[0]) & (slab < bounds_ref[1]), 1.0, 0.0)
    even_is_mine = bounds_ref[2] == 0

    def at(x, a, b):
        return slice(x * WINDOW + a, x * WINDOW + b)

    def get(ref, rows):
        return flat(ref[rows, :, :])

    def put(ref, rows, values):
        ref[rows, :, :] = values.reshape(-1, EY, LANES)

    def fine_gather(ref, x, a, b):
        return (
            fine_faces.select(
                0,
                get(ref, at(x - 1, a, b)) if x > 0 else None,
                get(ref, at(x + 1, a, b)) if x < EX - 1 else None,
            ),
            fine_faces.select(1, *beside(ref, at(x, a, b))),
            fine_faces.select(2, get(ref, at(x, a - 1, b - 1)), get(ref, at(x, a + 1, b + 1))),
        )

    def fine_sweep(source, target, a, b, keep):
        for x in range(EX):
            for c, d in cuts(a, b):
                rows = at(x, c, d)
                faces = fine_gather(source, x, c, d)
                if keep is not None:
                    for ref, face in zip(lefts, faces):
                        if keep[0]:
                            put(ref, rows, keep[1] * face)
                        else:
                            put(ref, rows, get(ref, rows) + keep[1] * face)
                moved = 0.3 * get(source, rows) + get(start, rows) + times(faces, *fine_tables)
                put(target, rows, moved * get(mask, at(0, c, d)))

    for x in range(EX):
        for c, d in cuts(0, WINDOW):
            values = []
            for z in range(c, d):
                place = pl.ds(x * HALF * WINDOW + z, HALF, stride=WINDOW)
                mine, other = mine_ref[place, :], other_ref[place, :]
                values.append(jnp.where(even_is_mine, mine, other))
                values.append(jnp.where(even_is_mine, other, mine))
            values = jnp.concatenate(values, axis=0)
            rows = at(x, c, d)
            put(left, rows, values)
            put(start, rows, 2.0 * times((values,), fine_table))

    fine_sweep(start, ping, 1, WINDOW - 1, (True, -0.21))
    fine_sweep(ping, pong, 2, WINDOW - 2, (False, -0.7))

    def mid_gather(faces, ref, a, b):
        here = get(ref, at(0, a, b))
        return (
            here,
            faces.select(1, *beside(ref, at(0, a, b))),
            faces.select(2, get(ref, at(0, a - 1, b - 1)), get(ref, at(0, a + 1, b + 1))),
        )

    for c, d in cuts(3, WINDOW - 3):
        values = []
        for x in range(EX):
            rest = 0.027 * get(left, at(x, c, d))
            for dimension, face in enumerate(fine_gather(pong, x, c, d)):
                face = 0.5 * (get(lefts[dimension], at(x, c, d)) + face)
                rest = rest + fine_faces.moved(dimension, face)
            values.append(rest)
        tables = [down_ref[x] for x in range(EX)]
        rows = at(0, c, d)
        total = times(values, *tables) * get(mask, rows)
        put(mid_left, rows, total)
        put(mid_start, rows, 2.0 * times((total,), mid_table))

    def mid_sweep(faces, tables, base, source, target, margin, keep=None):
        for c, d in cuts(margin, WINDOW - margin):
            rows = at(0, c, d)
            values = mid_gather(faces, source, c, d)
            if keep is not None:
                for ref, face in zip(mid_lefts, values):
                    if keep[0]:
                        put(ref, rows, keep[1] * face)
                    else:
                        put(ref, rows, get(ref, rows) + keep[1] * face)
            moved = 0.3 * get(source, rows) + get(base, rows) + times(values, *tables)
            put(target, rows, moved * get(mask, rows))

    mid_sweep(mid_faces, mid_tables, mid_start, mid_start, mid_ping, 4, (True, -0.21))
    mid_sweep(mid_faces, mid_tables, mid_start, mid_ping, mid_pong, 5, (False, -0.7))

    base = ping.at[0:WINDOW]
    even = ping.at[WINDOW : 2 * WINDOW]
    odd = ping.at[2 * WINDOW : 3 * WINDOW]
    for c, d in cuts(6, WINDOW - 6):
        rows = at(0, c, d)
        values = [get(mid_left, rows)]
        for ref, face in zip(mid_lefts, mid_gather(mid_faces, mid_pong, c, d)):
            values.append(get(ref, rows) + face)
        low = times(values, *[low_ref[i] for i in range(4)]) * get(mask, rows)
        put(base, rows, 2.0 * times((low,), coarse_table))
    mid_sweep(coarse_faces, coarse_tables, base, base, even, 7)
    mid_sweep(coarse_faces, coarse_tables, base, even, odd, 8)
    mid_sweep(coarse_faces, coarse_tables, base, odd, even, 9)

    for c, d in cuts(9, WINDOW - 9):
        rows = at(0, c, d)
        put(mid_pong, rows, get(mid_pong, rows) + times((get(even, rows),), high_ref[...]))
    mid_sweep(mid_faces, mid_tables, mid_start, mid_pong, mid_ping, 10)
    mid_sweep(mid_faces, mid_tables, mid_start, mid_ping, mid_pong, 11)
    mid_sweep(mid_faces, mid_tables, mid_start, mid_pong, mid_ping, 12)

    lifted = two_way(get(mid_ping, at(0, 12, WINDOW - 12)))
    for x in range(EX):
        rows = at(x, 12, WINDOW - 12)
        added = jnp.dot(lifted, up_ref[x], preferred_element_type=f32)
        added = added[:, 0:LANES] + added[:, LANES : 2 * LANES]
        put(pong, rows, get(pong, rows) + added)
    fine_sweep(pong, ping, 13, WINDOW - 13, None)
    fine_sweep(ping, pong, 14, WINDOW - 14, None)
    fine_sweep(pong, ping, RADIUS, WINDOW - RADIUS, None)

    for x in range(EX):
        for z in range(OWN):
            for y in range(2):
                values = ping[x * WINDOW + RADIUS + z, y * HALF : (y + 1) * HALF, :]
                first = x * HALF * OWN * 2 + z * 2 + y
                out_ref[pl.ds(first, HALF, stride=2 * OWN), :] = values


def cycle(bounds, mine, other, fine, mid, coarse, down, up, low, high):
    big = pltpu.VMEM((EX * WINDOW, EY, LANES), f32)
    small = pltpu.VMEM((WINDOW, EY, LANES), f32)
    vmem = pl.BlockSpec(memory_space=pltpu.VMEM)
    return pl.pallas_call(
        cycle_body,
        out_shape=jax.ShapeDtypeStruct((EX * HALF * 2 * OWN, LANES), f32),
        in_specs=[pl.BlockSpec(memory_space=pltpu.SMEM)] + [vmem] * 9,
        out_specs=vmem,
        scratch_shapes=[big] * 7 + [small] * 8,
        compiler_params=pltpu.CompilerParams(vmem_limit_bytes=32 * MIB),
        name="cycle",
    )(bounds, mine, other, fine, mid, coarse, down, up, low, high)


def per_device(fine_source_field, scaling, block_fine, block_mid, block_coarse):
    count_z = scaling.shape[2]
    parts = lax.axis_size("gx") * lax.axis_size("gy")
    groups = lax.axis_size("gz")
    down, up, low, high = transfer_tables()
    group = lax.axis_index("gz")
    core = group % 2
    cores = core.astype(jnp.int32).reshape(1)

    own, edge = pack(cores, fine_source_field, scaling)
    ties = [(i, i + 1) for i in range(1, groups - 1, 2)]
    halo = lax.ppermute(edge, "gz", ties + [(j, i) for i, j in ties])
    pairs = [(i, i ^ 1) for i in range(groups)]
    mine, give = join(cores, own, halo)
    other = lax.ppermute(give, "gz", pairs)
    chunks = window(cores, mine, other, parts)
    chunks, *matrices = lax.optimization_barrier((chunks, block_fine, block_mid, block_coarse))
    recv = lax.all_to_all(
        chunks.reshape(parts * WINDOW // 2, 2, LANES), ("gx", "gy"), 0, 0, tiled=True
    ).reshape(parts * WINDOW, LANES)
    recv, fine, mid, coarse = lax.optimization_barrier(
        (recv, *inverses(*matrices))
    )
    other = lax.ppermute(recv, "gz", pairs)

    part = lax.axis_index("gx") * lax.axis_size("gy") + lax.axis_index("gy")
    first = (group - core) * count_z + OWN * part - RADIUS
    bounds = jnp.stack(
        [jnp.maximum(0, -first), jnp.minimum(WINDOW, groups * count_z - first), core]
    )
    result = cycle(
        bounds.astype(jnp.int32), recv, other, fine, mid, coarse, down, up, low, high
    )
    back = lax.all_to_all(
        result.reshape(parts, 2 * OWN, LANES), ("gx", "gy"), 0, 0, tiled=True
    ).reshape(parts * 2 * OWN, LANES)
    return unpack(cores, back, scaling, fine_source_field.shape)


def solution(mesh):
    in_specs = (P("gx", "gy", "gz"), P("gx", "gy", "gz"), P(), P(), P())
    out_specs = P("gx", "gy", "gz")
    return jax.shard_map(
        per_device, mesh=mesh, in_specs=in_specs, out_specs=out_specs, check_vma=False
    )
```

```python
import math

import jax
import jax.numpy as jnp
import numpy as np
from jax import lax
from jax.experimental import pallas as pl
from jax.experimental.pallas import tpu as pltpu
from jax.sharding import PartitionSpec as P

FINE = 5
MID = 3
COARSE = 2
CSWEEPS = 4
RADIUS = 15
HALO = 16
OWN = 4
WINDOW = OWN + 2 * RADIUS
EX = 4
EY = 16
HALF = EY // 2
LANES = 128

f32 = jnp.float32
bf16 = jnp.bfloat16
HIGHEST = lax.Precision.HIGHEST
MIB = 1 << 20


def gll_points(points):
    if points == 5:
        return np.array([-1.0, -math.sqrt(3.0 / 7.0), 0.0, math.sqrt(3.0 / 7.0), 1.0])
    if points == 3:
        return np.array([-1.0, 0.0, 1.0])
    return np.array([-1.0, 1.0])


def lagrange(fine_points, coarse_points):
    fine_nodes = gll_points(fine_points)
    coarse_nodes = gll_points(coarse_points)
    table = np.ones((fine_points, coarse_points))
    for column in range(coarse_points):
        for other in range(coarse_points):
            if other != column:
                table[:, column] *= (fine_nodes - coarse_nodes[other]) / (
                    coarse_nodes[column] - coarse_nodes[other]
                )
    return table


def halves(table):
    table = np.asarray(table, np.float32)
    hi = table.astype(jnp.bfloat16)
    lo = (table - hi.astype(np.float32)).astype(jnp.bfloat16)
    return np.concatenate([hi, lo], axis=1)


def transfer_tables():
    fine_mid = np.kron(np.kron(lagrange(5, 3), lagrange(5, 3)), lagrange(5, 3))
    mid_coarse = np.kron(np.kron(lagrange(3, 2), lagrange(3, 2)), lagrange(3, 2))
    down, up = [], []
    for place in range(EX):
        table = np.zeros((LANES, LANES))
        table[:125, place * 32 : place * 32 + 27] = fine_mid
        down.append(halves(table))
        up.append(halves(table.T))
    middle = np.zeros((LANES, LANES))
    for place in range(EX):
        middle[place * 32 : place * 32 + 27, place * 32 : place * 32 + 8] = mid_coarse
    low = [halves(0.027 * middle)]
    low += [halves(0.5 * np.dot(move, middle)) for move in exchanges(MID, True)]
    return np.stack(down), np.stack(up), np.stack(low), halves(middle.T)


def iota(shape, dimension):
    return lax.broadcasted_iota(jnp.int32, shape, dimension)


def three_way(values):
    one = values.astype(bf16)
    rest = values - one.astype(f32)
    two = rest.astype(bf16)
    three = (rest - two.astype(f32)).astype(bf16)
    return jnp.concatenate([one, two, three], axis=0)


def place_of(lane, y):
    i, j, k = lane // (FINE * FINE), (lane // FINE) % FINE, lane % FINE
    return jnp.where(lane < FINE**3, k * LANES + i * 2 * FINE + y * FINE + j, -1)


def pack_body(core_ref, field_ref, scale_ref, own_ref, edge_ref, lines, turned, *, count_z):
    lines[...] = jnp.zeros_like(lines)
    for i in range(FINE):
        lines[i * 2 * FINE : (i + 1) * 2 * FINE, 0 : count_z * FINE] = field_ref[i]
    for part in range(lines.shape[1] // LANES):
        lanes = slice(part * LANES, (part + 1) * LANES)
        turned[lanes, :] = lines[:, lanes].T
    lane = iota((1, 2 * LANES), 1)
    place = place_of(lane % LANES, lane // LANES)
    table = jnp.where(iota((FINE * LANES, 2 * LANES), 0) == place, 1.0, 0.0).astype(bf16)
    values = [turned[pl.ds(k, count_z, stride=FINE), :] for k in range(FINE)]
    nodes = jnp.dot(
        three_way(jnp.concatenate(values, axis=1)), table, preferred_element_type=f32
    )
    nodes = nodes[0:count_z] + nodes[count_z : 2 * count_z] + nodes[2 * count_z : 3 * count_z]
    scale = scale_ref[0].T
    for y in range(2):
        own_ref[y] = nodes[:, y * LANES : (y + 1) * LANES] / scale[:, y : y + 1]
    start = pl.multiple_of(core_ref[0] * (count_z - HALO), HALO)
    for y in range(2):
        edge_ref[y] = own_ref[y, pl.ds(start, HALO), :]


def pack(core, field, scaling):
    count_z = scaling.shape[2]
    width = -(-count_z * FINE // LANES) * LANES

    def body(*refs):
        pack_body(*refs, count_z=count_z)

    vmem = pl.BlockSpec(memory_space=pltpu.VMEM)
    return pl.pallas_call(
        body,
        out_shape=(
            jax.ShapeDtypeStruct((2, count_z, LANES), f32),
            jax.ShapeDtypeStruct((2, HALO, LANES), f32),
        ),
        in_specs=[pl.BlockSpec(memory_space=pltpu.SMEM), vmem, vmem],
        out_specs=(vmem, vmem),
        scratch_shapes=[pltpu.VMEM((LANES, width), f32), pltpu.VMEM((width, LANES), f32)],
        compiler_params=pltpu.CompilerParams(vmem_limit_bytes=8 * MIB),
        name="pack",
    )(core, field, scaling)


def join_body(core_ref, own_ref, halo_ref, mine_ref, give_ref, *, count_z):
    core = core_ref[0]
    own_at = pl.multiple_of((1 - core) * HALO, HALO)
    halo_at = pl.multiple_of(core * count_z, HALO)
    for ref, y in ((mine_ref, core), (give_ref, 1 - core)):
        ref[pl.ds(own_at, count_z), :] = own_ref[y]
        ref[pl.ds(halo_at, HALO), :] = halo_ref[y]


def join(core, own, halo):
    count_z = own.shape[1]

    def body(*refs):
        join_body(*refs, count_z=count_z)

    vmem = pl.BlockSpec(memory_space=pltpu.VMEM)
    line = jax.ShapeDtypeStruct((count_z + HALO, LANES), f32)
    return pl.pallas_call(
        body,
        out_shape=(line, line),
        in_specs=[pl.BlockSpec(memory_space=pltpu.SMEM), vmem, vmem],
        out_specs=(vmem, vmem),
        compiler_params=pltpu.CompilerParams(vmem_limit_bytes=8 * MIB),
        name="join",
    )(core, own, halo)


def window_body(core_ref, mine_ref, other_ref, out_ref, line, *, parts):
    length = mine_ref.shape[0]
    core = core_ref[0]
    line[pl.ds(pl.multiple_of(core * length, HALO), length), :] = mine_ref[...]
    line[pl.ds(pl.multiple_of((1 - core) * length, HALO), length), :] = other_ref[...]
    for part in range(parts):
        start = HALO - RADIUS + OWN * part
        out_ref[part * WINDOW : (part + 1) * WINDOW, :] = line[start : start + WINDOW, :]


def window(core, mine, other, parts):
    def body(*refs):
        window_body(*refs, parts=parts)

    vmem = pl.BlockSpec(memory_space=pltpu.VMEM)
    return pl.pallas_call(
        body,
        out_shape=jax.ShapeDtypeStruct((parts * WINDOW, LANES), f32),
        in_specs=[pl.BlockSpec(memory_space=pltpu.SMEM), vmem, vmem],
        out_specs=vmem,
        scratch_shapes=[pltpu.VMEM((2 * mine.shape[0], LANES), f32)],
        compiler_params=pltpu.CompilerParams(vmem_limit_bytes=8 * MIB),
        name="window",
    )(core, mine, other)


def unpack_body(core_ref, back_ref, scale_ref, out_ref, turned, *, count_z):
    scale = scale_ref[0].T
    base = core_ref[0] * (2 * count_z)
    rows = [
        back_ref[pl.ds(base + y, count_z, stride=2), :] / scale[:, y : y + 1] for y in range(2)
    ]
    table = jnp.concatenate(
        [
            jnp.where(
                iota((LANES, FINE * LANES), 1) == place_of(iota((LANES, 1), 0), y), 1.0, 0.0
            )
            for y in range(2)
        ],
        axis=0,
    ).astype(bf16)
    spread = jnp.dot(
        three_way(jnp.concatenate(rows, axis=1)), table, preferred_element_type=f32
    )
    spread = spread[0:count_z] + spread[count_z : 2 * count_z] + spread[2 * count_z : 3 * count_z]
    for k in range(FINE):
        turned[pl.ds(k, count_z, stride=FINE), :] = spread[:, k * LANES : (k + 1) * LANES]
    lines = [
        turned[part * LANES : (part + 1) * LANES, :].T for part in range(turned.shape[0] // LANES)
    ]
    lines = jnp.concatenate(lines, axis=1)
    for i in range(FINE):
        out_ref[i] = lines[i * 2 * FINE : (i + 1) * 2 * FINE, 0 : count_z * FINE]


def unpack(core, back, scaling, shape):
    count_z = scaling.shape[2]
    width = -(-count_z * FINE // LANES) * LANES

    def body(*refs):
        unpack_body(*refs, count_z=count_z)

    vmem = pl.BlockSpec(memory_space=pltpu.VMEM)
    return pl.pallas_call(
        body,
        out_shape=jax.ShapeDtypeStruct(shape, f32),
        in_specs=[pl.BlockSpec(memory_space=pltpu.SMEM), vmem, vmem],
        out_specs=vmem,
        scratch_shapes=[pltpu.VMEM((width, LANES), f32)],
        compiler_params=pltpu.CompilerParams(vmem_limit_bytes=8 * MIB),
        name="unpack",
    )(core, back, scaling)


def shifted_block(ref, pad, points):
    nodes = points**3
    pad[...] = jnp.zeros((LANES, LANES), f32)
    pad[0:nodes, 0:nodes] = ref[...]
    lane, row = iota((LANES, LANES), 1), iota((LANES, LANES), 0)
    count = jnp.zeros((LANES, LANES), f32)
    for stride in (points * points, points, 1):
        index = (lane // stride) % points
        count = count + jnp.where((index == 0) | (index == points - 1), 0.5, 0.0)
    diagonal = jnp.where(lane < nodes, count, 1.0)
    return pad[...] + jnp.where(lane == row, diagonal, 0.0)


def invert(matrix, panels):
    lane, row = iota((LANES, LANES), 1), iota((LANES, LANES), 0)
    lane1, lane16, row16 = iota((1, LANES), 1), iota((16, LANES), 1), iota((16, LANES), 0)
    for panel in range(panels):
        top = panel * 16
        rows = matrix[top : top + 16, :]
        for step in range(0, 16, 2):
            pivot = top + step
            left = jnp.broadcast_to(rows[:, pivot : pivot + 1], (16, LANES))
            right = jnp.broadcast_to(rows[:, pivot + 1 : pivot + 2], (16, LANES))
            a, b = left[step : step + 1], right[step : step + 1]
            c, d = left[step + 1 : step + 2], right[step + 1 : step + 2]
            scale = 1.0 / (a * d - b * c)
            here = (lane1 == pivot) | (lane1 == pivot + 1)
            one = jnp.where(here, jnp.where(lane1 == pivot, 1.0, 0.0), rows[step : step + 1])
            two = jnp.where(here, jnp.where(lane1 == pivot, 0.0, 1.0), rows[step + 1 : step + 2])
            one, two = (d * one - b * two) * scale, (a * two - c * one) * scale
            others = jnp.where((lane16 == pivot) | (lane16 == pivot + 1), 0.0, rows)
            others = others - left * one - right * two
            rows = jnp.where(row16 == step, one, jnp.where(row16 == step + 1, two, others))
        stacked = jnp.concatenate([rows] * 8, axis=0)
        inside = (lane >= top) & (lane < top + 16)
        update = jnp.dot(
            jnp.where(inside, matrix, 0.0), stacked, precision=HIGHEST, preferred_element_type=f32
        )
        matrix = jnp.where(
            (row >= top) & (row < top + 16), stacked, jnp.where(inside, 0.0, matrix) - update
        )
    return matrix


def repeated(matrix):
    lane, row = iota((LANES, LANES), 1), iota((LANES, LANES), 0)
    pick = jnp.where((row % 32 == lane) & (lane < 32), 1.0, 0.0)
    put = jnp.where((lane % 32 == row) & (row < 32), 1.0, 0.0)
    tall = jnp.dot(pick, matrix, precision=HIGHEST, preferred_element_type=f32)
    wide = jnp.dot(tall, put, precision=HIGHEST, preferred_element_type=f32)
    return jnp.where(row // 32 == lane // 32, wide, 0.0)


def moves(points, in_lanes):
    lane, row = iota((1, LANES), 1), iota((LANES, LANES), 0)
    local, place = (lane % 32, lane // 32) if in_lanes else (lane, 0)
    tables = []
    for dimension, stride in enumerate((points * points, points, 1)):
        index = (local // stride) % points
        first = (index == 0) & (local < points**3)
        last = (index == points - 1) & (local < points**3)
        reach = (points - 1) * stride
        if dimension == 0 and in_lanes:
            first, last = first & (place > 0), last & (place < EX - 1)
            reach = reach - 32
        source = jnp.where(first, lane + reach, jnp.where(last, lane - reach, -1))
        tables.append(jnp.where(row == source, 1.0, 0.0))
    return tables


def inverses_body(fine_ref, mid_ref, coarse_ref, out_ref, pad):
    coarse = invert(shifted_block(coarse_ref, pad, COARSE), 1)
    mid = invert(shifted_block(mid_ref, pad, MID), 2)
    fine = invert(shifted_block(fine_ref, pad, FINE), 8)
    levels = ((fine, FINE), (repeated(mid), MID), (repeated(coarse), COARSE))
    for level, (inverse, points) in enumerate(levels):
        inverse = 0.35 * inverse
        out_ref[4 * level] = two_way(inverse)
        for dimension, move in enumerate(moves(points, points < FINE)):
            moved = jnp.dot(move, inverse, precision=HIGHEST, preferred_element_type=f32)
            out_ref[4 * level + 1 + dimension] = two_way(moved)


def inverses(block_fine, block_mid, block_coarse):
    return pl.pallas_call(
        inverses_body,
        out_shape=jax.ShapeDtypeStruct((12, LANES, 2 * LANES), bf16),
        scratch_shapes=[pltpu.VMEM((LANES, LANES), f32)],
        compiler_params=pltpu.CompilerParams(vmem_limit_bytes=8 * MIB),
        cost_estimate=pl.CostEstimate(
            flops=2_000_000_000, bytes_accessed=20_000_000, transcendentals=0
        ),
        name="inverses",
    )(block_fine, block_mid, block_coarse)


def two_way(values):
    hi = values.astype(bf16)
    lo = (values - hi.astype(f32)).astype(bf16)
    return jnp.concatenate([hi, lo], axis=1)


def times(values, *tables):
    values = jnp.concatenate([two_way(value) for value in values], axis=1)
    stack = []
    for table in tables:
        high = table[:, 0:LANES]
        stack += [table, jnp.concatenate([high, jnp.zeros_like(high)], axis=1)]
    result = jnp.dot(values, jnp.concatenate(stack, axis=0), preferred_element_type=f32)
    return result[:, 0:LANES] + result[:, LANES : 2 * LANES]


def exchanges(points, in_lanes):
    nodes = points**3
    tables = []
    for dimension, stride in enumerate((points * points, points, 1)):
        table = np.zeros((LANES, LANES), np.float32)
        for place in range(EX if in_lanes else 1):
            for node in range(nodes):
                index = (node // stride) % points
                for end, step in ((0, -1), (points - 1, 1)):
                    if index != end:
                        continue
                    source = place * 32 + node - step * (points - 1) * stride
                    if dimension == 0 and in_lanes:
                        if not 0 <= place + step < EX:
                            continue
                        source += step * 32
                    table[source, place * 32 + node] = 1.0
        tables.append(table)
    return tables


class Faces:
    def __init__(self, points, in_lanes):
        lane, row = iota((EY, LANES), 1), iota((EY, LANES), 0)
        local = lane % 32 if in_lanes else lane
        self.masks = []
        for dimension, stride in enumerate((points * points, points, 1)):
            index = (local // stride) % points
            first, last = index == 0, index == points - 1
            if dimension == 1:
                self.masks.append((last & (row > 0), first & (row < EY - 1)))
            else:
                self.masks.append((last, first))

    def moved(self, dimension, faces):
        reach = (FINE - 1) * FINE ** (2 - dimension)
        lane = iota((1, LANES), 1)
        index = (lane // FINE ** (2 - dimension)) % FINE
        node = lane < FINE**3
        order = jnp.where((index == 0) & node, lane + reach, LANES - 1)
        order = jnp.where((index == FINE - 1) & node, lane - reach, order)
        turned = jnp.take_along_axis(
            faces, jnp.broadcast_to(order, faces.shape), axis=1, mode="promise_in_bounds"
        )
        return jnp.where(order < LANES - 1, turned, 0.0)

    def select(self, dimension, before, after):
        from_before, from_after = self.masks[dimension]
        if before is None:
            before, after = 0.0, flat_slabs(after)
        elif after is None:
            before, after = flat_slabs(before), 0.0
        else:
            before, after = flat_slabs(before), flat_slabs(after)
        if dimension == 1:
            after = jnp.where(from_after[None], after, 0.0)
        return flat(jnp.where(from_before[None], before, after))


def flat_slabs(values):
    return values.reshape(-1, EY, LANES)


CHUNK = 16


def cuts(start, stop):
    count = -(-(stop - start) // CHUNK)
    edges = [start + (stop - start) * piece // count for piece in range(count + 1)]
    return list(zip(edges[:-1], edges[1:]))


def flat(values):
    return values.reshape(-1, LANES)


def beside(ref, rows):
    before = jnp.concatenate([ref[rows, HALF - 1 : EY - 1, :], ref[rows, 0:HALF, :]], axis=1)
    after = jnp.concatenate([ref[rows, HALF:EY, :], ref[rows, 1 : HALF + 1, :]], axis=1)
    return flat(before), flat(after)


def cycle_body(
    bounds_ref,
    mine_ref,
    other_ref,
    tables_ref,
    down_ref,
    up_ref,
    low_ref,
    high_ref,
    out_ref,
    start,
    ping,
    pong,
    left,
    left_x,
    left_y,
    left_z,
    mid_start,
    mid_ping,
    mid_pong,
    mid_left,
    mid_left_x,
    mid_left_y,
    mid_left_z,
    mask,
):
    lefts = (left_x, left_y, left_z)
    mid_lefts = (mid_left_x, mid_left_y, mid_left_z)
    fine_faces = Faces(FINE, False)
    mid_faces = Faces(MID, True)
    coarse_faces = Faces(COARSE, True)
    fine_table, *fine_tables = [tables_ref[i] for i in range(4)]
    mid_table, *mid_tables = [tables_ref[i] for i in range(4, 8)]
    coarse_table, *coarse_tables = [tables_ref[i] for i in range(8, 12)]

    slab = iota((WINDOW, EY, LANES), 0)
    mask[...] = jnp.where((slab >= bounds_ref[0]) & (slab < bounds_ref[1]), 1.0, 0.0)
    even_is_mine = bounds_ref[2] == 0

    def at(x, a, b):
        return slice(x * WINDOW + a, x * WINDOW + b)

    def get(ref, rows):
        return flat(ref[rows, :, :])

    def put(ref, rows, values):
        ref[rows, :, :] = values.reshape(-1, EY, LANES)

    def fine_gather(ref, x, a, b):
        return (
            fine_faces.select(
                0,
                get(ref, at(x - 1, a, b)) if x > 0 else None,
                get(ref, at(x + 1, a, b)) if x < EX - 1 else None,
            ),
            fine_faces.select(1, *beside(ref, at(x, a, b))),
            fine_faces.select(2, get(ref, at(x, a - 1, b - 1)), get(ref, at(x, a + 1, b + 1))),
        )

    def fine_sweep(source, target, a, b, keep):
        for x in range(EX):
            for c, d in cuts(a, b):
                rows = at(x, c, d)
                faces = fine_gather(source, x, c, d)
                if keep is not None:
                    for ref, face in zip(lefts, faces):
                        if keep[0]:
                            put(ref, rows, keep[1] * face)
                        else:
                            put(ref, rows, get(ref, rows) + keep[1] * face)
                moved = 0.3 * get(source, rows) + get(start, rows) + times(faces, *fine_tables)
                put(target, rows, moved * get(mask, at(0, c, d)))

    for x in range(EX):
        for c, d in cuts(0, WINDOW):
            values = []
            for z in range(c, d):
                place = pl.ds(x * HALF * WINDOW + z, HALF, stride=WINDOW)
                mine, other = mine_ref[place, :], other_ref[place, :]
                values.append(jnp.where(even_is_mine, mine, other))
                values.append(jnp.where(even_is_mine, other, mine))
            values = jnp.concatenate(values, axis=0)
            rows = at(x, c, d)
            put(left, rows, values)
            put(start, rows, 2.0 * times((values,), fine_table))

    fine_sweep(start, ping, 1, WINDOW - 1, (True, -0.21))
    fine_sweep(ping, pong, 2, WINDOW - 2, (False, -0.7))

    def mid_gather(faces, ref, a, b):
        here = get(ref, at(0, a, b))
        return (
            here,
            faces.select(1, *beside(ref, at(0, a, b))),
            faces.select(2, get(ref, at(0, a - 1, b - 1)), get(ref, at(0, a + 1, b + 1))),
        )

    for c, d in cuts(3, WINDOW - 3):
        values = []
        for x in range(EX):
            rest = 0.027 * get(left, at(x, c, d))
            for dimension, face in enumerate(fine_gather(pong, x, c, d)):
                face = 0.5 * (get(lefts[dimension], at(x, c, d)) + face)
                rest = rest + fine_faces.moved(dimension, face)
            values.append(rest)
        tables = [down_ref[x] for x in range(EX)]
        rows = at(0, c, d)
        total = times(values, *tables) * get(mask, rows)
        put(mid_left, rows, total)
        put(mid_start, rows, 2.0 * times((total,), mid_table))

    def mid_sweep(faces, tables, base, source, target, margin, keep=None):
        for c, d in cuts(margin, WINDOW - margin):
            rows = at(0, c, d)
            values = mid_gather(faces, source, c, d)
            if keep is not None:
                for ref, face in zip(mid_lefts, values):
                    if keep[0]:
                        put(ref, rows, keep[1] * face)
                    else:
                        put(ref, rows, get(ref, rows) + keep[1] * face)
            moved = 0.3 * get(source, rows) + get(base, rows) + times(values, *tables)
            put(target, rows, moved * get(mask, rows))

    mid_sweep(mid_faces, mid_tables, mid_start, mid_start, mid_ping, 4, (True, -0.21))
    mid_sweep(mid_faces, mid_tables, mid_start, mid_ping, mid_pong, 5, (False, -0.7))

    base = ping.at[0:WINDOW]
    even = ping.at[WINDOW : 2 * WINDOW]
    odd = ping.at[2 * WINDOW : 3 * WINDOW]
    for c, d in cuts(6, WINDOW - 6):
        rows = at(0, c, d)
        values = [get(mid_left, rows)]
        for ref, face in zip(mid_lefts, mid_gather(mid_faces, mid_pong, c, d)):
            values.append(get(ref, rows) + face)
        low = times(values, *[low_ref[i] for i in range(4)]) * get(mask, rows)
        put(base, rows, 2.0 * times((low,), coarse_table))
    mid_sweep(coarse_faces, coarse_tables, base, base, even, 7)
    mid_sweep(coarse_faces, coarse_tables, base, even, odd, 8)
    mid_sweep(coarse_faces, coarse_tables, base, odd, even, 9)

    for c, d in cuts(9, WINDOW - 9):
        rows = at(0, c, d)
        put(mid_pong, rows, get(mid_pong, rows) + times((get(even, rows),), high_ref[...]))
    mid_sweep(mid_faces, mid_tables, mid_start, mid_pong, mid_ping, 10)
    mid_sweep(mid_faces, mid_tables, mid_start, mid_ping, mid_pong, 11)
    mid_sweep(mid_faces, mid_tables, mid_start, mid_pong, mid_ping, 12)

    lifted = get(mid_ping, at(0, 12, WINDOW - 12))
    for x in range(EX):
        rows = at(x, 12, WINDOW - 12)
        put(pong, rows, get(pong, rows) + times((lifted,), up_ref[x]))
    fine_sweep(pong, ping, 13, WINDOW - 13, None)
    fine_sweep(ping, pong, 14, WINDOW - 14, None)
    fine_sweep(pong, ping, RADIUS, WINDOW - RADIUS, None)

    for x in range(EX):
        for z in range(OWN):
            for y in range(2):
                values = ping[x * WINDOW + RADIUS + z, y * HALF : (y + 1) * HALF, :]
                first = x * HALF * OWN * 2 + z * 2 + y
                out_ref[pl.ds(first, HALF, stride=2 * OWN), :] = values


def cycle(bounds, mine, other, tables, down, up, low, high):
    big = pltpu.VMEM((EX * WINDOW, EY, LANES), f32)
    small = pltpu.VMEM((WINDOW, EY, LANES), f32)
    vmem = pl.BlockSpec(memory_space=pltpu.VMEM)
    return pl.pallas_call(
        cycle_body,
        out_shape=jax.ShapeDtypeStruct((EX * HALF * 2 * OWN, LANES), f32),
        in_specs=[pl.BlockSpec(memory_space=pltpu.SMEM)] + [vmem] * 7,
        out_specs=vmem,
        scratch_shapes=[big] * 7 + [small] * 8,
        compiler_params=pltpu.CompilerParams(vmem_limit_bytes=20 * MIB),
        name="cycle",
    )(bounds, mine, other, tables, down, up, low, high)


def per_device(fine_source_field, scaling, block_fine, block_mid, block_coarse):
    count_z = scaling.shape[2]
    parts = lax.axis_size("gx") * lax.axis_size("gy")
    groups = lax.axis_size("gz")
    down, up, low, high = transfer_tables()
    group = lax.axis_index("gz")
    core = group % 2
    cores = core.astype(jnp.int32).reshape(1)

    own, edge = pack(cores, fine_source_field, scaling)
    ties = [(i, i + 1) for i in range(1, groups - 1, 2)]
    halo = lax.ppermute(edge, "gz", ties + [(j, i) for i, j in ties])
    pairs = [(i, i ^ 1) for i in range(groups)]
    mine, give = join(cores, own, halo)
    other = lax.ppermute(give, "gz", pairs)
    chunks = window(cores, mine, other, parts)
    chunks, *matrices = lax.optimization_barrier((chunks, block_fine, block_mid, block_coarse))
    recv = lax.all_to_all(
        chunks.reshape(parts * WINDOW // 2, 2, LANES), ("gx", "gy"), 0, 0, tiled=True
    ).reshape(parts * WINDOW, LANES)
    recv, tables = lax.optimization_barrier((recv, inverses(*matrices)))
    other = lax.ppermute(recv, "gz", pairs)

    part = lax.axis_index("gx") * lax.axis_size("gy") + lax.axis_index("gy")
    first = (group - core) * count_z + OWN * part - RADIUS
    bounds = jnp.stack(
        [jnp.maximum(0, -first), jnp.minimum(WINDOW, groups * count_z - first), core]
    )
    result = cycle(
        bounds.astype(jnp.int32), recv, other, tables, down, up, low, high
    )
    back = lax.all_to_all(
        result.reshape(parts, 2 * OWN, LANES), ("gx", "gy"), 0, 0, tiled=True
    ).reshape(parts * 2 * OWN, LANES)
    return unpack(cores, back, scaling, fine_source_field.shape)


def solution(mesh):
    in_specs = (P("gx", "gy", "gz"), P("gx", "gy", "gz"), P(), P(), P())
    out_specs = P("gx", "gy", "gz")
    return jax.shard_map(
        per_device, mesh=mesh, in_specs=in_specs, out_specs=out_specs, check_vma=False
    )
```

```python
import math

import jax
import jax.numpy as jnp
import numpy as np
from jax import lax
from jax.experimental import pallas as pl
from jax.experimental.pallas import tpu as pltpu
from jax.sharding import PartitionSpec as P

FINE = 5
MID = 3
COARSE = 2
CSWEEPS = 4
RADIUS = 15
HALO = 16
OWN = 4
WINDOW = OWN + 2 * RADIUS
SPLIT = WINDOW // 2
EX = 4
EY = 16
HALF = EY // 2
LANES = 128

f32 = jnp.float32
bf16 = jnp.bfloat16
HIGHEST = lax.Precision.HIGHEST
MIB = 1 << 20


def gll_points(points):
    if points == 5:
        return np.array([-1.0, -math.sqrt(3.0 / 7.0), 0.0, math.sqrt(3.0 / 7.0), 1.0])
    if points == 3:
        return np.array([-1.0, 0.0, 1.0])
    return np.array([-1.0, 1.0])


def lagrange(fine_points, coarse_points):
    fine_nodes = gll_points(fine_points)
    coarse_nodes = gll_points(coarse_points)
    table = np.ones((fine_points, coarse_points))
    for column in range(coarse_points):
        for other in range(coarse_points):
            if other != column:
                table[:, column] *= (fine_nodes - coarse_nodes[other]) / (
                    coarse_nodes[column] - coarse_nodes[other]
                )
    return table


def halves(table):
    table = np.asarray(table, np.float32)
    hi = table.astype(jnp.bfloat16)
    lo = (table - hi.astype(np.float32)).astype(jnp.bfloat16)
    return np.concatenate([hi, lo], axis=1)


def transfer_tables():
    fine_mid = np.kron(np.kron(lagrange(5, 3), lagrange(5, 3)), lagrange(5, 3))
    mid_coarse = np.kron(np.kron(lagrange(3, 2), lagrange(3, 2)), lagrange(3, 2))
    down, up = [], []
    for place in range(EX):
        table = np.zeros((LANES, LANES))
        table[:125, place * 32 : place * 32 + 27] = fine_mid
        down.append(halves(table))
        up.append(halves(table.T))
    middle = np.zeros((LANES, LANES))
    for place in range(EX):
        middle[place * 32 : place * 32 + 27, place * 32 : place * 32 + 8] = mid_coarse
    low = [halves(0.027 * middle)]
    low += [halves(0.5 * np.dot(move, middle)) for move in exchanges(MID, True)]
    return np.stack(down), np.stack(up), np.stack(low), halves(middle.T)


def iota(shape, dimension):
    return lax.broadcasted_iota(jnp.int32, shape, dimension)


def three_way(values):
    one = values.astype(bf16)
    rest = values - one.astype(f32)
    two = rest.astype(bf16)
    three = (rest - two.astype(f32)).astype(bf16)
    return jnp.concatenate([one, two, three], axis=0)


def place_of(lane, y):
    i, j, k = lane // (FINE * FINE), (lane // FINE) % FINE, lane % FINE
    return jnp.where(lane < FINE**3, k * LANES + i * 2 * FINE + y * FINE + j, -1)


def pack_body(core_ref, field_ref, scale_ref, own_ref, edge_ref, lines, turned, *, count_z):
    lines[...] = jnp.zeros_like(lines)
    for i in range(FINE):
        lines[i * 2 * FINE : (i + 1) * 2 * FINE, 0 : count_z * FINE] = field_ref[i]
    for part in range(lines.shape[1] // LANES):
        lanes = slice(part * LANES, (part + 1) * LANES)
        turned[lanes, :] = lines[:, lanes].T
    lane = iota((1, 2 * LANES), 1)
    place = place_of(lane % LANES, lane // LANES)
    table = jnp.where(iota((FINE * LANES, 2 * LANES), 0) == place, 1.0, 0.0).astype(bf16)
    values = [turned[pl.ds(k, count_z, stride=FINE), :] for k in range(FINE)]
    nodes = jnp.dot(
        three_way(jnp.concatenate(values, axis=1)), table, preferred_element_type=f32
    )
    nodes = nodes[0:count_z] + nodes[count_z : 2 * count_z] + nodes[2 * count_z : 3 * count_z]
    scale = scale_ref[0].T
    for y in range(2):
        own_ref[y] = nodes[:, y * LANES : (y + 1) * LANES] / scale[:, y : y + 1]
    start = pl.multiple_of(core_ref[0] * (count_z - HALO), HALO)
    for y in range(2):
        edge_ref[y] = own_ref[y, pl.ds(start, HALO), :]


def pack(core, field, scaling):
    count_z = scaling.shape[2]
    width = -(-count_z * FINE // LANES) * LANES

    def body(*refs):
        pack_body(*refs, count_z=count_z)

    vmem = pl.BlockSpec(memory_space=pltpu.VMEM)
    return pl.pallas_call(
        body,
        out_shape=(
            jax.ShapeDtypeStruct((2, count_z, LANES), f32),
            jax.ShapeDtypeStruct((2, HALO, LANES), f32),
        ),
        in_specs=[pl.BlockSpec(memory_space=pltpu.SMEM), vmem, vmem],
        out_specs=(vmem, vmem),
        scratch_shapes=[pltpu.VMEM((LANES, width), f32), pltpu.VMEM((width, LANES), f32)],
        compiler_params=pltpu.CompilerParams(vmem_limit_bytes=8 * MIB),
        name="pack",
    )(core, field, scaling)


def window_body(core_ref, own_ref, sibling_ref, halo_ref, out_ref, line, *, parts):
    count_z = own_ref.shape[1]
    for core in range(2):
        places = (HALO, HALO + count_z, 0) if core == 0 else (count_z, 0, 2 * count_z)

        @pl.when(core_ref[0] == core)
        def _(core=core, places=places):
            for ref, place in zip((own_ref, sibling_ref, halo_ref), places):
                line[:, place : place + ref.shape[1], :] = ref[...]
            first = HALO - RADIUS if core == 0 else SPLIT - RADIUS
            for part in range(parts):
                for y in range(2):
                    start = first + OWN * part
                    row = part * WINDOW + y * SPLIT
                    out_ref[row : row + SPLIT, :] = line[y, start : start + SPLIT, :]


def window(core, own, sibling, halo, parts):
    def body(*refs):
        window_body(*refs, parts=parts)

    vmem = pl.BlockSpec(memory_space=pltpu.VMEM)
    return pl.pallas_call(
        body,
        out_shape=jax.ShapeDtypeStruct((parts * WINDOW, LANES), f32),
        in_specs=[pl.BlockSpec(memory_space=pltpu.SMEM), vmem, vmem, vmem],
        out_specs=vmem,
        scratch_shapes=[pltpu.VMEM((2, 2 * own.shape[1] + HALO, LANES), f32)],
        compiler_params=pltpu.CompilerParams(vmem_limit_bytes=8 * MIB),
        name="window",
    )(core, own, sibling, halo)


def unpack_body(core_ref, back_ref, scale_ref, out_ref, turned, *, count_z):
    scale = scale_ref[0].T
    base = core_ref[0] * (2 * count_z)
    rows = [
        back_ref[pl.ds(base + y, count_z, stride=2), :] / scale[:, y : y + 1] for y in range(2)
    ]
    table = jnp.concatenate(
        [
            jnp.where(
                iota((LANES, FINE * LANES), 1) == place_of(iota((LANES, 1), 0), y), 1.0, 0.0
            )
            for y in range(2)
        ],
        axis=0,
    ).astype(bf16)
    spread = jnp.dot(
        three_way(jnp.concatenate(rows, axis=1)), table, preferred_element_type=f32
    )
    spread = spread[0:count_z] + spread[count_z : 2 * count_z] + spread[2 * count_z : 3 * count_z]
    for k in range(FINE):
        turned[pl.ds(k, count_z, stride=FINE), :] = spread[:, k * LANES : (k + 1) * LANES]
    lines = [
        turned[part * LANES : (part + 1) * LANES, :].T for part in range(turned.shape[0] // LANES)
    ]
    lines = jnp.concatenate(lines, axis=1)
    for i in range(FINE):
        out_ref[i] = lines[i * 2 * FINE : (i + 1) * 2 * FINE, 0 : count_z * FINE]


def unpack(core, back, scaling, shape):
    count_z = scaling.shape[2]
    width = -(-count_z * FINE // LANES) * LANES

    def body(*refs):
        unpack_body(*refs, count_z=count_z)

    vmem = pl.BlockSpec(memory_space=pltpu.VMEM)
    return pl.pallas_call(
        body,
        out_shape=jax.ShapeDtypeStruct(shape, f32),
        in_specs=[pl.BlockSpec(memory_space=pltpu.SMEM), vmem, vmem],
        out_specs=vmem,
        scratch_shapes=[pltpu.VMEM((width, LANES), f32)],
        compiler_params=pltpu.CompilerParams(vmem_limit_bytes=8 * MIB),
        name="unpack",
    )(core, back, scaling)


def shifted_block(ref, pad, points):
    nodes = points**3
    pad[...] = jnp.zeros((LANES, LANES), f32)
    pad[0:nodes, 0:nodes] = ref[...]
    lane, row = iota((LANES, LANES), 1), iota((LANES, LANES), 0)
    count = jnp.zeros((LANES, LANES), f32)
    for stride in (points * points, points, 1):
        index = (lane // stride) % points
        count = count + jnp.where((index == 0) | (index == points - 1), 0.5, 0.0)
    diagonal = jnp.where(lane < nodes, count, 1.0)
    return pad[...] + jnp.where(lane == row, diagonal, 0.0)


def invert(matrix, panels):
    lane, row = iota((LANES, LANES), 1), iota((LANES, LANES), 0)
    lane1, lane16, row16 = iota((1, LANES), 1), iota((16, LANES), 1), iota((16, LANES), 0)
    for panel in range(panels):
        top = panel * 16
        rows = matrix[top : top + 16, :]
        for step in range(0, 16, 2):
            pivot = top + step
            left = jnp.broadcast_to(rows[:, pivot : pivot + 1], (16, LANES))
            right = jnp.broadcast_to(rows[:, pivot + 1 : pivot + 2], (16, LANES))
            a, b = left[step : step + 1], right[step : step + 1]
            c, d = left[step + 1 : step + 2], right[step + 1 : step + 2]
            scale = 1.0 / (a * d - b * c)
            here = (lane1 == pivot) | (lane1 == pivot + 1)
            one = jnp.where(here, jnp.where(lane1 == pivot, 1.0, 0.0), rows[step : step + 1])
            two = jnp.where(here, jnp.where(lane1 == pivot, 0.0, 1.0), rows[step + 1 : step + 2])
            one, two = (d * one - b * two) * scale, (a * two - c * one) * scale
            others = jnp.where((lane16 == pivot) | (lane16 == pivot + 1), 0.0, rows)
            others = others - left * one - right * two
            rows = jnp.where(row16 == step, one, jnp.where(row16 == step + 1, two, others))
        stacked = jnp.concatenate([rows] * 8, axis=0)
        inside = (lane >= top) & (lane < top + 16)
        update = jnp.dot(
            jnp.where(inside, matrix, 0.0), stacked, precision=HIGHEST, preferred_element_type=f32
        )
        matrix = jnp.where(
            (row >= top) & (row < top + 16), stacked, jnp.where(inside, 0.0, matrix) - update
        )
    return matrix


def repeated(matrix):
    lane, row = iota((LANES, LANES), 1), iota((LANES, LANES), 0)
    pick = jnp.where((row % 32 == lane) & (lane < 32), 1.0, 0.0)
    put = jnp.where((lane % 32 == row) & (row < 32), 1.0, 0.0)
    tall = jnp.dot(pick, matrix, precision=HIGHEST, preferred_element_type=f32)
    wide = jnp.dot(tall, put, precision=HIGHEST, preferred_element_type=f32)
    return jnp.where(row // 32 == lane // 32, wide, 0.0)


def moves(points, in_lanes):
    lane, row = iota((1, LANES), 1), iota((LANES, LANES), 0)
    local, place = (lane % 32, lane // 32) if in_lanes else (lane, 0)
    tables = []
    for dimension, stride in enumerate((points * points, points, 1)):
        index = (local // stride) % points
        first = (index == 0) & (local < points**3)
        last = (index == points - 1) & (local < points**3)
        reach = (points - 1) * stride
        if dimension == 0 and in_lanes:
            first, last = first & (place > 0), last & (place < EX - 1)
            reach = reach - 32
        source = jnp.where(first, lane + reach, jnp.where(last, lane - reach, -1))
        tables.append(jnp.where(row == source, 1.0, 0.0))
    return tables


def inverses_body(fine_ref, mid_ref, coarse_ref, out_ref, pad):
    coarse = invert(shifted_block(coarse_ref, pad, COARSE), 1)
    mid = invert(shifted_block(mid_ref, pad, MID), 2)
    fine = invert(shifted_block(fine_ref, pad, FINE), 8)
    levels = ((fine, FINE), (repeated(mid), MID), (repeated(coarse), COARSE))
    for level, (inverse, points) in enumerate(levels):
        inverse = 0.35 * inverse
        out_ref[4 * level] = two_way(inverse)
        for dimension, move in enumerate(moves(points, points < FINE)):
            moved = jnp.dot(move, inverse, precision=HIGHEST, preferred_element_type=f32)
            out_ref[4 * level + 1 + dimension] = two_way(moved)


def inverses(block_fine, block_mid, block_coarse):
    return pl.pallas_call(
        inverses_body,
        out_shape=jax.ShapeDtypeStruct((12, LANES, 2 * LANES), bf16),
        scratch_shapes=[pltpu.VMEM((LANES, LANES), f32)],
        compiler_params=pltpu.CompilerParams(vmem_limit_bytes=8 * MIB),
        cost_estimate=pl.CostEstimate(
            flops=2_000_000_000, bytes_accessed=20_000_000, transcendentals=0
        ),
        name="inverses",
    )(block_fine, block_mid, block_coarse)


def two_way(values):
    hi = values.astype(bf16)
    lo = (values - hi.astype(f32)).astype(bf16)
    return jnp.concatenate([hi, lo], axis=1)


def times(values, *tables):
    values = jnp.concatenate([two_way(value) for value in values], axis=1)
    stack = []
    for table in tables:
        high = table[:, 0:LANES]
        stack += [table, jnp.concatenate([high, jnp.zeros_like(high)], axis=1)]
    result = jnp.dot(values, jnp.concatenate(stack, axis=0), preferred_element_type=f32)
    return result[:, 0:LANES] + result[:, LANES : 2 * LANES]


def exchanges(points, in_lanes):
    nodes = points**3
    tables = []
    for dimension, stride in enumerate((points * points, points, 1)):
        table = np.zeros((LANES, LANES), np.float32)
        for place in range(EX if in_lanes else 1):
            for node in range(nodes):
                index = (node // stride) % points
                for end, step in ((0, -1), (points - 1, 1)):
                    if index != end:
                        continue
                    source = place * 32 + node - step * (points - 1) * stride
                    if dimension == 0 and in_lanes:
                        if not 0 <= place + step < EX:
                            continue
                        source += step * 32
                    table[source, place * 32 + node] = 1.0
        tables.append(table)
    return tables


class Faces:
    def __init__(self, points, in_lanes):
        lane, row = iota((EY, LANES), 1), iota((EY, LANES), 0)
        local = lane % 32 if in_lanes else lane
        self.masks = []
        for dimension, stride in enumerate((points * points, points, 1)):
            index = (local // stride) % points
            first, last = index == 0, index == points - 1
            if dimension == 1:
                self.masks.append((last & (row > 0), first & (row < EY - 1)))
            else:
                self.masks.append((last, first))

    def moved(self, dimension, faces):
        reach = (FINE - 1) * FINE ** (2 - dimension)
        lane = iota((1, LANES), 1)
        index = (lane // FINE ** (2 - dimension)) % FINE
        node = lane < FINE**3
        order = jnp.where((index == 0) & node, lane + reach, LANES - 1)
        order = jnp.where((index == FINE - 1) & node, lane - reach, order)
        turned = jnp.take_along_axis(
            faces, jnp.broadcast_to(order, faces.shape), axis=1, mode="promise_in_bounds"
        )
        return jnp.where(order < LANES - 1, turned, 0.0)

    def select(self, dimension, before, after):
        from_before, from_after = self.masks[dimension]
        if before is None:
            before, after = 0.0, flat_slabs(after)
        elif after is None:
            before, after = flat_slabs(before), 0.0
        else:
            before, after = flat_slabs(before), flat_slabs(after)
        if dimension == 1:
            after = jnp.where(from_after[None], after, 0.0)
        return flat(jnp.where(from_before[None], before, after))


def flat_slabs(values):
    return values.reshape(-1, EY, LANES)


CHUNK = 16


def cuts(start, stop, chunk=CHUNK):
    count = -(-(stop - start) // chunk)
    edges = [start + (stop - start) * piece // count for piece in range(count + 1)]
    return list(zip(edges[:-1], edges[1:]))


def flat(values):
    return values.reshape(-1, LANES)


def beside(ref, rows):
    before = jnp.concatenate([ref[rows, HALF - 1 : EY - 1, :], ref[rows, 0:HALF, :]], axis=1)
    after = jnp.concatenate([ref[rows, HALF:EY, :], ref[rows, 1 : HALF + 1, :]], axis=1)
    return flat(before), flat(after)


def cycle_body(
    bounds_ref,
    mine_ref,
    other_ref,
    tables_ref,
    down_ref,
    up_ref,
    low_ref,
    high_ref,
    out_ref,
    start,
    ping,
    pong,
    left,
    left_x,
    left_y,
    left_z,
    mid_start,
    mid_ping,
    mid_pong,
    mid_left,
    mid_left_x,
    mid_left_y,
    mid_left_z,
    mask,
):
    lefts = (left_x, left_y, left_z)
    mid_lefts = (mid_left_x, mid_left_y, mid_left_z)
    fine_faces = Faces(FINE, False)
    mid_faces = Faces(MID, True)
    coarse_faces = Faces(COARSE, True)
    fine_table, *fine_tables = [tables_ref[i] for i in range(4)]
    mid_table, *mid_tables = [tables_ref[i] for i in range(4, 8)]
    coarse_table, *coarse_tables = [tables_ref[i] for i in range(8, 12)]

    slab = iota((WINDOW, EY, LANES), 0)
    mask[...] = jnp.where((slab >= bounds_ref[0]) & (slab < bounds_ref[1]), 1.0, 0.0)
    upper_is_mine = bounds_ref[2] == 1

    def at(x, a, b):
        return slice(x * WINDOW + a, x * WINDOW + b)

    def get(ref, rows):
        return flat(ref[rows, :, :])

    def put(ref, rows, values):
        ref[rows, :, :] = values.reshape(-1, EY, LANES)

    def fine_gather(ref, x, a, b):
        return (
            fine_faces.select(
                0,
                get(ref, at(x - 1, a, b)) if x > 0 else None,
                get(ref, at(x + 1, a, b)) if x < EX - 1 else None,
            ),
            fine_faces.select(1, *beside(ref, at(x, a, b))),
            fine_faces.select(2, get(ref, at(x, a - 1, b - 1)), get(ref, at(x, a + 1, b + 1))),
        )

    def fine_sweep(source, target, a, b, keep):
        for x in range(EX):
            for c, d in cuts(a, b):
                rows = at(x, c, d)
                faces = fine_gather(source, x, c, d)
                if keep is not None:
                    for ref, face in zip(lefts, faces):
                        if keep[0]:
                            put(ref, rows, keep[1] * face)
                        else:
                            put(ref, rows, get(ref, rows) + keep[1] * face)
                moved = 0.3 * get(source, rows) + get(start, rows) + times(faces, *fine_tables)
                put(target, rows, moved * get(mask, at(0, c, d)))

    for x in range(EX):
        for c, d in cuts(0, WINDOW):
            values = []
            for z in range(c, d):
                for y in range(2):
                    first = x * HALF * WINDOW + y * SPLIT + z % SPLIT
                    place = pl.ds(first, HALF, stride=WINDOW)
                    mine, other = mine_ref[place, :], other_ref[place, :]
                    if z < SPLIT:
                        mine, other = other, mine
                    values.append(jnp.where(upper_is_mine, mine, other))
            values = jnp.concatenate(values, axis=0)
            rows = at(x, c, d)
            put(left, rows, values)
            put(start, rows, 2.0 * times((values,), fine_table))

    fine_sweep(start, ping, 1, WINDOW - 1, (True, -0.21))
    fine_sweep(ping, pong, 2, WINDOW - 2, (False, -0.7))

    def mid_gather(faces, ref, a, b):
        here = get(ref, at(0, a, b))
        return (
            here,
            faces.select(1, *beside(ref, at(0, a, b))),
            faces.select(2, get(ref, at(0, a - 1, b - 1)), get(ref, at(0, a + 1, b + 1))),
        )

    for c, d in cuts(3, WINDOW - 3):
        values = []
        for x in range(EX):
            rest = 0.027 * get(left, at(x, c, d))
            for dimension, face in enumerate(fine_gather(pong, x, c, d)):
                face = 0.5 * (get(lefts[dimension], at(x, c, d)) + face)
                rest = rest + fine_faces.moved(dimension, face)
            values.append(rest)
        tables = [down_ref[x] for x in range(EX)]
        rows = at(0, c, d)
        total = times(values, *tables) * get(mask, rows)
        put(mid_left, rows, total)
        put(mid_start, rows, 2.0 * times((total,), mid_table))

    def mid_sweep(faces, tables, base, source, target, margin, keep=None):
        for c, d in cuts(margin, WINDOW - margin, CHUNK // 2):
            rows = at(0, c, d)
            values = mid_gather(faces, source, c, d)
            if keep is not None:
                for ref, face in zip(mid_lefts, values):
                    if keep[0]:
                        put(ref, rows, keep[1] * face)
                    else:
                        put(ref, rows, get(ref, rows) + keep[1] * face)
            moved = 0.3 * get(source, rows) + get(base, rows) + times(values, *tables)
            put(target, rows, moved * get(mask, rows))

    mid_sweep(mid_faces, mid_tables, mid_start, mid_start, mid_ping, 4, (True, -0.21))
    mid_sweep(mid_faces, mid_tables, mid_start, mid_ping, mid_pong, 5, (False, -0.7))

    base = ping.at[0:WINDOW]
    even = ping.at[WINDOW : 2 * WINDOW]
    odd = ping.at[2 * WINDOW : 3 * WINDOW]
    for c, d in cuts(6, WINDOW - 6):
        rows = at(0, c, d)
        values = [get(mid_left, rows)]
        for ref, face in zip(mid_lefts, mid_gather(mid_faces, mid_pong, c, d)):
            values.append(get(ref, rows) + face)
        low = times(values, *[low_ref[i] for i in range(4)]) * get(mask, rows)
        put(base, rows, 2.0 * times((low,), coarse_table))
    mid_sweep(coarse_faces, coarse_tables, base, base, even, 7)
    mid_sweep(coarse_faces, coarse_tables, base, even, odd, 8)
    mid_sweep(coarse_faces, coarse_tables, base, odd, even, 9)

    for c, d in cuts(9, WINDOW - 9):
        rows = at(0, c, d)
        put(mid_pong, rows, get(mid_pong, rows) + times((get(even, rows),), high_ref[...]))
    mid_sweep(mid_faces, mid_tables, mid_start, mid_pong, mid_ping, 10)
    mid_sweep(mid_faces, mid_tables, mid_start, mid_ping, mid_pong, 11)
    mid_sweep(mid_faces, mid_tables, mid_start, mid_pong, mid_ping, 12)

    lifted = get(mid_ping, at(0, 12, WINDOW - 12))
    for x in range(EX):
        rows = at(x, 12, WINDOW - 12)
        put(pong, rows, get(pong, rows) + times((lifted,), up_ref[x]))
    fine_sweep(pong, ping, 13, WINDOW - 13, None)
    fine_sweep(ping, pong, 14, WINDOW - 14, None)
    fine_sweep(pong, ping, RADIUS, WINDOW - RADIUS, None)

    for x in range(EX):
        for z in range(OWN):
            for y in range(2):
                values = ping[x * WINDOW + RADIUS + z, y * HALF : (y + 1) * HALF, :]
                first = x * HALF * OWN * 2 + z * 2 + y
                out_ref[pl.ds(first, HALF, stride=2 * OWN), :] = values


def cycle(bounds, mine, other, tables, down, up, low, high):
    big = pltpu.VMEM((EX * WINDOW, EY, LANES), f32)
    small = pltpu.VMEM((WINDOW, EY, LANES), f32)
    vmem = pl.BlockSpec(memory_space=pltpu.VMEM)
    return pl.pallas_call(
        cycle_body,
        out_shape=jax.ShapeDtypeStruct((EX * HALF * 2 * OWN, LANES), f32),
        in_specs=[pl.BlockSpec(memory_space=pltpu.SMEM)] + [vmem] * 7,
        out_specs=vmem,
        scratch_shapes=[big] * 7 + [small] * 8,
        compiler_params=pltpu.CompilerParams(vmem_limit_bytes=20 * MIB),
        name="cycle",
    )(bounds, mine, other, tables, down, up, low, high)


def per_device(fine_source_field, scaling, block_fine, block_mid, block_coarse):
    count_z = scaling.shape[2]
    parts = lax.axis_size("gx") * lax.axis_size("gy")
    groups = lax.axis_size("gz")
    down, up, low, high = transfer_tables()
    group = lax.axis_index("gz")
    core = group % 2
    cores = core.astype(jnp.int32).reshape(1)

    own, edge = pack(cores, fine_source_field, scaling)
    ties = [(i, i + 1) for i in range(1, groups - 1, 2)]
    pairs = [(i, i ^ 1) for i in range(groups)]
    halo = lax.ppermute(edge, "gz", ties + [(j, i) for i, j in ties])
    sibling = lax.ppermute(own, "gz", pairs)
    chunks = window(cores, own, sibling, halo, parts)
    chunks, *matrices = lax.optimization_barrier((chunks, block_fine, block_mid, block_coarse))
    recv = lax.all_to_all(
        chunks.reshape(parts * WINDOW // 2, 2, LANES), ("gx", "gy"), 0, 0, tiled=True
    ).reshape(parts * WINDOW, LANES)
    recv, tables = lax.optimization_barrier((recv, inverses(*matrices)))
    other = lax.ppermute(recv, "gz", pairs)

    part = lax.axis_index("gx") * lax.axis_size("gy") + lax.axis_index("gy")
    first = (group - core) * count_z + OWN * part - RADIUS
    bounds = jnp.stack(
        [jnp.maximum(0, -first), jnp.minimum(WINDOW, groups * count_z - first), core]
    )
    result = cycle(
        bounds.astype(jnp.int32), recv, other, tables, down, up, low, high
    )
    back = lax.all_to_all(
        result.reshape(parts, 2 * OWN, LANES), ("gx", "gy"), 0, 0, tiled=True
    ).reshape(parts * 2 * OWN, LANES)
    return unpack(cores, back, scaling, fine_source_field.shape)


def solution(mesh):
    in_specs = (P("gx", "gy", "gz"), P("gx", "gy", "gz"), P(), P(), P())
    out_specs = P("gx", "gy", "gz")
    return jax.shard_map(
        per_device, mesh=mesh, in_specs=in_specs, out_specs=out_specs, check_vma=False
    )
```

```python
import math

import jax
import jax.numpy as jnp
import numpy as np
from jax import lax
from jax.experimental import pallas as pl
from jax.experimental.pallas import tpu as pltpu
from jax.sharding import PartitionSpec as P

FINE = 5
MID = 3
COARSE = 2
CSWEEPS = 4
RADIUS = 15
HALO = 16
OWN = 4
WINDOW = OWN + 2 * RADIUS
SPLIT = WINDOW // 2
EX = 4
EY = 16
HALF = EY // 2
LANES = 128

f32 = jnp.float32
bf16 = jnp.bfloat16
HIGHEST = lax.Precision.HIGHEST
MIB = 1 << 20


def gll_points(points):
    if points == 5:
        return np.array([-1.0, -math.sqrt(3.0 / 7.0), 0.0, math.sqrt(3.0 / 7.0), 1.0])
    if points == 3:
        return np.array([-1.0, 0.0, 1.0])
    return np.array([-1.0, 1.0])


def lagrange(fine_points, coarse_points):
    fine_nodes = gll_points(fine_points)
    coarse_nodes = gll_points(coarse_points)
    table = np.ones((fine_points, coarse_points))
    for column in range(coarse_points):
        for other in range(coarse_points):
            if other != column:
                table[:, column] *= (fine_nodes - coarse_nodes[other]) / (
                    coarse_nodes[column] - coarse_nodes[other]
                )
    return table


def halves(table):
    table = np.asarray(table, np.float32)
    hi = table.astype(jnp.bfloat16)
    lo = (table - hi.astype(np.float32)).astype(jnp.bfloat16)
    return np.concatenate([hi, lo], axis=1)


def transfer_tables():
    fine_mid = np.kron(np.kron(lagrange(5, 3), lagrange(5, 3)), lagrange(5, 3))
    mid_coarse = np.kron(np.kron(lagrange(3, 2), lagrange(3, 2)), lagrange(3, 2))
    down, up = [], []
    for place in range(EX):
        table = np.zeros((LANES, LANES))
        table[:125, place * 32 : place * 32 + 27] = fine_mid
        down.append(halves(table))
        up.append(halves(table.T))
    middle = np.zeros((LANES, LANES), np.float32)
    for place in range(EX):
        middle[place * 32 : place * 32 + 27, place * 8 : place * 8 + 8] = mid_coarse
    low = [0.027 * middle]
    low += [0.5 * np.dot(move, middle) for move in exchanges(MID, True)]
    high = [np.roll(middle.T, 32 * copy, axis=0) for copy in range(3)]
    return np.stack(down), np.stack(up), np.stack(low), np.stack(high)


def iota(shape, dimension):
    return lax.broadcasted_iota(jnp.int32, shape, dimension)


def three_way(values):
    one = values.astype(bf16)
    rest = values - one.astype(f32)
    two = rest.astype(bf16)
    three = (rest - two.astype(f32)).astype(bf16)
    return jnp.concatenate([one, two, three], axis=0)


def place_of(lane, y):
    i, j, k = lane // (FINE * FINE), (lane // FINE) % FINE, lane % FINE
    return jnp.where(lane < FINE**3, k * LANES + i * 2 * FINE + y * FINE + j, -1)


def pack_body(core_ref, field_ref, scale_ref, own_ref, edge_ref, lines, turned, *, count_z):
    lines[...] = jnp.zeros_like(lines)
    for i in range(FINE):
        lines[i * 2 * FINE : (i + 1) * 2 * FINE, 0 : count_z * FINE] = field_ref[i]
    for part in range(lines.shape[1] // LANES):
        lanes = slice(part * LANES, (part + 1) * LANES)
        turned[lanes, :] = lines[:, lanes].T
    lane = iota((1, 2 * LANES), 1)
    place = place_of(lane % LANES, lane // LANES)
    table = jnp.where(iota((FINE * LANES, 2 * LANES), 0) == place, 1.0, 0.0).astype(bf16)
    values = [turned[pl.ds(k, count_z, stride=FINE), :] for k in range(FINE)]
    nodes = jnp.dot(
        three_way(jnp.concatenate(values, axis=1)), table, preferred_element_type=f32
    )
    nodes = nodes[0:count_z] + nodes[count_z : 2 * count_z] + nodes[2 * count_z : 3 * count_z]
    scale = scale_ref[0].T
    for y in range(2):
        own_ref[y] = nodes[:, y * LANES : (y + 1) * LANES] / scale[:, y : y + 1]
    start = pl.multiple_of(core_ref[0] * (count_z - HALO), HALO)
    for y in range(2):
        edge_ref[y] = own_ref[y, pl.ds(start, HALO), :]


def pack(core, field, scaling):
    count_z = scaling.shape[2]
    width = -(-count_z * FINE // LANES) * LANES

    def body(*refs):
        pack_body(*refs, count_z=count_z)

    vmem = pl.BlockSpec(memory_space=pltpu.VMEM)
    return pl.pallas_call(
        body,
        out_shape=(
            jax.ShapeDtypeStruct((2, count_z, LANES), f32),
            jax.ShapeDtypeStruct((2, HALO, LANES), f32),
        ),
        in_specs=[pl.BlockSpec(memory_space=pltpu.SMEM), vmem, vmem],
        out_specs=(vmem, vmem),
        scratch_shapes=[pltpu.VMEM((LANES, width), f32), pltpu.VMEM((width, LANES), f32)],
        compiler_params=pltpu.CompilerParams(vmem_limit_bytes=8 * MIB),
        name="pack",
    )(core, field, scaling)


def window_body(core_ref, own_ref, sibling_ref, halo_ref, out_ref, line, *, parts):
    count_z = own_ref.shape[1]
    for core in range(2):
        places = (HALO, HALO + count_z, 0) if core == 0 else (count_z, 0, 2 * count_z)

        @pl.when(core_ref[0] == core)
        def _(core=core, places=places):
            for ref, place in zip((own_ref, sibling_ref, halo_ref), places):
                line[:, place : place + ref.shape[1], :] = ref[...]
            first = HALO - RADIUS if core == 0 else SPLIT - RADIUS
            for part in range(parts):
                for y in range(2):
                    start = first + OWN * part
                    row = part * WINDOW + y * SPLIT
                    out_ref[row : row + SPLIT, :] = line[y, start : start + SPLIT, :]


def window(core, own, sibling, halo, parts):
    def body(*refs):
        window_body(*refs, parts=parts)

    vmem = pl.BlockSpec(memory_space=pltpu.VMEM)
    return pl.pallas_call(
        body,
        out_shape=jax.ShapeDtypeStruct((parts * WINDOW, LANES), f32),
        in_specs=[pl.BlockSpec(memory_space=pltpu.SMEM), vmem, vmem, vmem],
        out_specs=vmem,
        scratch_shapes=[pltpu.VMEM((2, 2 * own.shape[1] + HALO, LANES), f32)],
        compiler_params=pltpu.CompilerParams(vmem_limit_bytes=8 * MIB),
        name="window",
    )(core, own, sibling, halo)


def unpack_body(core_ref, back_ref, scale_ref, out_ref, turned, *, count_z):
    scale = scale_ref[0].T
    base = core_ref[0] * (2 * count_z)
    rows = [
        back_ref[pl.ds(base + y, count_z, stride=2), :] / scale[:, y : y + 1] for y in range(2)
    ]
    table = jnp.concatenate(
        [
            jnp.where(
                iota((LANES, FINE * LANES), 1) == place_of(iota((LANES, 1), 0), y), 1.0, 0.0
            )
            for y in range(2)
        ],
        axis=0,
    ).astype(bf16)
    spread = jnp.dot(
        three_way(jnp.concatenate(rows, axis=1)), table, preferred_element_type=f32
    )
    spread = spread[0:count_z] + spread[count_z : 2 * count_z] + spread[2 * count_z : 3 * count_z]
    for k in range(FINE):
        turned[pl.ds(k, count_z, stride=FINE), :] = spread[:, k * LANES : (k + 1) * LANES]
    lines = [
        turned[part * LANES : (part + 1) * LANES, :].T for part in range(turned.shape[0] // LANES)
    ]
    lines = jnp.concatenate(lines, axis=1)
    for i in range(FINE):
        out_ref[i] = lines[i * 2 * FINE : (i + 1) * 2 * FINE, 0 : count_z * FINE]


def unpack(core, back, scaling, shape):
    count_z = scaling.shape[2]
    width = -(-count_z * FINE // LANES) * LANES

    def body(*refs):
        unpack_body(*refs, count_z=count_z)

    vmem = pl.BlockSpec(memory_space=pltpu.VMEM)
    return pl.pallas_call(
        body,
        out_shape=jax.ShapeDtypeStruct(shape, f32),
        in_specs=[pl.BlockSpec(memory_space=pltpu.SMEM), vmem, vmem],
        out_specs=vmem,
        scratch_shapes=[pltpu.VMEM((width, LANES), f32)],
        compiler_params=pltpu.CompilerParams(vmem_limit_bytes=8 * MIB),
        name="unpack",
    )(core, back, scaling)


def shifted_block(ref, pad, points):
    nodes = points**3
    pad[...] = jnp.zeros((LANES, LANES), f32)
    pad[0:nodes, 0:nodes] = ref[...]
    lane, row = iota((LANES, LANES), 1), iota((LANES, LANES), 0)
    count = jnp.zeros((LANES, LANES), f32)
    for stride in (points * points, points, 1):
        index = (lane // stride) % points
        count = count + jnp.where((index == 0) | (index == points - 1), 0.5, 0.0)
    diagonal = jnp.where(lane < nodes, count, 1.0)
    return pad[...] + jnp.where(lane == row, diagonal, 0.0)


def invert(matrix, panels):
    lane, row = iota((LANES, LANES), 1), iota((LANES, LANES), 0)
    lane1, lane16, row16 = iota((1, LANES), 1), iota((16, LANES), 1), iota((16, LANES), 0)
    for panel in range(panels):
        top = panel * 16
        rows = matrix[top : top + 16, :]
        for step in range(0, 16, 2):
            pivot = top + step
            left = jnp.broadcast_to(rows[:, pivot : pivot + 1], (16, LANES))
            right = jnp.broadcast_to(rows[:, pivot + 1 : pivot + 2], (16, LANES))
            a, b = left[step : step + 1], right[step : step + 1]
            c, d = left[step + 1 : step + 2], right[step + 1 : step + 2]
            scale = 1.0 / (a * d - b * c)
            here = (lane1 == pivot) | (lane1 == pivot + 1)
            one = jnp.where(here, jnp.where(lane1 == pivot, 1.0, 0.0), rows[step : step + 1])
            two = jnp.where(here, jnp.where(lane1 == pivot, 0.0, 1.0), rows[step + 1 : step + 2])
            one, two = (d * one - b * two) * scale, (a * two - c * one) * scale
            others = jnp.where((lane16 == pivot) | (lane16 == pivot + 1), 0.0, rows)
            others = others - left * one - right * two
            rows = jnp.where(row16 == step, one, jnp.where(row16 == step + 1, two, others))
        stacked = jnp.concatenate([rows] * 8, axis=0)
        inside = (lane >= top) & (lane < top + 16)
        update = jnp.dot(
            jnp.where(inside, matrix, 0.0), stacked, precision=HIGHEST, preferred_element_type=f32
        )
        matrix = jnp.where(
            (row >= top) & (row < top + 16), stacked, jnp.where(inside, 0.0, matrix) - update
        )
    return matrix


def exact(left, right):
    return jnp.dot(left, right, precision=HIGHEST, preferred_element_type=f32)


def repeated(matrix, width):
    lane, row = iota((LANES, LANES), 1), iota((LANES, LANES), 0)
    used = (lane < EX * width) & (row < EX * width)
    pick = jnp.where((row % width == lane) & (lane < width), 1.0, 0.0)
    put = jnp.where((lane % width == row) & (row < width), 1.0, 0.0)
    wide = exact(exact(pick, matrix), put)
    return jnp.where(used & (row // width == lane // width), wide, 0.0)


def moves(points, width):
    lane, row = iota((1, LANES), 1), iota((LANES, LANES), 0)
    local, place = lane % width, lane // width
    tables = []
    for dimension, stride in enumerate((points * points, points, 1)):
        index = (local // stride) % points
        first = (index == 0) & (local < points**3)
        last = (index == points - 1) & (local < points**3)
        reach = (points - 1) * stride
        if dimension == 0 and width < LANES:
            first, last = first & (place > 0), last & (place < EX - 1)
            reach = reach - width
        source = jnp.where(first, lane + reach, jnp.where(last, lane - reach, -LANES))
        tables.append((row, source))
    return tables


def inverses_body(fine_ref, mid_ref, coarse_ref, low_ref, high_ref, out_ref, pad):
    lane, row = iota((LANES, LANES), 1), iota((LANES, LANES), 0)
    coarse = invert(shifted_block(coarse_ref, pad, COARSE), 1)
    mid = invert(shifted_block(mid_ref, pad, MID), 2)
    fine = invert(shifted_block(fine_ref, pad, FINE), 8)
    levels = ((fine, FINE, LANES), (repeated(mid, 32), MID, 32))
    for level, (inverse, points, width) in enumerate(levels):
        inverse = 0.35 * inverse
        out_ref[4 * level] = two_way(inverse)
        moved = []
        for dimension, (own, source) in enumerate(moves(points, width)):
            moved.append(exact(jnp.where(own == source, 1.0, 0.0), inverse))
            out_ref[4 * level + 1 + dimension] = two_way(moved[dimension])
    lifted = 0.3 * high_ref[0]
    for dimension in range(3):
        lifted = lifted + exact(high_ref[dimension], moved[dimension])
    out_ref[8] = two_way(lifted)
    copies = jnp.where((lane % 32 == row) & (lane < 96), 1.0, 0.0)
    inverse = exact(0.35 * repeated(coarse, 8), copies)
    gather = jnp.zeros((LANES, LANES), f32)
    for dimension, (own, source) in enumerate(moves(COARSE, 8)):
        gather = gather + jnp.where((own == source + 32 * dimension) & (lane < 32), 1.0, 0.0)
    out_ref[9] = two_way(exact(gather, inverse))
    for part in range(4):
        out_ref[10 + part] = two_way(exact(low_ref[part], 2.0 * inverse))


def inverses(block_fine, block_mid, block_coarse, low, high):
    return pl.pallas_call(
        inverses_body,
        out_shape=jax.ShapeDtypeStruct((14, LANES, 2 * LANES), bf16),
        scratch_shapes=[pltpu.VMEM((LANES, LANES), f32)],
        compiler_params=pltpu.CompilerParams(vmem_limit_bytes=8 * MIB),
        cost_estimate=pl.CostEstimate(
            flops=2_000_000_000, bytes_accessed=20_000_000, transcendentals=0
        ),
        name="inverses",
    )(block_fine, block_mid, block_coarse, low, high)


def two_way(values):
    hi = values.astype(bf16)
    lo = (values - hi.astype(f32)).astype(bf16)
    return jnp.concatenate([hi, lo], axis=1)


def times(values, *tables):
    values = jnp.concatenate([two_way(value) for value in values], axis=1)
    stack = []
    for table in tables:
        high = table[:, 0:LANES]
        stack += [table, jnp.concatenate([high, jnp.zeros_like(high)], axis=1)]
    result = jnp.dot(values, jnp.concatenate(stack, axis=0), preferred_element_type=f32)
    return result[:, 0:LANES] + result[:, LANES : 2 * LANES]


def exchanges(points, in_lanes):
    nodes = points**3
    tables = []
    for dimension, stride in enumerate((points * points, points, 1)):
        table = np.zeros((LANES, LANES), np.float32)
        for place in range(EX if in_lanes else 1):
            for node in range(nodes):
                index = (node // stride) % points
                for end, step in ((0, -1), (points - 1, 1)):
                    if index != end:
                        continue
                    source = place * 32 + node - step * (points - 1) * stride
                    if dimension == 0 and in_lanes:
                        if not 0 <= place + step < EX:
                            continue
                        source += step * 32
                    table[source, place * 32 + node] = 1.0
        tables.append(table)
    return tables


class Faces:
    def __init__(self, points, in_lanes):
        lane, row = iota((EY, LANES), 1), iota((EY, LANES), 0)
        local = lane % 32 if in_lanes else lane
        self.masks = []
        for dimension, stride in enumerate((points * points, points, 1)):
            index = (local // stride) % points
            first, last = index == 0, index == points - 1
            if dimension == 1:
                self.masks.append((last & (row > 0), first & (row < EY - 1)))
            else:
                self.masks.append((last, first))

    def moved(self, dimension, faces):
        reach = (FINE - 1) * FINE ** (2 - dimension)
        lane = iota((1, LANES), 1)
        index = (lane // FINE ** (2 - dimension)) % FINE
        node = lane < FINE**3
        order = jnp.where((index == 0) & node, lane + reach, LANES - 1)
        order = jnp.where((index == FINE - 1) & node, lane - reach, order)
        turned = jnp.take_along_axis(
            faces, jnp.broadcast_to(order, faces.shape), axis=1, mode="promise_in_bounds"
        )
        return jnp.where(order < LANES - 1, turned, 0.0)

    def select(self, dimension, before, after):
        from_before, from_after = self.masks[dimension]
        if before is None:
            before, after = 0.0, flat_slabs(after)
        elif after is None:
            before, after = flat_slabs(before), 0.0
        else:
            before, after = flat_slabs(before), flat_slabs(after)
        if dimension == 1:
            after = jnp.where(from_after[None], after, 0.0)
        return flat(jnp.where(from_before[None], before, after))


def coarse_rows():
    lane, row = iota((EY, LANES), 1), iota((EY, LANES), 0)
    copy, j, k = lane // 32, (lane // 2) % 2, lane % 2
    masks = (
        copy == 0,
        (copy == 1) & (j == 1) & (row > 0),
        (copy == 1) & (j == 0) & (row < EY - 1),
        (copy == 2) & (k == 1),
        (copy == 2) & (k == 0),
    )

    def build(*parts):
        result = 0.0
        for mask, part in zip(masks, parts):
            result = jnp.where(mask[None], flat_slabs(part), result)
        return flat(result)

    return build


def flat_slabs(values):
    return values.reshape(-1, EY, LANES)


CHUNK = 16


def cuts(start, stop, chunk=CHUNK):
    count = -(-(stop - start) // chunk)
    edges = [start + (stop - start) * piece // count for piece in range(count + 1)]
    return list(zip(edges[:-1], edges[1:]))


def flat(values):
    return values.reshape(-1, LANES)


def beside(ref, rows):
    before = jnp.concatenate([ref[rows, HALF - 1 : EY - 1, :], ref[rows, 0:HALF, :]], axis=1)
    after = jnp.concatenate([ref[rows, HALF:EY, :], ref[rows, 1 : HALF + 1, :]], axis=1)
    return flat(before), flat(after)


def cycle_body(
    bounds_ref,
    mine_ref,
    other_ref,
    tables_ref,
    down_ref,
    up_ref,
    out_ref,
    start,
    ping,
    pong,
    left,
    left_x,
    left_y,
    left_z,
    mid_start,
    mid_ping,
    mid_pong,
    mid_left,
    mid_left_x,
    mid_left_y,
    mid_left_z,
    mask,
):
    lefts = (left_x, left_y, left_z)
    mid_lefts = (mid_left_x, mid_left_y, mid_left_z)
    fine_faces = Faces(FINE, False)
    mid_faces = Faces(MID, True)
    coarse_row = coarse_rows()
    fine_table, *fine_tables = [tables_ref[i] for i in range(4)]
    mid_table, *mid_tables = [tables_ref[i] for i in range(4, 8)]
    lift_table, coarse_table, *low_tables = [tables_ref[i] for i in range(8, 14)]

    slab = iota((WINDOW, EY, LANES), 0)
    mask[...] = jnp.where((slab >= bounds_ref[0]) & (slab < bounds_ref[1]), 1.0, 0.0)
    upper_is_mine = bounds_ref[2] == 1

    def at(x, a, b):
        return slice(x * WINDOW + a, x * WINDOW + b)

    def get(ref, rows):
        return flat(ref[rows, :, :])

    def put(ref, rows, values):
        ref[rows, :, :] = values.reshape(-1, EY, LANES)

    def fine_gather(ref, x, a, b):
        return (
            fine_faces.select(
                0,
                get(ref, at(x - 1, a, b)) if x > 0 else None,
                get(ref, at(x + 1, a, b)) if x < EX - 1 else None,
            ),
            fine_faces.select(1, *beside(ref, at(x, a, b))),
            fine_faces.select(2, get(ref, at(x, a - 1, b - 1)), get(ref, at(x, a + 1, b + 1))),
        )

    def fine_sweep(source, target, a, b, keep):
        for x in range(EX):
            for c, d in cuts(a, b):
                rows = at(x, c, d)
                faces = fine_gather(source, x, c, d)
                if keep is not None:
                    for ref, face in zip(lefts, faces):
                        if keep[0]:
                            put(ref, rows, keep[1] * face)
                        else:
                            put(ref, rows, get(ref, rows) + keep[1] * face)
                moved = 0.3 * get(source, rows) + get(start, rows) + times(faces, *fine_tables)
                put(target, rows, moved * get(mask, at(0, c, d)))

    for x in range(EX):
        for c, d in cuts(0, WINDOW):
            values = []
            for z in range(c, d):
                for y in range(2):
                    first = x * HALF * WINDOW + y * SPLIT + z % SPLIT
                    place = pl.ds(first, HALF, stride=WINDOW)
                    mine, other = mine_ref[place, :], other_ref[place, :]
                    if z < SPLIT:
                        mine, other = other, mine
                    values.append(jnp.where(upper_is_mine, mine, other))
            values = jnp.concatenate(values, axis=0)
            rows = at(x, c, d)
            put(left, rows, values)
            put(start, rows, 2.0 * times((values,), fine_table))

    fine_sweep(start, ping, 1, WINDOW - 1, (True, -0.21))
    fine_sweep(ping, pong, 2, WINDOW - 2, (False, -0.7))

    def mid_gather(faces, ref, a, b):
        here = get(ref, at(0, a, b))
        return (
            here,
            faces.select(1, *beside(ref, at(0, a, b))),
            faces.select(2, get(ref, at(0, a - 1, b - 1)), get(ref, at(0, a + 1, b + 1))),
        )

    for c, d in cuts(3, WINDOW - 3):
        values = []
        for x in range(EX):
            rest = 0.027 * get(left, at(x, c, d))
            for dimension, face in enumerate(fine_gather(pong, x, c, d)):
                face = 0.5 * (get(lefts[dimension], at(x, c, d)) + face)
                rest = rest + fine_faces.moved(dimension, face)
            values.append(rest)
        tables = [down_ref[x] for x in range(EX)]
        rows = at(0, c, d)
        total = times(values, *tables) * get(mask, rows)
        put(mid_left, rows, total)
        put(mid_start, rows, 2.0 * times((total,), mid_table))

    def mid_sweep(faces, tables, base, source, target, margin, keep=None):
        for c, d in cuts(margin, WINDOW - margin, CHUNK // 2):
            rows = at(0, c, d)
            values = mid_gather(faces, source, c, d)
            if keep is not None:
                for ref, face in zip(mid_lefts, values):
                    if keep[0]:
                        put(ref, rows, keep[1] * face)
                    else:
                        put(ref, rows, get(ref, rows) + keep[1] * face)
            moved = 0.3 * get(source, rows) + get(base, rows) + times(values, *tables)
            put(target, rows, moved * get(mask, rows))

    mid_sweep(mid_faces, mid_tables, mid_start, mid_start, mid_ping, 4, (True, -0.21))
    mid_sweep(mid_faces, mid_tables, mid_start, mid_ping, mid_pong, 5, (False, -0.7))

    base = ping.at[0:WINDOW]
    even = ping.at[WINDOW : 2 * WINDOW]
    odd = ping.at[2 * WINDOW : 3 * WINDOW]
    for c, d in cuts(6, WINDOW - 6):
        rows = at(0, c, d)
        faces = mid_gather(mid_faces, mid_pong, c, d)
        values = [get(mid_left, rows)]
        for ref, face in zip(mid_lefts, faces):
            values.append(get(ref, rows) + face)
        put(base, rows, times(values, *low_tables) * get(mask, rows))

    for c, d in cuts(10, WINDOW - 10, CHUNK // 2):
        rows = at(0, c, d)
        moved = times(mid_gather(mid_faces, mid_pong, c, d), *mid_tables)
        put(mid_left, rows, 0.3 * get(mid_pong, rows) + get(mid_start, rows) + moved)

    def coarse_gather(ref, a, b):
        rows = at(0, a, b)
        near = beside(ref, rows)
        return coarse_row(
            get(ref, rows), *near, get(ref, at(0, a - 1, b - 1)), get(ref, at(0, a + 1, b + 1))
        )

    def coarse_sweep(source, target, margin):
        for c, d in cuts(margin, WINDOW - margin, CHUNK // 2):
            rows = at(0, c, d)
            moved = times((coarse_gather(source, c, d),), coarse_table)
            moved = 0.3 * get(source, rows) + get(base, rows) + moved
            put(target, rows, moved * get(mask, rows))

    coarse_sweep(base, even, 7)
    coarse_sweep(even, odd, 8)
    coarse_sweep(odd, even, 9)

    for c, d in cuts(10, WINDOW - 10, CHUNK // 2):
        rows = at(0, c, d)
        moved = get(mid_left, rows) + times((coarse_gather(even, c, d),), lift_table)
        put(mid_ping, rows, moved * get(mask, rows))
    mid_sweep(mid_faces, mid_tables, mid_start, mid_ping, mid_pong, 11)
    mid_sweep(mid_faces, mid_tables, mid_start, mid_pong, mid_ping, 12)

    lifted = get(mid_ping, at(0, 12, WINDOW - 12))
    for x in range(EX):
        rows = at(x, 12, WINDOW - 12)
        put(pong, rows, get(pong, rows) + times((lifted,), up_ref[x]))
    fine_sweep(pong, ping, 13, WINDOW - 13, None)
    fine_sweep(ping, pong, 14, WINDOW - 14, None)
    fine_sweep(pong, ping, RADIUS, WINDOW - RADIUS, None)

    for x in range(EX):
        for z in range(OWN):
            for y in range(2):
                values = ping[x * WINDOW + RADIUS + z, y * HALF : (y + 1) * HALF, :]
                first = x * HALF * OWN * 2 + z * 2 + y
                out_ref[pl.ds(first, HALF, stride=2 * OWN), :] = values


def cycle(bounds, mine, other, tables, down, up):
    big = pltpu.VMEM((EX * WINDOW, EY, LANES), f32)
    small = pltpu.VMEM((WINDOW, EY, LANES), f32)
    vmem = pl.BlockSpec(memory_space=pltpu.VMEM)
    return pl.pallas_call(
        cycle_body,
        out_shape=jax.ShapeDtypeStruct((EX * HALF * 2 * OWN, LANES), f32),
        in_specs=[pl.BlockSpec(memory_space=pltpu.SMEM)] + [vmem] * 5,
        out_specs=vmem,
        scratch_shapes=[big] * 7 + [small] * 8,
        compiler_params=pltpu.CompilerParams(vmem_limit_bytes=20 * MIB),
        name="cycle",
    )(bounds, mine, other, tables, down, up)


def per_device(fine_source_field, scaling, block_fine, block_mid, block_coarse):
    count_z = scaling.shape[2]
    parts = lax.axis_size("gx") * lax.axis_size("gy")
    groups = lax.axis_size("gz")
    down, up, low, high = transfer_tables()
    group = lax.axis_index("gz")
    core = group % 2
    cores = core.astype(jnp.int32).reshape(1)

    own, edge = pack(cores, fine_source_field, scaling)
    ties = [(i, i + 1) for i in range(1, groups - 1, 2)]
    pairs = [(i, i ^ 1) for i in range(groups)]
    halo = lax.ppermute(edge, "gz", ties + [(j, i) for i, j in ties])
    sibling = lax.ppermute(own, "gz", pairs)
    chunks = window(cores, own, sibling, halo, parts)
    chunks, *matrices = lax.optimization_barrier((chunks, block_fine, block_mid, block_coarse))
    recv = lax.all_to_all(
        chunks.reshape(parts * WINDOW // 2, 2, LANES), ("gx", "gy"), 0, 0, tiled=True
    ).reshape(parts * WINDOW, LANES)
    recv, tables = lax.optimization_barrier((recv, inverses(*matrices, low, high)))
    other = lax.ppermute(recv, "gz", pairs)

    part = lax.axis_index("gx") * lax.axis_size("gy") + lax.axis_index("gy")
    first = (group - core) * count_z + OWN * part - RADIUS
    bounds = jnp.stack(
        [jnp.maximum(0, -first), jnp.minimum(WINDOW, groups * count_z - first), core]
    )
    result = cycle(
        bounds.astype(jnp.int32), recv, other, tables, down, up
    )
    back = lax.all_to_all(
        result.reshape(parts, 2 * OWN, LANES), ("gx", "gy"), 0, 0, tiled=True
    ).reshape(parts * 2 * OWN, LANES)
    return unpack(cores, back, scaling, fine_source_field.shape)


def solution(mesh):
    in_specs = (P("gx", "gy", "gz"), P("gx", "gy", "gz"), P(), P(), P())
    out_specs = P("gx", "gy", "gz")
    return jax.shard_map(
        per_device, mesh=mesh, in_specs=in_specs, out_specs=out_specs, check_vma=False
    )
```

```python
import math

import jax
import jax.numpy as jnp
import numpy as np
from jax import lax
from jax.experimental import pallas as pl
from jax.experimental.pallas import tpu as pltpu
from jax.sharding import PartitionSpec as P

FINE = 5
MID = 3
COARSE = 2
CSWEEPS = 4
RADIUS = 15
HALO = 16
OWN = 4
WINDOW = OWN + 2 * RADIUS
SPLIT = WINDOW // 2
EX = 4
EY = 16
HALF = EY // 2
LANES = 128

f32 = jnp.float32
bf16 = jnp.bfloat16
HIGHEST = lax.Precision.HIGHEST
MIB = 1 << 20


def gll_points(points):
    if points == 5:
        return np.array([-1.0, -math.sqrt(3.0 / 7.0), 0.0, math.sqrt(3.0 / 7.0), 1.0])
    if points == 3:
        return np.array([-1.0, 0.0, 1.0])
    return np.array([-1.0, 1.0])


def lagrange(fine_points, coarse_points):
    fine_nodes = gll_points(fine_points)
    coarse_nodes = gll_points(coarse_points)
    table = np.ones((fine_points, coarse_points))
    for column in range(coarse_points):
        for other in range(coarse_points):
            if other != column:
                table[:, column] *= (fine_nodes - coarse_nodes[other]) / (
                    coarse_nodes[column] - coarse_nodes[other]
                )
    return table


def halves(table):
    table = np.asarray(table, np.float32)
    hi = table.astype(jnp.bfloat16)
    lo = (table - hi.astype(np.float32)).astype(jnp.bfloat16)
    return np.concatenate([hi, lo], axis=1)


def transfer_tables():
    fine_mid = np.kron(np.kron(lagrange(5, 3), lagrange(5, 3)), lagrange(5, 3))
    mid_coarse = np.kron(np.kron(lagrange(3, 2), lagrange(3, 2)), lagrange(3, 2))
    down, up = [], []
    for place in range(EX):
        table = np.zeros((LANES, LANES))
        table[:125, place * 32 : place * 32 + 27] = fine_mid
        down.append(halves(table))
        up.append(halves(table.T))
    middle = np.zeros((LANES, LANES), np.float32)
    for place in range(EX):
        middle[place * 32 : place * 32 + 27, place * 8 : place * 8 + 8] = mid_coarse
    low = [0.027 * middle]
    low += [0.5 * np.dot(move, middle) for move in exchanges(MID, True)]
    high = [np.roll(middle.T, 32 * copy, axis=0) for copy in range(3)]
    return np.stack(down), np.stack(up), np.stack(low), np.stack(high)


def iota(shape, dimension):
    return lax.broadcasted_iota(jnp.int32, shape, dimension)


def three_way(values):
    one = values.astype(bf16)
    rest = values - one.astype(f32)
    two = rest.astype(bf16)
    three = (rest - two.astype(f32)).astype(bf16)
    return jnp.concatenate([one, two, three], axis=0)


def place_of(lane, y):
    i, j, k = lane // (FINE * FINE), (lane // FINE) % FINE, lane % FINE
    return jnp.where(lane < FINE**3, k * LANES + i * 2 * FINE + y * FINE + j, -1)


def pack_body(core_ref, field_ref, scale_ref, own_ref, edge_ref, lines, turned, *, count_z):
    lines[...] = jnp.zeros_like(lines)
    for i in range(FINE):
        lines[i * 2 * FINE : (i + 1) * 2 * FINE, 0 : count_z * FINE] = field_ref[i]
    for part in range(lines.shape[1] // LANES):
        lanes = slice(part * LANES, (part + 1) * LANES)
        turned[lanes, :] = lines[:, lanes].T
    lane = iota((1, 2 * LANES), 1)
    place = place_of(lane % LANES, lane // LANES)
    table = jnp.where(iota((FINE * LANES, 2 * LANES), 0) == place, 1.0, 0.0).astype(bf16)
    values = [turned[pl.ds(k, count_z, stride=FINE), :] for k in range(FINE)]
    nodes = jnp.dot(
        three_way(jnp.concatenate(values, axis=1)), table, preferred_element_type=f32
    )
    nodes = nodes[0:count_z] + nodes[count_z : 2 * count_z] + nodes[2 * count_z : 3 * count_z]
    scale = scale_ref[0].T
    for y in range(2):
        own_ref[y] = nodes[:, y * LANES : (y + 1) * LANES] / scale[:, y : y + 1]
    start = pl.multiple_of(core_ref[0] * (count_z - HALO), HALO)
    for y in range(2):
        edge_ref[y] = own_ref[y, pl.ds(start, HALO), :]


def pack(core, field, scaling):
    count_z = scaling.shape[2]
    width = -(-count_z * FINE // LANES) * LANES

    def body(*refs):
        pack_body(*refs, count_z=count_z)

    vmem = pl.BlockSpec(memory_space=pltpu.VMEM)
    return pl.pallas_call(
        body,
        out_shape=(
            jax.ShapeDtypeStruct((2, count_z, LANES), f32),
            jax.ShapeDtypeStruct((2, HALO, LANES), f32),
        ),
        in_specs=[pl.BlockSpec(memory_space=pltpu.SMEM), vmem, vmem],
        out_specs=(vmem, vmem),
        scratch_shapes=[pltpu.VMEM((LANES, width), f32), pltpu.VMEM((width, LANES), f32)],
        compiler_params=pltpu.CompilerParams(vmem_limit_bytes=8 * MIB),
        name="pack",
    )(core, field, scaling)


def starts(core, parts):
    first = HALO - RADIUS if core == 0 else HALO + SPLIT - RADIUS
    return [first + OWN * part for part in parts]


def lay(line, core, count_z, own_ref, sibling_ref):
    own_at, sibling_at = (HALO, HALO + count_z) if core == 0 else (HALO + count_z, HALO)
    line[:, own_at : own_at + count_z, :] = own_ref[...]
    line[:, sibling_at : sibling_at + count_z, :] = sibling_ref[...]


def cut(line, core, parts, out_ref):
    for row, start in enumerate(starts(core, parts)):
        for y in range(2):
            place = row * WINDOW + y * SPLIT
            out_ref[place : place + SPLIT, :] = line[y, start : start + SPLIT, :]


def window_body(core_ref, own_ref, sibling_ref, out_ref, line, *, parts):
    count_z = own_ref.shape[1]
    line[:, 0:HALO, :] = jnp.zeros((2, HALO, LANES), f32)
    line[:, HALO + 2 * count_z :, :] = jnp.zeros((2, HALO, LANES), f32)
    for core in range(2):

        @pl.when(core_ref[0] == core)
        def _(core=core):
            lay(line, core, count_z, own_ref, sibling_ref)
            cut(line, core, range(parts), out_ref)


def window(core, own, sibling, parts):
    def body(*refs):
        window_body(*refs, parts=parts)

    vmem = pl.BlockSpec(memory_space=pltpu.VMEM)
    return pl.pallas_call(
        body,
        out_shape=jax.ShapeDtypeStruct((parts * WINDOW, LANES), f32),
        in_specs=[pl.BlockSpec(memory_space=pltpu.SMEM), vmem, vmem],
        out_specs=vmem,
        scratch_shapes=[pltpu.VMEM((2, 2 * own.shape[1] + 2 * HALO, LANES), f32)],
        compiler_params=pltpu.CompilerParams(vmem_limit_bytes=8 * MIB),
        name="window",
    )(core, own, sibling)


ENDS = 4


def ends_body(core_ref, own_ref, sibling_ref, halo_ref, _, out_ref, line, block, sem, *, parts):
    count_z = own_ref.shape[1]
    for core in range(2):

        @pl.when(core_ref[0] == core)
        def _(core=core):
            lay(line, core, count_z, own_ref, sibling_ref)
            halo_at = 0 if core == 0 else HALO + 2 * count_z
            line[:, halo_at : halo_at + HALO, :] = halo_ref[...]
            first = 0 if core == 0 else parts - ENDS
            cut(line, core, range(first, first + ENDS), block)
            place = out_ref.at[first * WINDOW : (first + ENDS) * WINDOW, :]
            copy = pltpu.make_async_copy(block, place, sem)
            copy.start()
            copy.wait()


def ends(core, own, sibling, halo, chunks, parts):
    def body(*refs):
        ends_body(*refs, parts=parts)

    vmem = pl.BlockSpec(memory_space=pltpu.VMEM)
    anywhere = pl.BlockSpec(memory_space=pl.ANY)
    return pl.pallas_call(
        body,
        out_shape=jax.ShapeDtypeStruct(chunks.shape, f32),
        in_specs=[pl.BlockSpec(memory_space=pltpu.SMEM), vmem, vmem, vmem, anywhere],
        out_specs=anywhere,
        scratch_shapes=[
            pltpu.VMEM((2, 2 * own.shape[1] + 2 * HALO, LANES), f32),
            pltpu.VMEM((ENDS * WINDOW, LANES), f32),
            pltpu.SemaphoreType.DMA,
        ],
        input_output_aliases={4: 0},
        compiler_params=pltpu.CompilerParams(vmem_limit_bytes=8 * MIB),
        name="ends",
    )(core, own, sibling, halo, chunks)


def unpack_body(core_ref, back_ref, scale_ref, out_ref, turned, *, count_z):
    scale = scale_ref[0].T
    base = core_ref[0] * (2 * count_z)
    rows = [
        back_ref[pl.ds(base + y, count_z, stride=2), :] / scale[:, y : y + 1] for y in range(2)
    ]
    table = jnp.concatenate(
        [
            jnp.where(
                iota((LANES, FINE * LANES), 1) == place_of(iota((LANES, 1), 0), y), 1.0, 0.0
            )
            for y in range(2)
        ],
        axis=0,
    ).astype(bf16)
    spread = jnp.dot(
        three_way(jnp.concatenate(rows, axis=1)), table, preferred_element_type=f32
    )
    spread = spread[0:count_z] + spread[count_z : 2 * count_z] + spread[2 * count_z : 3 * count_z]
    for k in range(FINE):
        turned[pl.ds(k, count_z, stride=FINE), :] = spread[:, k * LANES : (k + 1) * LANES]
    lines = [
        turned[part * LANES : (part + 1) * LANES, :].T for part in range(turned.shape[0] // LANES)
    ]
    lines = jnp.concatenate(lines, axis=1)
    for i in range(FINE):
        out_ref[i] = lines[i * 2 * FINE : (i + 1) * 2 * FINE, 0 : count_z * FINE]


def unpack(core, back, scaling, shape):
    count_z = scaling.shape[2]
    width = -(-count_z * FINE // LANES) * LANES

    def body(*refs):
        unpack_body(*refs, count_z=count_z)

    vmem = pl.BlockSpec(memory_space=pltpu.VMEM)
    return pl.pallas_call(
        body,
        out_shape=jax.ShapeDtypeStruct(shape, f32),
        in_specs=[pl.BlockSpec(memory_space=pltpu.SMEM), vmem, vmem],
        out_specs=vmem,
        scratch_shapes=[pltpu.VMEM((width, LANES), f32)],
        compiler_params=pltpu.CompilerParams(vmem_limit_bytes=8 * MIB),
        name="unpack",
    )(core, back, scaling)


def shifted_block(ref, pad, points):
    nodes = points**3
    pad[...] = jnp.zeros((LANES, LANES), f32)
    pad[0:nodes, 0:nodes] = ref[...]
    lane, row = iota((LANES, LANES), 1), iota((LANES, LANES), 0)
    count = jnp.zeros((LANES, LANES), f32)
    for stride in (points * points, points, 1):
        index = (lane // stride) % points
        count = count + jnp.where((index == 0) | (index == points - 1), 0.5, 0.0)
    diagonal = jnp.where(lane < nodes, count, 1.0)
    return pad[...] + jnp.where(lane == row, diagonal, 0.0)


def invert(matrix, panels):
    lane, row = iota((LANES, LANES), 1), iota((LANES, LANES), 0)
    lane1, lane16, row16 = iota((1, LANES), 1), iota((16, LANES), 1), iota((16, LANES), 0)
    for panel in range(panels):
        top = panel * 16
        rows = matrix[top : top + 16, :]
        for step in range(0, 16, 2):
            pivot = top + step
            left = jnp.broadcast_to(rows[:, pivot : pivot + 1], (16, LANES))
            right = jnp.broadcast_to(rows[:, pivot + 1 : pivot + 2], (16, LANES))
            a, b = left[step : step + 1], right[step : step + 1]
            c, d = left[step + 1 : step + 2], right[step + 1 : step + 2]
            scale = 1.0 / (a * d - b * c)
            here = (lane1 == pivot) | (lane1 == pivot + 1)
            one = jnp.where(here, jnp.where(lane1 == pivot, 1.0, 0.0), rows[step : step + 1])
            two = jnp.where(here, jnp.where(lane1 == pivot, 0.0, 1.0), rows[step + 1 : step + 2])
            one, two = (d * one - b * two) * scale, (a * two - c * one) * scale
            others = jnp.where((lane16 == pivot) | (lane16 == pivot + 1), 0.0, rows)
            others = others - left * one - right * two
            rows = jnp.where(row16 == step, one, jnp.where(row16 == step + 1, two, others))
        stacked = jnp.concatenate([rows] * 8, axis=0)
        inside = (lane >= top) & (lane < top + 16)
        update = jnp.dot(
            jnp.where(inside, matrix, 0.0), stacked, precision=HIGHEST, preferred_element_type=f32
        )
        matrix = jnp.where(
            (row >= top) & (row < top + 16), stacked, jnp.where(inside, 0.0, matrix) - update
        )
    return matrix


def exact(left, right):
    return jnp.dot(left, right, precision=HIGHEST, preferred_element_type=f32)


def repeated(matrix, width):
    lane, row = iota((LANES, LANES), 1), iota((LANES, LANES), 0)
    used = (lane < EX * width) & (row < EX * width)
    pick = jnp.where((row % width == lane) & (lane < width), 1.0, 0.0)
    put = jnp.where((lane % width == row) & (row < width), 1.0, 0.0)
    wide = exact(exact(pick, matrix), put)
    return jnp.where(used & (row // width == lane // width), wide, 0.0)


def moves(points, width):
    lane, row = iota((1, LANES), 1), iota((LANES, LANES), 0)
    local, place = lane % width, lane // width
    tables = []
    for dimension, stride in enumerate((points * points, points, 1)):
        index = (local // stride) % points
        first = (index == 0) & (local < points**3)
        last = (index == points - 1) & (local < points**3)
        reach = (points - 1) * stride
        if dimension == 0 and width < LANES:
            first, last = first & (place > 0), last & (place < EX - 1)
            reach = reach - width
        source = jnp.where(first, lane + reach, jnp.where(last, lane - reach, -LANES))
        tables.append((row, source))
    return tables


def inverses_body(fine_ref, mid_ref, coarse_ref, low_ref, high_ref, out_ref, pad):
    lane, row = iota((LANES, LANES), 1), iota((LANES, LANES), 0)
    coarse = invert(shifted_block(coarse_ref, pad, COARSE), 1)
    mid = invert(shifted_block(mid_ref, pad, MID), 2)
    fine = invert(shifted_block(fine_ref, pad, FINE), 8)
    levels = ((fine, FINE, LANES), (repeated(mid, 32), MID, 32))
    for level, (inverse, points, width) in enumerate(levels):
        inverse = 0.35 * inverse
        out_ref[4 * level] = two_way(inverse)
        moved = []
        for dimension, (own, source) in enumerate(moves(points, width)):
            moved.append(exact(jnp.where(own == source, 1.0, 0.0), inverse))
            out_ref[4 * level + 1 + dimension] = two_way(moved[dimension])
    lifted = 0.3 * high_ref[0]
    for dimension in range(3):
        lifted = lifted + exact(high_ref[dimension], moved[dimension])
    out_ref[8] = two_way(lifted)
    copies = jnp.where((lane % 32 == row) & (lane < 96), 1.0, 0.0)
    inverse = exact(0.35 * repeated(coarse, 8), copies)
    gather = jnp.zeros((LANES, LANES), f32)
    for dimension, (own, source) in enumerate(moves(COARSE, 8)):
        gather = gather + jnp.where((own == source + 32 * dimension) & (lane < 32), 1.0, 0.0)
    out_ref[9] = two_way(exact(gather, inverse))
    for part in range(4):
        out_ref[10 + part] = two_way(exact(low_ref[part], 2.0 * inverse))


def inverses(block_fine, block_mid, block_coarse, low, high):
    return pl.pallas_call(
        inverses_body,
        out_shape=jax.ShapeDtypeStruct((14, LANES, 2 * LANES), bf16),
        scratch_shapes=[pltpu.VMEM((LANES, LANES), f32)],
        compiler_params=pltpu.CompilerParams(vmem_limit_bytes=8 * MIB),
        cost_estimate=pl.CostEstimate(
            flops=2_000_000_000, bytes_accessed=20_000_000, transcendentals=0
        ),
        name="inverses",
    )(block_fine, block_mid, block_coarse, low, high)


def two_way(values):
    hi = values.astype(bf16)
    lo = (values - hi.astype(f32)).astype(bf16)
    return jnp.concatenate([hi, lo], axis=1)


def times(values, *tables):
    values = jnp.concatenate([two_way(value) for value in values], axis=1)
    stack = []
    for table in tables:
        high = table[:, 0:LANES]
        stack += [table, jnp.concatenate([high, jnp.zeros_like(high)], axis=1)]
    result = jnp.dot(values, jnp.concatenate(stack, axis=0), preferred_element_type=f32)
    return result[:, 0:LANES] + result[:, LANES : 2 * LANES]


def exchanges(points, in_lanes):
    nodes = points**3
    tables = []
    for dimension, stride in enumerate((points * points, points, 1)):
        table = np.zeros((LANES, LANES), np.float32)
        for place in range(EX if in_lanes else 1):
            for node in range(nodes):
                index = (node // stride) % points
                for end, step in ((0, -1), (points - 1, 1)):
                    if index != end:
                        continue
                    source = place * 32 + node - step * (points - 1) * stride
                    if dimension == 0 and in_lanes:
                        if not 0 <= place + step < EX:
                            continue
                        source += step * 32
                    table[source, place * 32 + node] = 1.0
        tables.append(table)
    return tables


class Faces:
    def __init__(self, points, in_lanes):
        lane, row = iota((EY, LANES), 1), iota((EY, LANES), 0)
        local = lane % 32 if in_lanes else lane
        self.masks = []
        for dimension, stride in enumerate((points * points, points, 1)):
            index = (local // stride) % points
            first, last = index == 0, index == points - 1
            if dimension == 1:
                self.masks.append((last & (row > 0), first & (row < EY - 1)))
            else:
                self.masks.append((last, first))

    def moved(self, dimension, faces):
        reach = (FINE - 1) * FINE ** (2 - dimension)
        lane = iota((1, LANES), 1)
        index = (lane // FINE ** (2 - dimension)) % FINE
        node = lane < FINE**3
        order = jnp.where((index == 0) & node, lane + reach, LANES - 1)
        order = jnp.where((index == FINE - 1) & node, lane - reach, order)
        turned = jnp.take_along_axis(
            faces, jnp.broadcast_to(order, faces.shape), axis=1, mode="promise_in_bounds"
        )
        return jnp.where(order < LANES - 1, turned, 0.0)

    def select(self, dimension, before, after):
        from_before, from_after = self.masks[dimension]
        if before is None:
            before, after = 0.0, flat_slabs(after)
        elif after is None:
            before, after = flat_slabs(before), 0.0
        else:
            before, after = flat_slabs(before), flat_slabs(after)
        if dimension == 1:
            after = jnp.where(from_after[None], after, 0.0)
        return flat(jnp.where(from_before[None], before, after))


def coarse_rows():
    lane, row = iota((EY, LANES), 1), iota((EY, LANES), 0)
    copy, j, k = lane // 32, (lane // 2) % 2, lane % 2
    masks = (
        copy == 0,
        (copy == 1) & (j == 1) & (row > 0),
        (copy == 1) & (j == 0) & (row < EY - 1),
        (copy == 2) & (k == 1),
        (copy == 2) & (k == 0),
    )

    def build(*parts):
        result = 0.0
        for mask, part in zip(masks, parts):
            result = jnp.where(mask[None], flat_slabs(part), result)
        return flat(result)

    return build


def flat_slabs(values):
    return values.reshape(-1, EY, LANES)


CHUNK = 16


def cuts(start, stop, chunk=CHUNK):
    count = -(-(stop - start) // chunk)
    edges = [start + (stop - start) * piece // count for piece in range(count + 1)]
    return list(zip(edges[:-1], edges[1:]))


def flat(values):
    return values.reshape(-1, LANES)


def beside(ref, rows):
    before = jnp.concatenate([ref[rows, HALF - 1 : EY - 1, :], ref[rows, 0:HALF, :]], axis=1)
    after = jnp.concatenate([ref[rows, HALF:EY, :], ref[rows, 1 : HALF + 1, :]], axis=1)
    return flat(before), flat(after)


def cycle_body(
    bounds_ref,
    mine_ref,
    other_ref,
    tables_ref,
    down_ref,
    up_ref,
    out_ref,
    start,
    ping,
    pong,
    left,
    left_x,
    left_y,
    left_z,
    mid_start,
    mid_ping,
    mid_pong,
    mid_left,
    mid_left_x,
    mid_left_y,
    mid_left_z,
    mask,
):
    lefts = (left_x, left_y, left_z)
    mid_lefts = (mid_left_x, mid_left_y, mid_left_z)
    fine_faces = Faces(FINE, False)
    mid_faces = Faces(MID, True)
    coarse_row = coarse_rows()
    fine_table, *fine_tables = [tables_ref[i] for i in range(4)]
    mid_table, *mid_tables = [tables_ref[i] for i in range(4, 8)]
    lift_table, coarse_table, *low_tables = [tables_ref[i] for i in range(8, 14)]

    slab = iota((WINDOW, EY, LANES), 0)
    mask[...] = jnp.where((slab >= bounds_ref[0]) & (slab < bounds_ref[1]), 1.0, 0.0)
    upper_is_mine = bounds_ref[2] == 1

    def at(x, a, b):
        return slice(x * WINDOW + a, x * WINDOW + b)

    def get(ref, rows):
        return flat(ref[rows, :, :])

    def put(ref, rows, values):
        ref[rows, :, :] = values.reshape(-1, EY, LANES)

    def fine_gather(ref, x, a, b):
        return (
            fine_faces.select(
                0,
                get(ref, at(x - 1, a, b)) if x > 0 else None,
                get(ref, at(x + 1, a, b)) if x < EX - 1 else None,
            ),
            fine_faces.select(1, *beside(ref, at(x, a, b))),
            fine_faces.select(2, get(ref, at(x, a - 1, b - 1)), get(ref, at(x, a + 1, b + 1))),
        )

    def fine_sweep(source, target, a, b, keep):
        for x in range(EX):
            for c, d in cuts(a, b):
                rows = at(x, c, d)
                faces = fine_gather(source, x, c, d)
                if keep is not None:
                    for ref, face in zip(lefts, faces):
                        if keep[0]:
                            put(ref, rows, keep[1] * face)
                        else:
                            put(ref, rows, get(ref, rows) + keep[1] * face)
                moved = 0.3 * get(source, rows) + get(start, rows) + times(faces, *fine_tables)
                put(target, rows, moved * get(mask, at(0, c, d)))

    for x in range(EX):
        for c, d in cuts(0, WINDOW):
            values = []
            for z in range(c, d):
                for y in range(2):
                    first = x * HALF * WINDOW + y * SPLIT + z % SPLIT
                    place = pl.ds(first, HALF, stride=WINDOW)
                    mine, other = mine_ref[place, :], other_ref[place, :]
                    if z < SPLIT:
                        mine, other = other, mine
                    values.append(jnp.where(upper_is_mine, mine, other))
            values = jnp.concatenate(values, axis=0)
            rows = at(x, c, d)
            put(left, rows, values)
            put(start, rows, 2.0 * times((values,), fine_table))

    fine_sweep(start, ping, 1, WINDOW - 1, (True, -0.21))
    fine_sweep(ping, pong, 2, WINDOW - 2, (False, -0.7))

    def mid_gather(faces, ref, a, b):
        here = get(ref, at(0, a, b))
        return (
            here,
            faces.select(1, *beside(ref, at(0, a, b))),
            faces.select(2, get(ref, at(0, a - 1, b - 1)), get(ref, at(0, a + 1, b + 1))),
        )

    for c, d in cuts(3, WINDOW - 3):
        values = []
        for x in range(EX):
            rest = 0.027 * get(left, at(x, c, d))
            for dimension, face in enumerate(fine_gather(pong, x, c, d)):
                face = 0.5 * (get(lefts[dimension], at(x, c, d)) + face)
                rest = rest + fine_faces.moved(dimension, face)
            values.append(rest)
        tables = [down_ref[x] for x in range(EX)]
        rows = at(0, c, d)
        total = times(values, *tables) * get(mask, rows)
        put(mid_left, rows, total)
        put(mid_start, rows, 2.0 * times((total,), mid_table))

    def mid_sweep(faces, tables, base, source, target, margin, keep=None):
        for c, d in cuts(margin, WINDOW - margin, CHUNK // 2):
            rows = at(0, c, d)
            values = mid_gather(faces, source, c, d)
            if keep is not None:
                for ref, face in zip(mid_lefts, values):
                    if keep[0]:
                        put(ref, rows, keep[1] * face)
                    else:
                        put(ref, rows, get(ref, rows) + keep[1] * face)
            moved = 0.3 * get(source, rows) + get(base, rows) + times(values, *tables)
            put(target, rows, moved * get(mask, rows))

    mid_sweep(mid_faces, mid_tables, mid_start, mid_start, mid_ping, 4, (True, -0.21))
    mid_sweep(mid_faces, mid_tables, mid_start, mid_ping, mid_pong, 5, (False, -0.7))

    base = ping.at[0:WINDOW]
    even = ping.at[WINDOW : 2 * WINDOW]
    odd = ping.at[2 * WINDOW : 3 * WINDOW]
    for c, d in cuts(6, WINDOW - 6):
        rows = at(0, c, d)
        faces = mid_gather(mid_faces, mid_pong, c, d)
        values = [get(mid_left, rows)]
        for ref, face in zip(mid_lefts, faces):
            values.append(get(ref, rows) + face)
        put(base, rows, times(values, *low_tables) * get(mask, rows))

    for c, d in cuts(10, WINDOW - 10, CHUNK // 2):
        rows = at(0, c, d)
        moved = times(mid_gather(mid_faces, mid_pong, c, d), *mid_tables)
        put(mid_left, rows, 0.3 * get(mid_pong, rows) + get(mid_start, rows) + moved)

    def coarse_gather(ref, a, b):
        rows = at(0, a, b)
        near = beside(ref, rows)
        return coarse_row(
            get(ref, rows), *near, get(ref, at(0, a - 1, b - 1)), get(ref, at(0, a + 1, b + 1))
        )

    def coarse_sweep(source, target, margin):
        for c, d in cuts(margin, WINDOW - margin, CHUNK // 2):
            rows = at(0, c, d)
            moved = times((coarse_gather(source, c, d),), coarse_table)
            moved = 0.3 * get(source, rows) + get(base, rows) + moved
            put(target, rows, moved * get(mask, rows))

    coarse_sweep(base, even, 7)
    coarse_sweep(even, odd, 8)
    coarse_sweep(odd, even, 9)

    for c, d in cuts(10, WINDOW - 10, CHUNK // 2):
        rows = at(0, c, d)
        moved = get(mid_left, rows) + times((coarse_gather(even, c, d),), lift_table)
        put(mid_ping, rows, moved * get(mask, rows))
    mid_sweep(mid_faces, mid_tables, mid_start, mid_ping, mid_pong, 11)
    mid_sweep(mid_faces, mid_tables, mid_start, mid_pong, mid_ping, 12)

    lifted = get(mid_ping, at(0, 12, WINDOW - 12))
    for x in range(EX):
        rows = at(x, 12, WINDOW - 12)
        put(pong, rows, get(pong, rows) + times((lifted,), up_ref[x]))
    fine_sweep(pong, ping, 13, WINDOW - 13, None)
    fine_sweep(ping, pong, 14, WINDOW - 14, None)
    fine_sweep(pong, ping, RADIUS, WINDOW - RADIUS, None)

    for x in range(EX):
        for z in range(OWN):
            for y in range(2):
                values = ping[x * WINDOW + RADIUS + z, y * HALF : (y + 1) * HALF, :]
                first = x * HALF * OWN * 2 + z * 2 + y
                out_ref[pl.ds(first, HALF, stride=2 * OWN), :] = values


def cycle(bounds, mine, other, tables, down, up):
    big = pltpu.VMEM((EX * WINDOW, EY, LANES), f32)
    small = pltpu.VMEM((WINDOW, EY, LANES), f32)
    vmem = pl.BlockSpec(memory_space=pltpu.VMEM)
    return pl.pallas_call(
        cycle_body,
        out_shape=jax.ShapeDtypeStruct((EX * HALF * 2 * OWN, LANES), f32),
        in_specs=[pl.BlockSpec(memory_space=pltpu.SMEM)] + [vmem] * 5,
        out_specs=vmem,
        scratch_shapes=[big] * 7 + [small] * 8,
        compiler_params=pltpu.CompilerParams(vmem_limit_bytes=20 * MIB),
        name="cycle",
    )(bounds, mine, other, tables, down, up)


def per_device(fine_source_field, scaling, block_fine, block_mid, block_coarse):
    count_z = scaling.shape[2]
    parts = lax.axis_size("gx") * lax.axis_size("gy")
    groups = lax.axis_size("gz")
    down, up, low, high = transfer_tables()
    group = lax.axis_index("gz")
    core = group % 2
    cores = core.astype(jnp.int32).reshape(1)

    own, edge = pack(cores, fine_source_field, scaling)
    ties = [(i, i + 1) for i in range(1, groups - 1, 2)]
    pairs = [(i, i ^ 1) for i in range(groups)]
    halo = lax.ppermute(edge, "gz", ties + [(j, i) for i, j in ties])
    sibling = lax.ppermute(own, "gz", pairs)
    chunks = window(cores, own, sibling, parts)
    chunks = ends(cores, own, sibling, halo, chunks, parts)
    chunks, *matrices = lax.optimization_barrier((chunks, block_fine, block_mid, block_coarse))
    recv = lax.all_to_all(
        chunks.reshape(parts * WINDOW // 2, 2, LANES), ("gx", "gy"), 0, 0, tiled=True
    ).reshape(parts * WINDOW, LANES)
    recv, tables = lax.optimization_barrier((recv, inverses(*matrices, low, high)))
    other = lax.ppermute(recv, "gz", pairs)

    part = lax.axis_index("gx") * lax.axis_size("gy") + lax.axis_index("gy")
    first = (group - core) * count_z + OWN * part - RADIUS
    bounds = jnp.stack(
        [jnp.maximum(0, -first), jnp.minimum(WINDOW, groups * count_z - first), core]
    )
    result = cycle(
        bounds.astype(jnp.int32), recv, other, tables, down, up
    )
    back = lax.all_to_all(
        result.reshape(parts, 2 * OWN, LANES), ("gx", "gy"), 0, 0, tiled=True
    ).reshape(parts * 2 * OWN, LANES)
    return unpack(cores, back, scaling, fine_source_field.shape)


def solution(mesh):
    in_specs = (P("gx", "gy", "gz"), P("gx", "gy", "gz"), P(), P(), P())
    out_specs = P("gx", "gy", "gz")
    return jax.shard_map(
        per_device, mesh=mesh, in_specs=in_specs, out_specs=out_specs, check_vma=False
    )
```

```python
import math

import jax
import jax.numpy as jnp
import numpy as np
from jax import lax
from jax.experimental import pallas as pl
from jax.experimental.pallas import tpu as pltpu
from jax.sharding import PartitionSpec as P

FINE = 5
MID = 3
COARSE = 2
CSWEEPS = 4
RADIUS = 15
HALO = 16
OWN = 4
WINDOW = OWN + 2 * RADIUS
SPLIT = WINDOW // 2
EX = 4
EY = 16
HALF = EY // 2
LANES = 128

f32 = jnp.float32
bf16 = jnp.bfloat16
HIGHEST = lax.Precision.HIGHEST
MIB = 1 << 20


def gll_points(points):
    if points == 5:
        return np.array([-1.0, -math.sqrt(3.0 / 7.0), 0.0, math.sqrt(3.0 / 7.0), 1.0])
    if points == 3:
        return np.array([-1.0, 0.0, 1.0])
    return np.array([-1.0, 1.0])


def lagrange(fine_points, coarse_points):
    fine_nodes = gll_points(fine_points)
    coarse_nodes = gll_points(coarse_points)
    table = np.ones((fine_points, coarse_points))
    for column in range(coarse_points):
        for other in range(coarse_points):
            if other != column:
                table[:, column] *= (fine_nodes - coarse_nodes[other]) / (
                    coarse_nodes[column] - coarse_nodes[other]
                )
    return table


def halves(table):
    table = np.asarray(table, np.float32)
    hi = table.astype(jnp.bfloat16)
    lo = (table - hi.astype(np.float32)).astype(jnp.bfloat16)
    return np.concatenate([hi, lo], axis=1)


def transfer_tables():
    fine_mid = np.kron(np.kron(lagrange(5, 3), lagrange(5, 3)), lagrange(5, 3))
    mid_coarse = np.kron(np.kron(lagrange(3, 2), lagrange(3, 2)), lagrange(3, 2))
    down, up = [], []
    for place in range(EX):
        table = np.zeros((LANES, LANES))
        table[:125, place * 32 : place * 32 + 27] = fine_mid
        down.append(halves(table))
        up.append(halves(table.T))
    middle = np.zeros((LANES, LANES), np.float32)
    for place in range(EX):
        middle[place * 32 : place * 32 + 27, place * 8 : place * 8 + 8] = mid_coarse
    low = [0.027 * middle]
    low += [0.5 * np.dot(move, middle) for move in exchanges(MID, True)]
    high = [np.roll(middle.T, 32 * copy, axis=0) for copy in range(3)]
    return np.stack(down), np.stack(up), np.stack(low), np.stack(high)


def iota(shape, dimension):
    return lax.broadcasted_iota(jnp.int32, shape, dimension)


def three_way(values):
    one = values.astype(bf16)
    rest = values - one.astype(f32)
    two = rest.astype(bf16)
    three = (rest - two.astype(f32)).astype(bf16)
    return jnp.concatenate([one, two, three], axis=0)


def place_of(lane, y):
    i, j, k = lane // (FINE * FINE), (lane // FINE) % FINE, lane % FINE
    return jnp.where(lane < FINE**3, k * LANES + i * 2 * FINE + y * FINE + j, -1)


def pack_body(core_ref, field_ref, scale_ref, own_ref, edge_ref, lines, turned, *, count_z):
    lines[...] = jnp.zeros_like(lines)
    for i in range(FINE):
        lines[i * 2 * FINE : (i + 1) * 2 * FINE, 0 : count_z * FINE] = field_ref[i]
    for part in range(lines.shape[1] // LANES):
        lanes = slice(part * LANES, (part + 1) * LANES)
        turned[lanes, :] = lines[:, lanes].T
    lane = iota((1, 2 * LANES), 1)
    place = place_of(lane % LANES, lane // LANES)
    table = jnp.where(iota((FINE * LANES, 2 * LANES), 0) == place, 1.0, 0.0).astype(bf16)
    values = [turned[pl.ds(k, count_z, stride=FINE), :] for k in range(FINE)]
    nodes = jnp.dot(
        three_way(jnp.concatenate(values, axis=1)), table, preferred_element_type=f32
    )
    nodes = nodes[0:count_z] + nodes[count_z : 2 * count_z] + nodes[2 * count_z : 3 * count_z]
    scale = scale_ref[0].T
    for y in range(2):
        own_ref[y] = nodes[:, y * LANES : (y + 1) * LANES] / scale[:, y : y + 1]
    start = pl.multiple_of(core_ref[0] * (count_z - HALO), HALO)
    for y in range(2):
        edge_ref[y] = own_ref[y, pl.ds(start, HALO), :]


def pack(core, field, scaling):
    count_z = scaling.shape[2]
    width = -(-count_z * FINE // LANES) * LANES

    def body(*refs):
        pack_body(*refs, count_z=count_z)

    vmem = pl.BlockSpec(memory_space=pltpu.VMEM)
    return pl.pallas_call(
        body,
        out_shape=(
            jax.ShapeDtypeStruct((2, count_z, LANES), f32),
            jax.ShapeDtypeStruct((2, HALO, LANES), f32),
        ),
        in_specs=[pl.BlockSpec(memory_space=pltpu.SMEM), vmem, vmem],
        out_specs=(vmem, vmem),
        scratch_shapes=[pltpu.VMEM((LANES, width), f32), pltpu.VMEM((width, LANES), f32)],
        compiler_params=pltpu.CompilerParams(vmem_limit_bytes=60 * MIB),
        name="pack",
    )(core, field, scaling)


PIECES = 4


def window_body(
    core_ref, own_ref, sibling_ref, halo_ref, out_ref, line, block, sems, *, parts
):
    count_z = own_ref.shape[1]
    rows = parts // PIECES * WINDOW
    for core in range(2):
        places = (HALO, HALO + count_z, 0) if core == 0 else (count_z, 0, 2 * count_z)

        @pl.when(core_ref[0] == core)
        def _(core=core, places=places):
            for ref, place in zip((own_ref, sibling_ref, halo_ref), places):
                line[:, place : place + ref.shape[1], :] = ref[...]
            first = HALO - RADIUS if core == 0 else SPLIT - RADIUS
            copies = []
            for part in range(parts):
                for y in range(2):
                    start = first + OWN * part
                    row = part * WINDOW + y * SPLIT
                    block[row : row + SPLIT, :] = line[y, start : start + SPLIT, :]
                if (part + 1) % (parts // PIECES) == 0:
                    piece = part // (parts // PIECES)
                    place = slice(piece * rows, (piece + 1) * rows)
                    copies.append(
                        pltpu.make_async_copy(
                            block.at[place, :], out_ref.at[place, :], sems.at[piece]
                        )
                    )
                    copies[-1].start()
            for copy in copies:
                copy.wait()


def window(core, own, sibling, halo, parts):
    def body(*refs):
        window_body(*refs, parts=parts)

    vmem = pl.BlockSpec(memory_space=pltpu.VMEM)
    return pl.pallas_call(
        body,
        out_shape=jax.ShapeDtypeStruct((parts * WINDOW, LANES), f32),
        in_specs=[pl.BlockSpec(memory_space=pltpu.SMEM), vmem, vmem, vmem],
        out_specs=pl.BlockSpec(memory_space=pl.ANY),
        scratch_shapes=[
            pltpu.VMEM((2, 2 * own.shape[1] + HALO, LANES), f32),
            pltpu.VMEM((parts * WINDOW, LANES), f32),
            pltpu.SemaphoreType.DMA((PIECES,)),
        ],
        compiler_params=pltpu.CompilerParams(vmem_limit_bytes=8 * MIB),
        name="window",
    )(core, own, sibling, halo)


def unpack_body(core_ref, back_ref, scale_ref, out_ref, turned, *, count_z):
    scale = scale_ref[0].T
    base = core_ref[0] * (2 * count_z)
    rows = [
        back_ref[pl.ds(base + y, count_z, stride=2), :] / scale[:, y : y + 1] for y in range(2)
    ]
    table = jnp.concatenate(
        [
            jnp.where(
                iota((LANES, FINE * LANES), 1) == place_of(iota((LANES, 1), 0), y), 1.0, 0.0
            )
            for y in range(2)
        ],
        axis=0,
    ).astype(bf16)
    spread = jnp.dot(
        three_way(jnp.concatenate(rows, axis=1)), table, preferred_element_type=f32
    )
    spread = spread[0:count_z] + spread[count_z : 2 * count_z] + spread[2 * count_z : 3 * count_z]
    for k in range(FINE):
        turned[pl.ds(k, count_z, stride=FINE), :] = spread[:, k * LANES : (k + 1) * LANES]
    lines = [
        turned[part * LANES : (part + 1) * LANES, :].T for part in range(turned.shape[0] // LANES)
    ]
    lines = jnp.concatenate(lines, axis=1)
    for i in range(FINE):
        out_ref[i] = lines[i * 2 * FINE : (i + 1) * 2 * FINE, 0 : count_z * FINE]


def unpack(core, back, scaling, shape):
    count_z = scaling.shape[2]
    width = -(-count_z * FINE // LANES) * LANES

    def body(*refs):
        unpack_body(*refs, count_z=count_z)

    vmem = pl.BlockSpec(memory_space=pltpu.VMEM)
    return pl.pallas_call(
        body,
        out_shape=jax.ShapeDtypeStruct(shape, f32),
        in_specs=[pl.BlockSpec(memory_space=pltpu.SMEM), vmem, vmem],
        out_specs=vmem,
        scratch_shapes=[pltpu.VMEM((width, LANES), f32)],
        compiler_params=pltpu.CompilerParams(vmem_limit_bytes=8 * MIB),
        name="unpack",
    )(core, back, scaling)


def shifted_block(ref, pad, points):
    nodes = points**3
    pad[...] = jnp.zeros((LANES, LANES), f32)
    pad[0:nodes, 0:nodes] = ref[...]
    lane, row = iota((LANES, LANES), 1), iota((LANES, LANES), 0)
    count = jnp.zeros((LANES, LANES), f32)
    for stride in (points * points, points, 1):
        index = (lane // stride) % points
        count = count + jnp.where((index == 0) | (index == points - 1), 0.5, 0.0)
    diagonal = jnp.where(lane < nodes, count, 1.0)
    return pad[...] + jnp.where(lane == row, diagonal, 0.0)


def invert(matrix, panels):
    lane, row = iota((LANES, LANES), 1), iota((LANES, LANES), 0)
    lane1, lane16, row16 = iota((1, LANES), 1), iota((16, LANES), 1), iota((16, LANES), 0)
    for panel in range(panels):
        top = panel * 16
        rows = matrix[top : top + 16, :]
        for step in range(0, 16, 2):
            pivot = top + step
            left = jnp.broadcast_to(rows[:, pivot : pivot + 1], (16, LANES))
            right = jnp.broadcast_to(rows[:, pivot + 1 : pivot + 2], (16, LANES))
            a, b = left[step : step + 1], right[step : step + 1]
            c, d = left[step + 1 : step + 2], right[step + 1 : step + 2]
            scale = 1.0 / (a * d - b * c)
            here = (lane1 == pivot) | (lane1 == pivot + 1)
            one = jnp.where(here, jnp.where(lane1 == pivot, 1.0, 0.0), rows[step : step + 1])
            two = jnp.where(here, jnp.where(lane1 == pivot, 0.0, 1.0), rows[step + 1 : step + 2])
            one, two = (d * one - b * two) * scale, (a * two - c * one) * scale
            others = jnp.where((lane16 == pivot) | (lane16 == pivot + 1), 0.0, rows)
            others = others - left * one - right * two
            rows = jnp.where(row16 == step, one, jnp.where(row16 == step + 1, two, others))
        stacked = jnp.concatenate([rows] * 8, axis=0)
        inside = (lane >= top) & (lane < top + 16)
        update = jnp.dot(
            jnp.where(inside, matrix, 0.0), stacked, precision=HIGHEST, preferred_element_type=f32
        )
        matrix = jnp.where(
            (row >= top) & (row < top + 16), stacked, jnp.where(inside, 0.0, matrix) - update
        )
    return matrix


def exact(left, right):
    return jnp.dot(left, right, precision=HIGHEST, preferred_element_type=f32)


def repeated(matrix, width):
    lane, row = iota((LANES, LANES), 1), iota((LANES, LANES), 0)
    used = (lane < EX * width) & (row < EX * width)
    pick = jnp.where((row % width == lane) & (lane < width), 1.0, 0.0)
    put = jnp.where((lane % width == row) & (row < width), 1.0, 0.0)
    wide = exact(exact(pick, matrix), put)
    return jnp.where(used & (row // width == lane // width), wide, 0.0)


def moves(points, width):
    lane, row = iota((1, LANES), 1), iota((LANES, LANES), 0)
    local, place = lane % width, lane // width
    tables = []
    for dimension, stride in enumerate((points * points, points, 1)):
        index = (local // stride) % points
        first = (index == 0) & (local < points**3)
        last = (index == points - 1) & (local < points**3)
        reach = (points - 1) * stride
        if dimension == 0 and width < LANES:
            first, last = first & (place > 0), last & (place < EX - 1)
            reach = reach - width
        source = jnp.where(first, lane + reach, jnp.where(last, lane - reach, -LANES))
        tables.append((row, source))
    return tables


def inverses_body(fine_ref, mid_ref, coarse_ref, low_ref, high_ref, out_ref, pad):
    lane, row = iota((LANES, LANES), 1), iota((LANES, LANES), 0)
    coarse = invert(shifted_block(coarse_ref, pad, COARSE), 1)
    mid = invert(shifted_block(mid_ref, pad, MID), 2)
    fine = invert(shifted_block(fine_ref, pad, FINE), 8)
    levels = ((fine, FINE, LANES), (repeated(mid, 32), MID, 32))
    for level, (inverse, points, width) in enumerate(levels):
        inverse = 0.35 * inverse
        out_ref[4 * level] = two_way(inverse)
        moved = []
        for dimension, (own, source) in enumerate(moves(points, width)):
            moved.append(exact(jnp.where(own == source, 1.0, 0.0), inverse))
            out_ref[4 * level + 1 + dimension] = two_way(moved[dimension])
    lifted = 0.3 * high_ref[0]
    for dimension in range(3):
        lifted = lifted + exact(high_ref[dimension], moved[dimension])
    out_ref[8] = two_way(lifted)
    copies = jnp.where((lane % 32 == row) & (lane < 96), 1.0, 0.0)
    inverse = exact(0.35 * repeated(coarse, 8), copies)
    gather = jnp.zeros((LANES, LANES), f32)
    for dimension, (own, source) in enumerate(moves(COARSE, 8)):
        gather = gather + jnp.where((own == source + 32 * dimension) & (lane < 32), 1.0, 0.0)
    out_ref[9] = two_way(exact(gather, inverse))
    for part in range(4):
        out_ref[10 + part] = two_way(exact(low_ref[part], 2.0 * inverse))


def inverses(block_fine, block_mid, block_coarse, low, high):
    return pl.pallas_call(
        inverses_body,
        out_shape=jax.ShapeDtypeStruct((14, LANES, 2 * LANES), bf16),
        scratch_shapes=[pltpu.VMEM((LANES, LANES), f32)],
        compiler_params=pltpu.CompilerParams(vmem_limit_bytes=8 * MIB),
        cost_estimate=pl.CostEstimate(
            flops=2_000_000_000, bytes_accessed=20_000_000, transcendentals=0
        ),
        name="inverses",
    )(block_fine, block_mid, block_coarse, low, high)


def two_way(values):
    hi = values.astype(bf16)
    lo = (values - hi.astype(f32)).astype(bf16)
    return jnp.concatenate([hi, lo], axis=1)


def times(values, *tables):
    values = jnp.concatenate([two_way(value) for value in values], axis=1)
    stack = []
    for table in tables:
        high = table[:, 0:LANES]
        stack += [table, jnp.concatenate([high, jnp.zeros_like(high)], axis=1)]
    result = jnp.dot(values, jnp.concatenate(stack, axis=0), preferred_element_type=f32)
    return result[:, 0:LANES] + result[:, LANES : 2 * LANES]


def exchanges(points, in_lanes):
    nodes = points**3
    tables = []
    for dimension, stride in enumerate((points * points, points, 1)):
        table = np.zeros((LANES, LANES), np.float32)
        for place in range(EX if in_lanes else 1):
            for node in range(nodes):
                index = (node // stride) % points
                for end, step in ((0, -1), (points - 1, 1)):
                    if index != end:
                        continue
                    source = place * 32 + node - step * (points - 1) * stride
                    if dimension == 0 and in_lanes:
                        if not 0 <= place + step < EX:
                            continue
                        source += step * 32
                    table[source, place * 32 + node] = 1.0
        tables.append(table)
    return tables


class Faces:
    def __init__(self, points, in_lanes):
        lane, row = iota((EY, LANES), 1), iota((EY, LANES), 0)
        local = lane % 32 if in_lanes else lane
        self.masks = []
        for dimension, stride in enumerate((points * points, points, 1)):
            index = (local // stride) % points
            first, last = index == 0, index == points - 1
            if dimension == 1:
                self.masks.append((last & (row > 0), first & (row < EY - 1)))
            else:
                self.masks.append((last, first))

    def moved(self, dimension, faces):
        reach = (FINE - 1) * FINE ** (2 - dimension)
        lane = iota((1, LANES), 1)
        index = (lane // FINE ** (2 - dimension)) % FINE
        node = lane < FINE**3
        order = jnp.where((index == 0) & node, lane + reach, LANES - 1)
        order = jnp.where((index == FINE - 1) & node, lane - reach, order)
        turned = jnp.take_along_axis(
            faces, jnp.broadcast_to(order, faces.shape), axis=1, mode="promise_in_bounds"
        )
        return jnp.where(order < LANES - 1, turned, 0.0)

    def select(self, dimension, before, after):
        from_before, from_after = self.masks[dimension]
        if before is None:
            before, after = 0.0, flat_slabs(after)
        elif after is None:
            before, after = flat_slabs(before), 0.0
        else:
            before, after = flat_slabs(before), flat_slabs(after)
        if dimension == 1:
            after = jnp.where(from_after[None], after, 0.0)
        return flat(jnp.where(from_before[None], before, after))


def coarse_rows():
    lane, row = iota((EY, LANES), 1), iota((EY, LANES), 0)
    copy, j, k = lane // 32, (lane // 2) % 2, lane % 2
    masks = (
        copy == 0,
        (copy == 1) & (j == 1) & (row > 0),
        (copy == 1) & (j == 0) & (row < EY - 1),
        (copy == 2) & (k == 1),
        (copy == 2) & (k == 0),
    )

    def build(*parts):
        result = 0.0
        for mask, part in zip(masks, parts):
            result = jnp.where(mask[None], flat_slabs(part), result)
        return flat(result)

    return build


def flat_slabs(values):
    return values.reshape(-1, EY, LANES)


CHUNK = 16


def cuts(start, stop, chunk=CHUNK):
    count = -(-(stop - start) // chunk)
    edges = [start + (stop - start) * piece // count for piece in range(count + 1)]
    return list(zip(edges[:-1], edges[1:]))


def flat(values):
    return values.reshape(-1, LANES)


def beside(ref, rows):
    before = jnp.concatenate([ref[rows, HALF - 1 : EY - 1, :], ref[rows, 0:HALF, :]], axis=1)
    after = jnp.concatenate([ref[rows, HALF:EY, :], ref[rows, 1 : HALF + 1, :]], axis=1)
    return flat(before), flat(after)


def cycle_body(
    bounds_ref,
    mine_ref,
    other_ref,
    tables_ref,
    down_ref,
    up_ref,
    out_ref,
    start,
    ping,
    pong,
    left,
    left_x,
    left_y,
    left_z,
    mid_start,
    mid_ping,
    mid_pong,
    mid_left,
    mid_left_x,
    mid_left_y,
    mid_left_z,
    mask,
):
    lefts = (left_x, left_y, left_z)
    mid_lefts = (mid_left_x, mid_left_y, mid_left_z)
    fine_faces = Faces(FINE, False)
    mid_faces = Faces(MID, True)
    coarse_row = coarse_rows()
    fine_table, *fine_tables = [tables_ref[i] for i in range(4)]
    mid_table, *mid_tables = [tables_ref[i] for i in range(4, 8)]
    lift_table, coarse_table, *low_tables = [tables_ref[i] for i in range(8, 14)]

    slab = iota((WINDOW, EY, LANES), 0)
    mask[...] = jnp.where((slab >= bounds_ref[0]) & (slab < bounds_ref[1]), 1.0, 0.0)
    upper_is_mine = bounds_ref[2] == 1

    def at(x, a, b):
        return slice(x * WINDOW + a, x * WINDOW + b)

    def get(ref, rows):
        return flat(ref[rows, :, :])

    def put(ref, rows, values):
        ref[rows, :, :] = values.reshape(-1, EY, LANES)

    def fine_gather(ref, x, a, b):
        return (
            fine_faces.select(
                0,
                get(ref, at(x - 1, a, b)) if x > 0 else None,
                get(ref, at(x + 1, a, b)) if x < EX - 1 else None,
            ),
            fine_faces.select(1, *beside(ref, at(x, a, b))),
            fine_faces.select(2, get(ref, at(x, a - 1, b - 1)), get(ref, at(x, a + 1, b + 1))),
        )

    def fine_sweep(source, target, a, b, keep):
        for x in range(EX):
            for c, d in cuts(a, b):
                rows = at(x, c, d)
                faces = fine_gather(source, x, c, d)
                if keep is not None:
                    for ref, face in zip(lefts, faces):
                        if keep[0]:
                            put(ref, rows, keep[1] * face)
                        else:
                            put(ref, rows, get(ref, rows) + keep[1] * face)
                moved = 0.3 * get(source, rows) + get(start, rows) + times(faces, *fine_tables)
                put(target, rows, moved * get(mask, at(0, c, d)))

    for x in range(EX):
        for c, d in cuts(0, WINDOW):
            values = []
            for z in range(c, d):
                for y in range(2):
                    first = x * HALF * WINDOW + y * SPLIT + z % SPLIT
                    place = pl.ds(first, HALF, stride=WINDOW)
                    mine, other = mine_ref[place, :], other_ref[place, :]
                    if z < SPLIT:
                        mine, other = other, mine
                    values.append(jnp.where(upper_is_mine, mine, other))
            values = jnp.concatenate(values, axis=0)
            rows = at(x, c, d)
            put(left, rows, values)
            put(start, rows, 2.0 * times((values,), fine_table))

    fine_sweep(start, ping, 1, WINDOW - 1, (True, -0.21))
    fine_sweep(ping, pong, 2, WINDOW - 2, (False, -0.7))

    def mid_gather(faces, ref, a, b):
        here = get(ref, at(0, a, b))
        return (
            here,
            faces.select(1, *beside(ref, at(0, a, b))),
            faces.select(2, get(ref, at(0, a - 1, b - 1)), get(ref, at(0, a + 1, b + 1))),
        )

    for c, d in cuts(3, WINDOW - 3):
        values = []
        for x in range(EX):
            rest = 0.027 * get(left, at(x, c, d))
            for dimension, face in enumerate(fine_gather(pong, x, c, d)):
                face = 0.5 * (get(lefts[dimension], at(x, c, d)) + face)
                rest = rest + fine_faces.moved(dimension, face)
            values.append(rest)
        tables = [down_ref[x] for x in range(EX)]
        rows = at(0, c, d)
        total = times(values, *tables) * get(mask, rows)
        put(mid_left, rows, total)
        put(mid_start, rows, 2.0 * times((total,), mid_table))

    def mid_sweep(faces, tables, base, source, target, margin, keep=None):
        for c, d in cuts(margin, WINDOW - margin, CHUNK // 2):
            rows = at(0, c, d)
            values = mid_gather(faces, source, c, d)
            if keep is not None:
                for ref, face in zip(mid_lefts, values):
                    if keep[0]:
                        put(ref, rows, keep[1] * face)
                    else:
                        put(ref, rows, get(ref, rows) + keep[1] * face)
            moved = 0.3 * get(source, rows) + get(base, rows) + times(values, *tables)
            put(target, rows, moved * get(mask, rows))

    mid_sweep(mid_faces, mid_tables, mid_start, mid_start, mid_ping, 4, (True, -0.21))
    mid_sweep(mid_faces, mid_tables, mid_start, mid_ping, mid_pong, 5, (False, -0.7))

    base = ping.at[0:WINDOW]
    even = ping.at[WINDOW : 2 * WINDOW]
    odd = ping.at[2 * WINDOW : 3 * WINDOW]
    for c, d in cuts(6, WINDOW - 6):
        rows = at(0, c, d)
        faces = mid_gather(mid_faces, mid_pong, c, d)
        values = [get(mid_left, rows)]
        for ref, face in zip(mid_lefts, faces):
            values.append(get(ref, rows) + face)
        put(base, rows, times(values, *low_tables) * get(mask, rows))

    for c, d in cuts(10, WINDOW - 10, CHUNK // 2):
        rows = at(0, c, d)
        moved = times(mid_gather(mid_faces, mid_pong, c, d), *mid_tables)
        put(mid_left, rows, 0.3 * get(mid_pong, rows) + get(mid_start, rows) + moved)

    def coarse_gather(ref, a, b):
        rows = at(0, a, b)
        near = beside(ref, rows)
        return coarse_row(
            get(ref, rows), *near, get(ref, at(0, a - 1, b - 1)), get(ref, at(0, a + 1, b + 1))
        )

    def coarse_sweep(source, target, margin):
        for c, d in cuts(margin, WINDOW - margin, CHUNK // 2):
            rows = at(0, c, d)
            moved = times((coarse_gather(source, c, d),), coarse_table)
            moved = 0.3 * get(source, rows) + get(base, rows) + moved
            put(target, rows, moved * get(mask, rows))

    coarse_sweep(base, even, 7)
    coarse_sweep(even, odd, 8)
    coarse_sweep(odd, even, 9)

    for c, d in cuts(10, WINDOW - 10, CHUNK // 2):
        rows = at(0, c, d)
        moved = get(mid_left, rows) + times((coarse_gather(even, c, d),), lift_table)
        put(mid_ping, rows, moved * get(mask, rows))
    mid_sweep(mid_faces, mid_tables, mid_start, mid_ping, mid_pong, 11)
    mid_sweep(mid_faces, mid_tables, mid_start, mid_pong, mid_ping, 12)

    lifted = get(mid_ping, at(0, 12, WINDOW - 12))
    for x in range(EX):
        rows = at(x, 12, WINDOW - 12)
        put(pong, rows, get(pong, rows) + times((lifted,), up_ref[x]))
    fine_sweep(pong, ping, 13, WINDOW - 13, None)
    fine_sweep(ping, pong, 14, WINDOW - 14, None)
    fine_sweep(pong, ping, RADIUS, WINDOW - RADIUS, None)

    for x in range(EX):
        for z in range(OWN):
            for y in range(2):
                values = ping[x * WINDOW + RADIUS + z, y * HALF : (y + 1) * HALF, :]
                first = x * HALF * OWN * 2 + z * 2 + y
                out_ref[pl.ds(first, HALF, stride=2 * OWN), :] = values


def cycle(bounds, mine, other, tables, down, up):
    big = pltpu.VMEM((EX * WINDOW, EY, LANES), f32)
    small = pltpu.VMEM((WINDOW, EY, LANES), f32)
    vmem = pl.BlockSpec(memory_space=pltpu.VMEM)
    return pl.pallas_call(
        cycle_body,
        out_shape=jax.ShapeDtypeStruct((EX * HALF * 2 * OWN, LANES), f32),
        in_specs=[pl.BlockSpec(memory_space=pltpu.SMEM)] + [vmem] * 5,
        out_specs=vmem,
        scratch_shapes=[big] * 7 + [small] * 8,
        compiler_params=pltpu.CompilerParams(vmem_limit_bytes=20 * MIB),
        name="cycle",
    )(bounds, mine, other, tables, down, up)


def per_device(fine_source_field, scaling, block_fine, block_mid, block_coarse):
    count_z = scaling.shape[2]
    parts = lax.axis_size("gx") * lax.axis_size("gy")
    groups = lax.axis_size("gz")
    down, up, low, high = transfer_tables()
    group = lax.axis_index("gz")
    core = group % 2
    cores = core.astype(jnp.int32).reshape(1)

    own, edge = pack(cores, fine_source_field, scaling)
    ties = [(i, i + 1) for i in range(1, groups - 1, 2)]
    pairs = [(i, i ^ 1) for i in range(groups)]
    halo = lax.ppermute(edge, "gz", ties + [(j, i) for i, j in ties])
    sibling = lax.ppermute(own, "gz", pairs)
    chunks = window(cores, own, sibling, halo, parts)
    chunks, *matrices = lax.optimization_barrier((chunks, block_fine, block_mid, block_coarse))
    recv = lax.all_to_all(
        chunks.reshape(parts * WINDOW // 2, 2, LANES), ("gx", "gy"), 0, 0, tiled=True
    ).reshape(parts * WINDOW, LANES)
    recv, tables = lax.optimization_barrier((recv, inverses(*matrices, low, high)))
    other = lax.ppermute(recv, "gz", pairs)

    part = lax.axis_index("gx") * lax.axis_size("gy") + lax.axis_index("gy")
    first = (group - core) * count_z + OWN * part - RADIUS
    bounds = jnp.stack(
        [jnp.maximum(0, -first), jnp.minimum(WINDOW, groups * count_z - first), core]
    )
    result = cycle(
        bounds.astype(jnp.int32), recv, other, tables, down, up
    )
    back = lax.all_to_all(
        result.reshape(parts, 2 * OWN, LANES), ("gx", "gy"), 0, 0, tiled=True
    ).reshape(parts * 2 * OWN, LANES)
    return unpack(cores, back, scaling, fine_source_field.shape)


def solution(mesh):
    in_specs = (P("gx", "gy", "gz"), P("gx", "gy", "gz"), P(), P(), P())
    out_specs = P("gx", "gy", "gz")
    return jax.shard_map(
        per_device, mesh=mesh, in_specs=in_specs, out_specs=out_specs, check_vma=False
    )
```

```python
import math

import jax
import jax.numpy as jnp
import numpy as np
from jax import lax
from jax.experimental import pallas as pl
from jax.experimental.pallas import tpu as pltpu
from jax.sharding import PartitionSpec as P

FINE = 5
MID = 3
COARSE = 2
CSWEEPS = 4
RADIUS = 15
HALO = 16
OWN = 4
WINDOW = OWN + 2 * RADIUS
SPLIT = WINDOW // 2
EX = 4
EY = 16
HALF = EY // 2
LANES = 128

f32 = jnp.float32
bf16 = jnp.bfloat16
HIGHEST = lax.Precision.HIGHEST
MIB = 1 << 20


def gll_points(points):
    if points == 5:
        return np.array([-1.0, -math.sqrt(3.0 / 7.0), 0.0, math.sqrt(3.0 / 7.0), 1.0])
    if points == 3:
        return np.array([-1.0, 0.0, 1.0])
    return np.array([-1.0, 1.0])


def lagrange(fine_points, coarse_points):
    fine_nodes = gll_points(fine_points)
    coarse_nodes = gll_points(coarse_points)
    table = np.ones((fine_points, coarse_points))
    for column in range(coarse_points):
        for other in range(coarse_points):
            if other != column:
                table[:, column] *= (fine_nodes - coarse_nodes[other]) / (
                    coarse_nodes[column] - coarse_nodes[other]
                )
    return table


def halves(table):
    table = np.asarray(table, np.float32)
    hi = table.astype(jnp.bfloat16)
    lo = (table - hi.astype(np.float32)).astype(jnp.bfloat16)
    return np.concatenate([hi, lo], axis=1)


def transfer_tables():
    fine_mid = np.kron(np.kron(lagrange(5, 3), lagrange(5, 3)), lagrange(5, 3))
    mid_coarse = np.kron(np.kron(lagrange(3, 2), lagrange(3, 2)), lagrange(3, 2))
    down, up = [], []
    for place in range(EX):
        table = np.zeros((LANES, LANES))
        table[:125, place * 32 : place * 32 + 27] = fine_mid
        down.append(halves(table))
        up.append(halves(table.T))
    middle = np.zeros((LANES, LANES), np.float32)
    for place in range(EX):
        middle[place * 32 : place * 32 + 27, place * 8 : place * 8 + 8] = mid_coarse
    low = [0.027 * middle]
    low += [0.5 * np.dot(move, middle) for move in exchanges(MID, True)]
    high = [np.roll(middle.T, 32 * copy, axis=0) for copy in range(3)]
    return np.stack(down), np.stack(up), np.stack(low), np.stack(high)


def iota(shape, dimension):
    return lax.broadcasted_iota(jnp.int32, shape, dimension)


def three_way(values):
    one = values.astype(bf16)
    rest = values - one.astype(f32)
    two = rest.astype(bf16)
    three = (rest - two.astype(f32)).astype(bf16)
    return jnp.concatenate([one, two, three], axis=0)


def place_of(lane, y):
    i, j, k = lane // (FINE * FINE), (lane // FINE) % FINE, lane % FINE
    return jnp.where(lane < FINE**3, k * LANES + i * 2 * FINE + y * FINE + j, -1)


def pack_body(core_ref, field_ref, scale_ref, own_ref, edge_ref, lines, turned, *, count_z):
    lines[...] = jnp.zeros_like(lines)
    for i in range(FINE):
        lines[i * 2 * FINE : (i + 1) * 2 * FINE, 0 : count_z * FINE] = field_ref[i]
    for part in range(lines.shape[1] // LANES):
        lanes = slice(part * LANES, (part + 1) * LANES)
        turned[lanes, :] = lines[:, lanes].T
    lane = iota((1, 2 * LANES), 1)
    place = place_of(lane % LANES, lane // LANES)
    table = jnp.where(iota((FINE * LANES, 2 * LANES), 0) == place, 1.0, 0.0).astype(bf16)
    values = [turned[pl.ds(k, count_z, stride=FINE), :] for k in range(FINE)]
    nodes = jnp.dot(
        three_way(jnp.concatenate(values, axis=1)), table, preferred_element_type=f32
    )
    nodes = nodes[0:count_z] + nodes[count_z : 2 * count_z] + nodes[2 * count_z : 3 * count_z]
    scale = scale_ref[0].T
    for y in range(2):
        own_ref[y] = nodes[:, y * LANES : (y + 1) * LANES] / scale[:, y : y + 1]
    start = pl.multiple_of(core_ref[0] * (count_z - HALO), HALO)
    for y in range(2):
        edge_ref[y] = own_ref[y, pl.ds(start, HALO), :]


def pack(core, field, scaling):
    count_z = scaling.shape[2]
    width = -(-count_z * FINE // LANES) * LANES

    def body(*refs):
        pack_body(*refs, count_z=count_z)

    vmem = pl.BlockSpec(memory_space=pltpu.VMEM)
    return pl.pallas_call(
        body,
        out_shape=(
            jax.ShapeDtypeStruct((2, count_z, LANES), f32),
            jax.ShapeDtypeStruct((2, HALO, LANES), f32),
        ),
        in_specs=[pl.BlockSpec(memory_space=pltpu.SMEM), vmem, vmem],
        out_specs=(vmem, vmem),
        scratch_shapes=[pltpu.VMEM((LANES, width), f32), pltpu.VMEM((width, LANES), f32)],
        compiler_params=pltpu.CompilerParams(vmem_limit_bytes=8 * MIB),
        name="pack",
    )(core, field, scaling)


def settle(halo):
    def body(in_ref, out_ref):
        out_ref[...] = in_ref[...]

    return pl.pallas_call(
        body,
        out_shape=jax.ShapeDtypeStruct(halo.shape, f32),
        cost_estimate=pl.CostEstimate(
            flops=2_000_000_000, bytes_accessed=20_000_000, transcendentals=0
        ),
        compiler_params=pltpu.CompilerParams(vmem_limit_bytes=8 * MIB),
        name="settle",
    )(halo)


def window_body(core_ref, own_ref, sibling_ref, halo_ref, out_ref, line, *, parts):
    count_z = own_ref.shape[1]
    for core in range(2):
        places = (HALO, HALO + count_z, 0) if core == 0 else (count_z, 0, 2 * count_z)

        @pl.when(core_ref[0] == core)
        def _(core=core, places=places):
            for ref, place in zip((own_ref, sibling_ref, halo_ref), places):
                line[:, place : place + ref.shape[1], :] = ref[...]
            first = HALO - RADIUS if core == 0 else SPLIT - RADIUS
            for part in range(parts):
                for y in range(2):
                    start = first + OWN * part
                    row = part * WINDOW + y * SPLIT
                    out_ref[row : row + SPLIT, :] = line[y, start : start + SPLIT, :]


def window(core, own, sibling, halo, parts):
    def body(*refs):
        window_body(*refs, parts=parts)

    vmem = pl.BlockSpec(memory_space=pltpu.VMEM)
    return pl.pallas_call(
        body,
        out_shape=jax.ShapeDtypeStruct((parts * WINDOW, LANES), f32),
        in_specs=[pl.BlockSpec(memory_space=pltpu.SMEM), vmem, vmem, vmem],
        out_specs=vmem,
        scratch_shapes=[pltpu.VMEM((2, 2 * own.shape[1] + HALO, LANES), f32)],
        compiler_params=pltpu.CompilerParams(vmem_limit_bytes=8 * MIB),
        name="window",
    )(core, own, sibling, halo)


def unpack_body(core_ref, back_ref, scale_ref, out_ref, turned, *, count_z):
    scale = scale_ref[0].T
    base = core_ref[0] * (2 * count_z)
    rows = [
        back_ref[pl.ds(base + y, count_z, stride=2), :] / scale[:, y : y + 1] for y in range(2)
    ]
    table = jnp.concatenate(
        [
            jnp.where(
                iota((LANES, FINE * LANES), 1) == place_of(iota((LANES, 1), 0), y), 1.0, 0.0
            )
            for y in range(2)
        ],
        axis=0,
    ).astype(bf16)
    spread = jnp.dot(
        three_way(jnp.concatenate(rows, axis=1)), table, preferred_element_type=f32
    )
    spread = spread[0:count_z] + spread[count_z : 2 * count_z] + spread[2 * count_z : 3 * count_z]
    for k in range(FINE):
        turned[pl.ds(k, count_z, stride=FINE), :] = spread[:, k * LANES : (k + 1) * LANES]
    lines = [
        turned[part * LANES : (part + 1) * LANES, :].T for part in range(turned.shape[0] // LANES)
    ]
    lines = jnp.concatenate(lines, axis=1)
    for i in range(FINE):
        out_ref[i] = lines[i * 2 * FINE : (i + 1) * 2 * FINE, 0 : count_z * FINE]


def unpack(core, back, scaling, shape):
    count_z = scaling.shape[2]
    width = -(-count_z * FINE // LANES) * LANES

    def body(*refs):
        unpack_body(*refs, count_z=count_z)

    vmem = pl.BlockSpec(memory_space=pltpu.VMEM)
    return pl.pallas_call(
        body,
        out_shape=jax.ShapeDtypeStruct(shape, f32),
        in_specs=[pl.BlockSpec(memory_space=pltpu.SMEM), vmem, vmem],
        out_specs=vmem,
        scratch_shapes=[pltpu.VMEM((width, LANES), f32)],
        compiler_params=pltpu.CompilerParams(vmem_limit_bytes=8 * MIB),
        name="unpack",
    )(core, back, scaling)


def shifted_block(ref, pad, points):
    nodes = points**3
    pad[...] = jnp.zeros((LANES, LANES), f32)
    pad[0:nodes, 0:nodes] = ref[...]
    lane, row = iota((LANES, LANES), 1), iota((LANES, LANES), 0)
    count = jnp.zeros((LANES, LANES), f32)
    for stride in (points * points, points, 1):
        index = (lane // stride) % points
        count = count + jnp.where((index == 0) | (index == points - 1), 0.5, 0.0)
    diagonal = jnp.where(lane < nodes, count, 1.0)
    return pad[...] + jnp.where(lane == row, diagonal, 0.0)


def invert(matrix, panels):
    lane, row = iota((LANES, LANES), 1), iota((LANES, LANES), 0)
    lane1, lane16, row16 = iota((1, LANES), 1), iota((16, LANES), 1), iota((16, LANES), 0)
    for panel in range(panels):
        top = panel * 16
        rows = matrix[top : top + 16, :]
        for step in range(0, 16, 2):
            pivot = top + step
            left = jnp.broadcast_to(rows[:, pivot : pivot + 1], (16, LANES))
            right = jnp.broadcast_to(rows[:, pivot + 1 : pivot + 2], (16, LANES))
            a, b = left[step : step + 1], right[step : step + 1]
            c, d = left[step + 1 : step + 2], right[step + 1 : step + 2]
            scale = 1.0 / (a * d - b * c)
            here = (lane1 == pivot) | (lane1 == pivot + 1)
            one = jnp.where(here, jnp.where(lane1 == pivot, 1.0, 0.0), rows[step : step + 1])
            two = jnp.where(here, jnp.where(lane1 == pivot, 0.0, 1.0), rows[step + 1 : step + 2])
            one, two = (d * one - b * two) * scale, (a * two - c * one) * scale
            others = jnp.where((lane16 == pivot) | (lane16 == pivot + 1), 0.0, rows)
            others = others - left * one - right * two
            rows = jnp.where(row16 == step, one, jnp.where(row16 == step + 1, two, others))
        stacked = jnp.concatenate([rows] * 8, axis=0)
        inside = (lane >= top) & (lane < top + 16)
        update = jnp.dot(
            jnp.where(inside, matrix, 0.0), stacked, precision=HIGHEST, preferred_element_type=f32
        )
        matrix = jnp.where(
            (row >= top) & (row < top + 16), stacked, jnp.where(inside, 0.0, matrix) - update
        )
    return matrix


def exact(left, right):
    return jnp.dot(left, right, precision=HIGHEST, preferred_element_type=f32)


def repeated(matrix, width):
    lane, row = iota((LANES, LANES), 1), iota((LANES, LANES), 0)
    used = (lane < EX * width) & (row < EX * width)
    pick = jnp.where((row % width == lane) & (lane < width), 1.0, 0.0)
    put = jnp.where((lane % width == row) & (row < width), 1.0, 0.0)
    wide = exact(exact(pick, matrix), put)
    return jnp.where(used & (row // width == lane // width), wide, 0.0)


def moves(points, width):
    lane, row = iota((1, LANES), 1), iota((LANES, LANES), 0)
    local, place = lane % width, lane // width
    tables = []
    for dimension, stride in enumerate((points * points, points, 1)):
        index = (local // stride) % points
        first = (index == 0) & (local < points**3)
        last = (index == points - 1) & (local < points**3)
        reach = (points - 1) * stride
        if dimension == 0 and width < LANES:
            first, last = first & (place > 0), last & (place < EX - 1)
            reach = reach - width
        source = jnp.where(first, lane + reach, jnp.where(last, lane - reach, -LANES))
        tables.append((row, source))
    return tables


def inverses_body(fine_ref, mid_ref, coarse_ref, low_ref, high_ref, out_ref, pad):
    lane, row = iota((LANES, LANES), 1), iota((LANES, LANES), 0)
    coarse = invert(shifted_block(coarse_ref, pad, COARSE), 1)
    mid = invert(shifted_block(mid_ref, pad, MID), 2)
    fine = invert(shifted_block(fine_ref, pad, FINE), 8)
    levels = ((fine, FINE, LANES), (repeated(mid, 32), MID, 32))
    for level, (inverse, points, width) in enumerate(levels):
        inverse = 0.35 * inverse
        out_ref[4 * level] = two_way(inverse)
        moved = []
        for dimension, (own, source) in enumerate(moves(points, width)):
            moved.append(exact(jnp.where(own == source, 1.0, 0.0), inverse))
            out_ref[4 * level + 1 + dimension] = two_way(moved[dimension])
    lifted = 0.3 * high_ref[0]
    for dimension in range(3):
        lifted = lifted + exact(high_ref[dimension], moved[dimension])
    out_ref[8] = two_way(lifted)
    copies = jnp.where((lane % 32 == row) & (lane < 96), 1.0, 0.0)
    inverse = exact(0.35 * repeated(coarse, 8), copies)
    gather = jnp.zeros((LANES, LANES), f32)
    for dimension, (own, source) in enumerate(moves(COARSE, 8)):
        gather = gather + jnp.where((own == source + 32 * dimension) & (lane < 32), 1.0, 0.0)
    out_ref[9] = two_way(exact(gather, inverse))
    for part in range(4):
        out_ref[10 + part] = two_way(exact(low_ref[part], 2.0 * inverse))


def inverses(block_fine, block_mid, block_coarse, low, high):
    return pl.pallas_call(
        inverses_body,
        out_shape=jax.ShapeDtypeStruct((14, LANES, 2 * LANES), bf16),
        scratch_shapes=[pltpu.VMEM((LANES, LANES), f32)],
        compiler_params=pltpu.CompilerParams(vmem_limit_bytes=8 * MIB),
        cost_estimate=pl.CostEstimate(
            flops=2_000_000_000, bytes_accessed=20_000_000, transcendentals=0
        ),
        name="inverses",
    )(block_fine, block_mid, block_coarse, low, high)


def two_way(values):
    hi = values.astype(bf16)
    lo = (values - hi.astype(f32)).astype(bf16)
    return jnp.concatenate([hi, lo], axis=1)


def times(values, *tables):
    values = jnp.concatenate([two_way(value) for value in values], axis=1)
    stack = []
    for table in tables:
        high = table[:, 0:LANES]
        stack += [table, jnp.concatenate([high, jnp.zeros_like(high)], axis=1)]
    result = jnp.dot(values, jnp.concatenate(stack, axis=0), preferred_element_type=f32)
    return result[:, 0:LANES] + result[:, LANES : 2 * LANES]


def exchanges(points, in_lanes):
    nodes = points**3
    tables = []
    for dimension, stride in enumerate((points * points, points, 1)):
        table = np.zeros((LANES, LANES), np.float32)
        for place in range(EX if in_lanes else 1):
            for node in range(nodes):
                index = (node // stride) % points
                for end, step in ((0, -1), (points - 1, 1)):
                    if index != end:
                        continue
                    source = place * 32 + node - step * (points - 1) * stride
                    if dimension == 0 and in_lanes:
                        if not 0 <= place + step < EX:
                            continue
                        source += step * 32
                    table[source, place * 32 + node] = 1.0
        tables.append(table)
    return tables


class Faces:
    def __init__(self, points, in_lanes):
        lane, row = iota((EY, LANES), 1), iota((EY, LANES), 0)
        local = lane % 32 if in_lanes else lane
        self.masks = []
        for dimension, stride in enumerate((points * points, points, 1)):
            index = (local // stride) % points
            first, last = index == 0, index == points - 1
            if dimension == 1:
                self.masks.append((last & (row > 0), first & (row < EY - 1)))
            else:
                self.masks.append((last, first))

    def moved(self, dimension, faces):
        reach = (FINE - 1) * FINE ** (2 - dimension)
        lane = iota((1, LANES), 1)
        index = (lane // FINE ** (2 - dimension)) % FINE
        node = lane < FINE**3
        order = jnp.where((index == 0) & node, lane + reach, LANES - 1)
        order = jnp.where((index == FINE - 1) & node, lane - reach, order)
        turned = jnp.take_along_axis(
            faces, jnp.broadcast_to(order, faces.shape), axis=1, mode="promise_in_bounds"
        )
        return jnp.where(order < LANES - 1, turned, 0.0)

    def select(self, dimension, before, after):
        from_before, from_after = self.masks[dimension]
        if before is None:
            before, after = 0.0, flat_slabs(after)
        elif after is None:
            before, after = flat_slabs(before), 0.0
        else:
            before, after = flat_slabs(before), flat_slabs(after)
        if dimension == 1:
            after = jnp.where(from_after[None], after, 0.0)
        return flat(jnp.where(from_before[None], before, after))


def coarse_rows():
    lane, row = iota((EY, LANES), 1), iota((EY, LANES), 0)
    copy, j, k = lane // 32, (lane // 2) % 2, lane % 2
    masks = (
        copy == 0,
        (copy == 1) & (j == 1) & (row > 0),
        (copy == 1) & (j == 0) & (row < EY - 1),
        (copy == 2) & (k == 1),
        (copy == 2) & (k == 0),
    )

    def build(*parts):
        result = 0.0
        for mask, part in zip(masks, parts):
            result = jnp.where(mask[None], flat_slabs(part), result)
        return flat(result)

    return build


def flat_slabs(values):
    return values.reshape(-1, EY, LANES)


CHUNK = 16


def cuts(start, stop, chunk=CHUNK):
    count = -(-(stop - start) // chunk)
    edges = [start + (stop - start) * piece // count for piece in range(count + 1)]
    return list(zip(edges[:-1], edges[1:]))


def flat(values):
    return values.reshape(-1, LANES)


def beside(ref, rows):
    before = jnp.concatenate([ref[rows, HALF - 1 : EY - 1, :], ref[rows, 0:HALF, :]], axis=1)
    after = jnp.concatenate([ref[rows, HALF:EY, :], ref[rows, 1 : HALF + 1, :]], axis=1)
    return flat(before), flat(after)


def cycle_body(
    bounds_ref,
    mine_ref,
    other_ref,
    tables_ref,
    down_ref,
    up_ref,
    out_ref,
    start,
    ping,
    pong,
    left,
    left_x,
    left_y,
    left_z,
    mid_start,
    mid_ping,
    mid_pong,
    mid_left,
    mid_left_x,
    mid_left_y,
    mid_left_z,
    mask,
):
    lefts = (left_x, left_y, left_z)
    mid_lefts = (mid_left_x, mid_left_y, mid_left_z)
    fine_faces = Faces(FINE, False)
    mid_faces = Faces(MID, True)
    coarse_row = coarse_rows()
    fine_table, *fine_tables = [tables_ref[i] for i in range(4)]
    mid_table, *mid_tables = [tables_ref[i] for i in range(4, 8)]
    lift_table, coarse_table, *low_tables = [tables_ref[i] for i in range(8, 14)]

    slab = iota((WINDOW, EY, LANES), 0)
    mask[...] = jnp.where((slab >= bounds_ref[0]) & (slab < bounds_ref[1]), 1.0, 0.0)
    upper_is_mine = bounds_ref[2] == 1

    def at(x, a, b):
        return slice(x * WINDOW + a, x * WINDOW + b)

    def get(ref, rows):
        return flat(ref[rows, :, :])

    def put(ref, rows, values):
        ref[rows, :, :] = values.reshape(-1, EY, LANES)

    def fine_gather(ref, x, a, b):
        return (
            fine_faces.select(
                0,
                get(ref, at(x - 1, a, b)) if x > 0 else None,
                get(ref, at(x + 1, a, b)) if x < EX - 1 else None,
            ),
            fine_faces.select(1, *beside(ref, at(x, a, b))),
            fine_faces.select(2, get(ref, at(x, a - 1, b - 1)), get(ref, at(x, a + 1, b + 1))),
        )

    def fine_sweep(source, target, a, b, keep):
        for x in range(EX):
            for c, d in cuts(a, b):
                rows = at(x, c, d)
                faces = fine_gather(source, x, c, d)
                if keep is not None:
                    for ref, face in zip(lefts, faces):
                        if keep[0]:
                            put(ref, rows, keep[1] * face)
                        else:
                            put(ref, rows, get(ref, rows) + keep[1] * face)
                moved = 0.3 * get(source, rows) + get(start, rows) + times(faces, *fine_tables)
                put(target, rows, moved * get(mask, at(0, c, d)))

    for x in range(EX):
        for c, d in cuts(0, WINDOW):
            values = []
            for z in range(c, d):
                for y in range(2):
                    first = x * HALF * WINDOW + y * SPLIT + z % SPLIT
                    place = pl.ds(first, HALF, stride=WINDOW)
                    mine, other = mine_ref[place, :], other_ref[place, :]
                    if z < SPLIT:
                        mine, other = other, mine
                    values.append(jnp.where(upper_is_mine, mine, other))
            values = jnp.concatenate(values, axis=0)
            rows = at(x, c, d)
            put(left, rows, values)
            put(start, rows, 2.0 * times((values,), fine_table))

    fine_sweep(start, ping, 1, WINDOW - 1, (True, -0.21))
    fine_sweep(ping, pong, 2, WINDOW - 2, (False, -0.7))

    def mid_gather(faces, ref, a, b):
        here = get(ref, at(0, a, b))
        return (
            here,
            faces.select(1, *beside(ref, at(0, a, b))),
            faces.select(2, get(ref, at(0, a - 1, b - 1)), get(ref, at(0, a + 1, b + 1))),
        )

    for c, d in cuts(3, WINDOW - 3):
        values = []
        for x in range(EX):
            rest = 0.027 * get(left, at(x, c, d))
            for dimension, face in enumerate(fine_gather(pong, x, c, d)):
                face = 0.5 * (get(lefts[dimension], at(x, c, d)) + face)
                rest = rest + fine_faces.moved(dimension, face)
            values.append(rest)
        tables = [down_ref[x] for x in range(EX)]
        rows = at(0, c, d)
        total = times(values, *tables) * get(mask, rows)
        put(mid_left, rows, total)
        put(mid_start, rows, 2.0 * times((total,), mid_table))

    def mid_sweep(faces, tables, base, source, target, margin, keep=None):
        for c, d in cuts(margin, WINDOW - margin, CHUNK // 2):
            rows = at(0, c, d)
            values = mid_gather(faces, source, c, d)
            if keep is not None:
                for ref, face in zip(mid_lefts, values):
                    if keep[0]:
                        put(ref, rows, keep[1] * face)
                    else:
                        put(ref, rows, get(ref, rows) + keep[1] * face)
            moved = 0.3 * get(source, rows) + get(base, rows) + times(values, *tables)
            put(target, rows, moved * get(mask, rows))

    mid_sweep(mid_faces, mid_tables, mid_start, mid_start, mid_ping, 4, (True, -0.21))
    mid_sweep(mid_faces, mid_tables, mid_start, mid_ping, mid_pong, 5, (False, -0.7))

    base = ping.at[0:WINDOW]
    even = ping.at[WINDOW : 2 * WINDOW]
    odd = ping.at[2 * WINDOW : 3 * WINDOW]
    for c, d in cuts(6, WINDOW - 6):
        rows = at(0, c, d)
        faces = mid_gather(mid_faces, mid_pong, c, d)
        values = [get(mid_left, rows)]
        for ref, face in zip(mid_lefts, faces):
            values.append(get(ref, rows) + face)
        put(base, rows, times(values, *low_tables) * get(mask, rows))

    for c, d in cuts(10, WINDOW - 10, CHUNK // 2):
        rows = at(0, c, d)
        moved = times(mid_gather(mid_faces, mid_pong, c, d), *mid_tables)
        put(mid_left, rows, 0.3 * get(mid_pong, rows) + get(mid_start, rows) + moved)

    def coarse_gather(ref, a, b):
        rows = at(0, a, b)
        near = beside(ref, rows)
        return coarse_row(
            get(ref, rows), *near, get(ref, at(0, a - 1, b - 1)), get(ref, at(0, a + 1, b + 1))
        )

    def coarse_sweep(source, target, margin):
        for c, d in cuts(margin, WINDOW - margin, CHUNK // 2):
            rows = at(0, c, d)
            moved = times((coarse_gather(source, c, d),), coarse_table)
            moved = 0.3 * get(source, rows) + get(base, rows) + moved
            put(target, rows, moved * get(mask, rows))

    coarse_sweep(base, even, 7)
    coarse_sweep(even, odd, 8)
    coarse_sweep(odd, even, 9)

    for c, d in cuts(10, WINDOW - 10, CHUNK // 2):
        rows = at(0, c, d)
        moved = get(mid_left, rows) + times((coarse_gather(even, c, d),), lift_table)
        put(mid_ping, rows, moved * get(mask, rows))
    mid_sweep(mid_faces, mid_tables, mid_start, mid_ping, mid_pong, 11)
    mid_sweep(mid_faces, mid_tables, mid_start, mid_pong, mid_ping, 12)

    lifted = get(mid_ping, at(0, 12, WINDOW - 12))
    for x in range(EX):
        rows = at(x, 12, WINDOW - 12)
        put(pong, rows, get(pong, rows) + times((lifted,), up_ref[x]))
    fine_sweep(pong, ping, 13, WINDOW - 13, None)
    fine_sweep(ping, pong, 14, WINDOW - 14, None)
    fine_sweep(pong, ping, RADIUS, WINDOW - RADIUS, None)

    for x in range(EX):
        for z in range(OWN):
            for y in range(2):
                values = ping[x * WINDOW + RADIUS + z, y * HALF : (y + 1) * HALF, :]
                first = x * HALF * OWN * 2 + z * 2 + y
                out_ref[pl.ds(first, HALF, stride=2 * OWN), :] = values


def cycle(bounds, mine, other, tables, down, up):
    big = pltpu.VMEM((EX * WINDOW, EY, LANES), f32)
    small = pltpu.VMEM((WINDOW, EY, LANES), f32)
    vmem = pl.BlockSpec(memory_space=pltpu.VMEM)
    return pl.pallas_call(
        cycle_body,
        out_shape=jax.ShapeDtypeStruct((EX * HALF * 2 * OWN, LANES), f32),
        in_specs=[pl.BlockSpec(memory_space=pltpu.SMEM)] + [vmem] * 5,
        out_specs=vmem,
        scratch_shapes=[big] * 7 + [small] * 8,
        compiler_params=pltpu.CompilerParams(vmem_limit_bytes=20 * MIB),
        name="cycle",
    )(bounds, mine, other, tables, down, up)


def per_device(fine_source_field, scaling, block_fine, block_mid, block_coarse):
    count_z = scaling.shape[2]
    parts = lax.axis_size("gx") * lax.axis_size("gy")
    groups = lax.axis_size("gz")
    down, up, low, high = transfer_tables()
    group = lax.axis_index("gz")
    core = group % 2
    cores = core.astype(jnp.int32).reshape(1)

    own, edge = pack(cores, fine_source_field, scaling)
    ties = [(i, i + 1) for i in range(1, groups - 1, 2)]
    pairs = [(i, i ^ 1) for i in range(groups)]
    halo = settle(lax.ppermute(edge, "gz", ties + [(j, i) for i, j in ties]))
    sibling = lax.ppermute(own, "gz", pairs)
    chunks = window(cores, own, sibling, halo, parts)
    chunks, *matrices = lax.optimization_barrier((chunks, block_fine, block_mid, block_coarse))
    recv = lax.all_to_all(
        chunks.reshape(parts * WINDOW // 2, 2, LANES), ("gx", "gy"), 0, 0, tiled=True
    ).reshape(parts * WINDOW, LANES)
    recv, tables = lax.optimization_barrier((recv, inverses(*matrices, low, high)))
    other = lax.ppermute(recv, "gz", pairs)

    part = lax.axis_index("gx") * lax.axis_size("gy") + lax.axis_index("gy")
    first = (group - core) * count_z + OWN * part - RADIUS
    bounds = jnp.stack(
        [jnp.maximum(0, -first), jnp.minimum(WINDOW, groups * count_z - first), core]
    )
    result = cycle(
        bounds.astype(jnp.int32), recv, other, tables, down, up
    )
    back = lax.all_to_all(
        result.reshape(parts, 2 * OWN, LANES), ("gx", "gy"), 0, 0, tiled=True
    ).reshape(parts * 2 * OWN, LANES)
    return unpack(cores, back, scaling, fine_source_field.shape)


def solution(mesh):
    in_specs = (P("gx", "gy", "gz"), P("gx", "gy", "gz"), P(), P(), P())
    out_specs = P("gx", "gy", "gz")
    return jax.shard_map(
        per_device, mesh=mesh, in_specs=in_specs, out_specs=out_specs, check_vma=False
    )
```

```python
import math

import jax
import jax.numpy as jnp
import numpy as np
from jax import lax
from jax.experimental import pallas as pl
from jax.experimental.pallas import tpu as pltpu
from jax.sharding import PartitionSpec as P

FINE = 5
MID = 3
COARSE = 2
CSWEEPS = 4
RADIUS = 15
HALO = 16
OWN = 4
WINDOW = OWN + 2 * RADIUS
SPLIT = WINDOW // 2
EX = 4
EY = 16
HALF = EY // 2
LANES = 128

f32 = jnp.float32
bf16 = jnp.bfloat16
HIGHEST = lax.Precision.HIGHEST
MIB = 1 << 20


def gll_points(points):
    if points == 5:
        return np.array([-1.0, -math.sqrt(3.0 / 7.0), 0.0, math.sqrt(3.0 / 7.0), 1.0])
    if points == 3:
        return np.array([-1.0, 0.0, 1.0])
    return np.array([-1.0, 1.0])


def lagrange(fine_points, coarse_points):
    fine_nodes = gll_points(fine_points)
    coarse_nodes = gll_points(coarse_points)
    table = np.ones((fine_points, coarse_points))
    for column in range(coarse_points):
        for other in range(coarse_points):
            if other != column:
                table[:, column] *= (fine_nodes - coarse_nodes[other]) / (
                    coarse_nodes[column] - coarse_nodes[other]
                )
    return table


def halves(table):
    table = np.asarray(table, np.float32)
    hi = table.astype(jnp.bfloat16)
    lo = (table - hi.astype(np.float32)).astype(jnp.bfloat16)
    return np.concatenate([hi, lo], axis=1)


def transfer_tables():
    fine_mid = np.kron(np.kron(lagrange(5, 3), lagrange(5, 3)), lagrange(5, 3))
    mid_coarse = np.kron(np.kron(lagrange(3, 2), lagrange(3, 2)), lagrange(3, 2))
    down, up = [], []
    for place in range(EX):
        table = np.zeros((LANES, LANES))
        table[:125, place * 32 : place * 32 + 27] = fine_mid
        down.append(halves(table))
        up.append(halves(table.T))
    middle = np.zeros((LANES, LANES), np.float32)
    for place in range(EX):
        middle[place * 32 : place * 32 + 27, place * 8 : place * 8 + 8] = mid_coarse
    low = [0.027 * middle]
    low += [0.5 * np.dot(move, middle) for move in exchanges(MID, True)]
    high = [np.roll(middle.T, 32 * copy, axis=0) for copy in range(3)]
    return np.stack(down), np.stack(up), np.stack(low), np.stack(high)


def iota(shape, dimension):
    return lax.broadcasted_iota(jnp.int32, shape, dimension)


def three_way(values):
    one = values.astype(bf16)
    rest = values - one.astype(f32)
    two = rest.astype(bf16)
    three = (rest - two.astype(f32)).astype(bf16)
    return jnp.concatenate([one, two, three], axis=0)


def place_of(lane, y):
    i, j, k = lane // (FINE * FINE), (lane // FINE) % FINE, lane % FINE
    return jnp.where(lane < FINE**3, k * LANES + i * 2 * FINE + y * FINE + j, -1)


def pack_body(core_ref, field_ref, scale_ref, own_ref, edge_ref, lines, turned, *, count_z):
    lines[...] = jnp.zeros_like(lines)
    for i in range(FINE):
        lines[i * 2 * FINE : (i + 1) * 2 * FINE, 0 : count_z * FINE] = field_ref[i]
    for part in range(lines.shape[1] // LANES):
        lanes = slice(part * LANES, (part + 1) * LANES)
        turned[lanes, :] = lines[:, lanes].T
    lane = iota((1, 2 * LANES), 1)
    place = place_of(lane % LANES, lane // LANES)
    table = jnp.where(iota((FINE * LANES, 2 * LANES), 0) == place, 1.0, 0.0).astype(bf16)
    values = [turned[pl.ds(k, count_z, stride=FINE), :] for k in range(FINE)]
    nodes = jnp.dot(
        three_way(jnp.concatenate(values, axis=1)), table, preferred_element_type=f32
    )
    nodes = nodes[0:count_z] + nodes[count_z : 2 * count_z] + nodes[2 * count_z : 3 * count_z]
    scale = scale_ref[0].T
    for y in range(2):
        own_ref[y] = nodes[:, y * LANES : (y + 1) * LANES] / scale[:, y : y + 1]
    start = pl.multiple_of(core_ref[0] * (count_z - HALO), HALO)
    for y in range(2):
        edge_ref[y] = own_ref[y, pl.ds(start, HALO), :]


def pack(core, field, scaling):
    count_z = scaling.shape[2]
    width = -(-count_z * FINE // LANES) * LANES

    def body(*refs):
        pack_body(*refs, count_z=count_z)

    vmem = pl.BlockSpec(memory_space=pltpu.VMEM)
    return pl.pallas_call(
        body,
        out_shape=(
            jax.ShapeDtypeStruct((2, count_z, LANES), f32),
            jax.ShapeDtypeStruct((2, HALO, LANES), f32),
        ),
        in_specs=[pl.BlockSpec(memory_space=pltpu.SMEM), vmem, vmem],
        out_specs=(vmem, vmem),
        scratch_shapes=[pltpu.VMEM((LANES, width), f32), pltpu.VMEM((width, LANES), f32)],
        compiler_params=pltpu.CompilerParams(vmem_limit_bytes=8 * MIB),
        name="pack",
    )(core, field, scaling)


def settle(halo):
    def body(in_ref, out_ref):
        out_ref[...] = in_ref[...]

    return pl.pallas_call(
        body,
        out_shape=jax.ShapeDtypeStruct(halo.shape, f32),
        cost_estimate=pl.CostEstimate(
            flops=2_000_000_000, bytes_accessed=20_000_000, transcendentals=0
        ),
        compiler_params=pltpu.CompilerParams(vmem_limit_bytes=8 * MIB),
        name="settle",
    )(halo)


def window_body(core_ref, own_ref, sibling_ref, halo_ref, out_ref, line, *, parts):
    count_z = own_ref.shape[1]
    for core in range(2):
        places = (HALO, HALO + count_z, 0) if core == 0 else (count_z, 0, 2 * count_z)

        @pl.when(core_ref[0] == core)
        def _(core=core, places=places):
            for ref, place in zip((own_ref, sibling_ref, halo_ref), places):
                line[:, place : place + ref.shape[1], :] = ref[...]
            first = HALO - RADIUS if core == 0 else SPLIT - RADIUS
            for part in range(parts):
                for y in range(2):
                    start = first + OWN * part
                    row = part * WINDOW + y * SPLIT
                    out_ref[row : row + SPLIT, :] = line[y, start : start + SPLIT, :]


def window(core, own, sibling, halo, parts):
    def body(*refs):
        window_body(*refs, parts=parts)

    vmem = pl.BlockSpec(memory_space=pltpu.VMEM)
    return pl.pallas_call(
        body,
        out_shape=jax.ShapeDtypeStruct((parts * WINDOW, LANES), f32),
        in_specs=[pl.BlockSpec(memory_space=pltpu.SMEM), vmem, vmem, vmem],
        out_specs=vmem,
        scratch_shapes=[pltpu.VMEM((2, 2 * own.shape[1] + HALO, LANES), f32)],
        compiler_params=pltpu.CompilerParams(vmem_limit_bytes=8 * MIB),
        name="window",
    )(core, own, sibling, halo)


def unpack_body(core_ref, back_ref, scale_ref, out_ref, turned, *, count_z):
    scale = scale_ref[0].T
    base = core_ref[0] * (2 * count_z)
    rows = [
        back_ref[pl.ds(base + y, count_z, stride=2), :] / scale[:, y : y + 1] for y in range(2)
    ]
    table = jnp.concatenate(
        [
            jnp.where(
                iota((LANES, FINE * LANES), 1) == place_of(iota((LANES, 1), 0), y), 1.0, 0.0
            )
            for y in range(2)
        ],
        axis=0,
    ).astype(bf16)
    spread = jnp.dot(
        three_way(jnp.concatenate(rows, axis=1)), table, preferred_element_type=f32
    )
    spread = spread[0:count_z] + spread[count_z : 2 * count_z] + spread[2 * count_z : 3 * count_z]
    for k in range(FINE):
        turned[pl.ds(k, count_z, stride=FINE), :] = spread[:, k * LANES : (k + 1) * LANES]
    lines = [
        turned[part * LANES : (part + 1) * LANES, :].T for part in range(turned.shape[0] // LANES)
    ]
    lines = jnp.concatenate(lines, axis=1)
    for i in range(FINE):
        out_ref[i] = lines[i * 2 * FINE : (i + 1) * 2 * FINE, 0 : count_z * FINE]


def unpack(core, back, scaling, shape):
    count_z = scaling.shape[2]
    width = -(-count_z * FINE // LANES) * LANES

    def body(*refs):
        unpack_body(*refs, count_z=count_z)

    vmem = pl.BlockSpec(memory_space=pltpu.VMEM)
    return pl.pallas_call(
        body,
        out_shape=jax.ShapeDtypeStruct(shape, f32),
        in_specs=[pl.BlockSpec(memory_space=pltpu.SMEM), vmem, vmem],
        out_specs=vmem,
        scratch_shapes=[pltpu.VMEM((width, LANES), f32)],
        compiler_params=pltpu.CompilerParams(vmem_limit_bytes=8 * MIB),
        name="unpack",
    )(core, back, scaling)


def shifted_block(ref, pad, points):
    nodes = points**3
    pad[...] = jnp.zeros((LANES, LANES), f32)
    pad[0:nodes, 0:nodes] = ref[...]
    lane, row = iota((LANES, LANES), 1), iota((LANES, LANES), 0)
    count = jnp.zeros((LANES, LANES), f32)
    for stride in (points * points, points, 1):
        index = (lane // stride) % points
        count = count + jnp.where((index == 0) | (index == points - 1), 0.5, 0.0)
    diagonal = jnp.where(lane < nodes, count, 1.0)
    return pad[...] + jnp.where(lane == row, diagonal, 0.0)


def invert(matrix, panels):
    lane, row = iota((LANES, LANES), 1), iota((LANES, LANES), 0)
    lane1, lane16, row16 = iota((1, LANES), 1), iota((16, LANES), 1), iota((16, LANES), 0)
    for panel in range(panels):
        top = panel * 16
        rows = matrix[top : top + 16, :]
        for step in range(0, 16, 2):
            pivot = top + step
            left = jnp.broadcast_to(rows[:, pivot : pivot + 1], (16, LANES))
            right = jnp.broadcast_to(rows[:, pivot + 1 : pivot + 2], (16, LANES))
            a, b = left[step : step + 1], right[step : step + 1]
            c, d = left[step + 1 : step + 2], right[step + 1 : step + 2]
            scale = 1.0 / (a * d - b * c)
            here = (lane1 == pivot) | (lane1 == pivot + 1)
            one = jnp.where(here, jnp.where(lane1 == pivot, 1.0, 0.0), rows[step : step + 1])
            two = jnp.where(here, jnp.where(lane1 == pivot, 0.0, 1.0), rows[step + 1 : step + 2])
            one, two = (d * one - b * two) * scale, (a * two - c * one) * scale
            others = jnp.where((lane16 == pivot) | (lane16 == pivot + 1), 0.0, rows)
            others = others - left * one - right * two
            rows = jnp.where(row16 == step, one, jnp.where(row16 == step + 1, two, others))
        stacked = jnp.concatenate([rows] * 8, axis=0)
        inside = (lane >= top) & (lane < top + 16)
        update = jnp.dot(
            jnp.where(inside, matrix, 0.0), stacked, precision=HIGHEST, preferred_element_type=f32
        )
        matrix = jnp.where(
            (row >= top) & (row < top + 16), stacked, jnp.where(inside, 0.0, matrix) - update
        )
    return matrix


def exact(left, right):
    return jnp.dot(left, right, precision=HIGHEST, preferred_element_type=f32)


def repeated(matrix, width):
    lane, row = iota((LANES, LANES), 1), iota((LANES, LANES), 0)
    used = (lane < EX * width) & (row < EX * width)
    pick = jnp.where((row % width == lane) & (lane < width), 1.0, 0.0)
    put = jnp.where((lane % width == row) & (row < width), 1.0, 0.0)
    wide = exact(exact(pick, matrix), put)
    return jnp.where(used & (row // width == lane // width), wide, 0.0)


def moves(points, width):
    lane, row = iota((1, LANES), 1), iota((LANES, LANES), 0)
    local, place = lane % width, lane // width
    tables = []
    for dimension, stride in enumerate((points * points, points, 1)):
        index = (local // stride) % points
        first = (index == 0) & (local < points**3)
        last = (index == points - 1) & (local < points**3)
        reach = (points - 1) * stride
        if dimension == 0 and width < LANES:
            first, last = first & (place > 0), last & (place < EX - 1)
            reach = reach - width
        source = jnp.where(first, lane + reach, jnp.where(last, lane - reach, -LANES))
        tables.append((row, source))
    return tables


def inverses_body(fine_ref, mid_ref, coarse_ref, low_ref, high_ref, out_ref, pad):
    lane, row = iota((LANES, LANES), 1), iota((LANES, LANES), 0)
    coarse = invert(shifted_block(coarse_ref, pad, COARSE), 1)
    mid = invert(shifted_block(mid_ref, pad, MID), 2)
    fine = invert(shifted_block(fine_ref, pad, FINE), 8)
    levels = ((fine, FINE, LANES), (repeated(mid, 32), MID, 32))
    for level, (inverse, points, width) in enumerate(levels):
        inverse = 0.35 * inverse
        out_ref[4 * level] = two_way(inverse)
        moved = []
        for dimension, (own, source) in enumerate(moves(points, width)):
            moved.append(exact(jnp.where(own == source, 1.0, 0.0), inverse))
            out_ref[4 * level + 1 + dimension] = two_way(moved[dimension])
    lifted = 0.3 * high_ref[0]
    for dimension in range(3):
        lifted = lifted + exact(high_ref[dimension], moved[dimension])
    out_ref[8] = two_way(lifted)
    copies = jnp.where((lane % 32 == row) & (lane < 96), 1.0, 0.0)
    inverse = exact(0.35 * repeated(coarse, 8), copies)
    gather = jnp.zeros((LANES, LANES), f32)
    for dimension, (own, source) in enumerate(moves(COARSE, 8)):
        gather = gather + jnp.where((own == source + 32 * dimension) & (lane < 32), 1.0, 0.0)
    out_ref[9] = two_way(exact(gather, inverse))
    for part in range(4):
        out_ref[10 + part] = two_way(exact(low_ref[part], 2.0 * inverse))


def inverses(block_fine, block_mid, block_coarse, low, high):
    return pl.pallas_call(
        inverses_body,
        out_shape=jax.ShapeDtypeStruct((14, LANES, 2 * LANES), bf16),
        scratch_shapes=[pltpu.VMEM((LANES, LANES), f32)],
        compiler_params=pltpu.CompilerParams(vmem_limit_bytes=8 * MIB),
        cost_estimate=pl.CostEstimate(
            flops=2_000_000_000, bytes_accessed=20_000_000, transcendentals=0
        ),
        name="inverses",
    )(block_fine, block_mid, block_coarse, low, high)


def two_way(values):
    hi = values.astype(bf16)
    lo = (values - hi.astype(f32)).astype(bf16)
    return jnp.concatenate([hi, lo], axis=1)


def times(values, *tables):
    values = jnp.concatenate([two_way(value) for value in values], axis=1)
    stack = []
    for table in tables:
        high = table[:, 0:LANES]
        stack += [table, jnp.concatenate([high, jnp.zeros_like(high)], axis=1)]
    result = jnp.dot(values, jnp.concatenate(stack, axis=0), preferred_element_type=f32)
    return result[:, 0:LANES] + result[:, LANES : 2 * LANES]


def exchanges(points, in_lanes):
    nodes = points**3
    tables = []
    for dimension, stride in enumerate((points * points, points, 1)):
        table = np.zeros((LANES, LANES), np.float32)
        for place in range(EX if in_lanes else 1):
            for node in range(nodes):
                index = (node // stride) % points
                for end, step in ((0, -1), (points - 1, 1)):
                    if index != end:
                        continue
                    source = place * 32 + node - step * (points - 1) * stride
                    if dimension == 0 and in_lanes:
                        if not 0 <= place + step < EX:
                            continue
                        source += step * 32
                    table[source, place * 32 + node] = 1.0
        tables.append(table)
    return tables


class Faces:
    def __init__(self, points, in_lanes):
        lane, row = iota((EY, LANES), 1), iota((EY, LANES), 0)
        local = lane % 32 if in_lanes else lane
        self.masks = []
        for dimension, stride in enumerate((points * points, points, 1)):
            index = (local // stride) % points
            first, last = index == 0, index == points - 1
            if dimension == 1:
                self.masks.append((last & (row > 0), first & (row < EY - 1)))
            else:
                self.masks.append((last, first))

    def moved(self, dimension, faces):
        reach = (FINE - 1) * FINE ** (2 - dimension)
        lane = iota((1, LANES), 1)
        index = (lane // FINE ** (2 - dimension)) % FINE
        node = lane < FINE**3
        order = jnp.where((index == 0) & node, lane + reach, LANES - 1)
        order = jnp.where((index == FINE - 1) & node, lane - reach, order)
        turned = jnp.take_along_axis(
            faces, jnp.broadcast_to(order, faces.shape), axis=1, mode="promise_in_bounds"
        )
        return jnp.where(order < LANES - 1, turned, 0.0)

    def select(self, dimension, before, after):
        from_before, from_after = self.masks[dimension]
        if before is None:
            before, after = 0.0, flat_slabs(after)
        elif after is None:
            before, after = flat_slabs(before), 0.0
        else:
            before, after = flat_slabs(before), flat_slabs(after)
        if dimension == 1:
            after = jnp.where(from_after[None], after, 0.0)
        return flat(jnp.where(from_before[None], before, after))


def coarse_rows():
    lane, row = iota((EY, LANES), 1), iota((EY, LANES), 0)
    copy, j, k = lane // 32, (lane // 2) % 2, lane % 2
    masks = (
        copy == 0,
        (copy == 1) & (j == 1) & (row > 0),
        (copy == 1) & (j == 0) & (row < EY - 1),
        (copy == 2) & (k == 1),
        (copy == 2) & (k == 0),
    )

    def build(*parts):
        result = 0.0
        for mask, part in zip(masks, parts):
            result = jnp.where(mask[None], flat_slabs(part), result)
        return flat(result)

    return build


def flat_slabs(values):
    return values.reshape(-1, EY, LANES)


CHUNK = 16


def cuts(start, stop, chunk=CHUNK):
    count = -(-(stop - start) // chunk)
    edges = [start + (stop - start) * piece // count for piece in range(count + 1)]
    return list(zip(edges[:-1], edges[1:]))


def flat(values):
    return values.reshape(-1, LANES)


def beside(ref, rows):
    before = jnp.concatenate([ref[rows, HALF - 1 : EY - 1, :], ref[rows, 0:HALF, :]], axis=1)
    after = jnp.concatenate([ref[rows, HALF:EY, :], ref[rows, 1 : HALF + 1, :]], axis=1)
    return flat(before), flat(after)


def cycle_body(
    bounds_ref,
    mine_ref,
    other_ref,
    tables_ref,
    down_ref,
    up_ref,
    out_ref,
    start,
    ping,
    pong,
    left,
    left_x,
    left_y,
    left_z,
    mid_start,
    mid_ping,
    mid_pong,
    mid_left,
    mid_left_x,
    mid_left_y,
    mid_left_z,
    mask,
):
    lefts = (left_x, left_y, left_z)
    mid_lefts = (mid_left_x, mid_left_y, mid_left_z)
    fine_faces = Faces(FINE, False)
    mid_faces = Faces(MID, True)
    coarse_row = coarse_rows()
    fine_table, *fine_tables = [tables_ref[i] for i in range(4)]
    mid_table, *mid_tables = [tables_ref[i] for i in range(4, 8)]
    lift_table, coarse_table, *low_tables = [tables_ref[i] for i in range(8, 14)]

    slab = iota((WINDOW, EY, LANES), 0)
    mask[...] = jnp.where((slab >= bounds_ref[0]) & (slab < bounds_ref[1]), 1.0, 0.0)
    upper_is_mine = bounds_ref[2] == 1

    def at(x, a, b):
        return slice(x * WINDOW + a, x * WINDOW + b)

    def get(ref, rows):
        return flat(ref[rows, :, :])

    def put(ref, rows, values):
        ref[rows, :, :] = values.reshape(-1, EY, LANES)

    def fine_gather(ref, x, a, b):
        return (
            fine_faces.select(
                0,
                get(ref, at(x - 1, a, b)) if x > 0 else None,
                get(ref, at(x + 1, a, b)) if x < EX - 1 else None,
            ),
            fine_faces.select(1, *beside(ref, at(x, a, b))),
            fine_faces.select(2, get(ref, at(x, a - 1, b - 1)), get(ref, at(x, a + 1, b + 1))),
        )

    def fine_sweep(source, target, a, b, keep):
        for x in range(EX):
            for c, d in cuts(a, b):
                rows = at(x, c, d)
                faces = fine_gather(source, x, c, d)
                if keep is not None:
                    for ref, face in zip(lefts, faces):
                        if keep[0]:
                            put(ref, rows, keep[1] * face)
                        else:
                            put(ref, rows, get(ref, rows) + keep[1] * face)
                moved = 0.3 * get(source, rows) + get(start, rows) + times(faces, *fine_tables)
                put(target, rows, moved * get(mask, at(0, c, d)))

    for x in range(EX):
        for c, d in cuts(0, WINDOW):
            values = []
            for z in range(c, d):
                for y in range(2):
                    first = x * HALF * WINDOW + y * SPLIT + z % SPLIT
                    place = pl.ds(first, HALF, stride=WINDOW)
                    mine, other = mine_ref[place, :], other_ref[place, :]
                    if z < SPLIT:
                        mine, other = other, mine
                    values.append(jnp.where(upper_is_mine, mine, other))
            values = jnp.concatenate(values, axis=0)
            rows = at(x, c, d)
            put(left, rows, values)
            put(start, rows, 2.0 * times((values,), fine_table))

    fine_sweep(start, ping, 1, WINDOW - 1, (True, -0.21))
    fine_sweep(ping, pong, 2, WINDOW - 2, (False, -0.7))

    def mid_gather(faces, ref, a, b):
        here = get(ref, at(0, a, b))
        return (
            here,
            faces.select(1, *beside(ref, at(0, a, b))),
            faces.select(2, get(ref, at(0, a - 1, b - 1)), get(ref, at(0, a + 1, b + 1))),
        )

    for c, d in cuts(3, WINDOW - 3):
        values = []
        for x in range(EX):
            rest = 0.027 * get(left, at(x, c, d))
            for dimension, face in enumerate(fine_gather(pong, x, c, d)):
                face = 0.5 * (get(lefts[dimension], at(x, c, d)) + face)
                rest = rest + fine_faces.moved(dimension, face)
            values.append(rest)
        tables = [down_ref[x] for x in range(EX)]
        rows = at(0, c, d)
        total = times(values, *tables) * get(mask, rows)
        put(mid_left, rows, total)
        put(mid_start, rows, 2.0 * times((total,), mid_table))

    def mid_sweep(faces, tables, base, source, target, margin, keep=None):
        for c, d in cuts(margin, WINDOW - margin, CHUNK // 2):
            rows = at(0, c, d)
            values = mid_gather(faces, source, c, d)
            if keep is not None:
                for ref, face in zip(mid_lefts, values):
                    if keep[0]:
                        put(ref, rows, keep[1] * face)
                    else:
                        put(ref, rows, get(ref, rows) + keep[1] * face)
            moved = 0.3 * get(source, rows) + get(base, rows) + times(values, *tables)
            put(target, rows, moved * get(mask, rows))

    mid_sweep(mid_faces, mid_tables, mid_start, mid_start, mid_ping, 4, (True, -0.21))
    mid_sweep(mid_faces, mid_tables, mid_start, mid_ping, mid_pong, 5, (False, -0.7))

    base = ping.at[0:WINDOW]
    even = ping.at[WINDOW : 2 * WINDOW]
    odd = ping.at[2 * WINDOW : 3 * WINDOW]
    for c, d in cuts(6, WINDOW - 6):
        rows = at(0, c, d)
        faces = mid_gather(mid_faces, mid_pong, c, d)
        values = [get(mid_left, rows)]
        for ref, face in zip(mid_lefts, faces):
            values.append(get(ref, rows) + face)
        put(base, rows, times(values, *low_tables) * get(mask, rows))

    for c, d in cuts(10, WINDOW - 10, CHUNK // 2):
        rows = at(0, c, d)
        moved = times(mid_gather(mid_faces, mid_pong, c, d), *mid_tables)
        put(mid_left, rows, 0.3 * get(mid_pong, rows) + get(mid_start, rows) + moved)

    def coarse_gather(ref, a, b):
        rows = at(0, a, b)
        near = beside(ref, rows)
        return coarse_row(
            get(ref, rows), *near, get(ref, at(0, a - 1, b - 1)), get(ref, at(0, a + 1, b + 1))
        )

    def coarse_sweep(source, target, margin):
        for c, d in cuts(margin, WINDOW - margin, CHUNK // 2):
            rows = at(0, c, d)
            moved = times((coarse_gather(source, c, d),), coarse_table)
            moved = 0.3 * get(source, rows) + get(base, rows) + moved
            put(target, rows, moved * get(mask, rows))

    coarse_sweep(base, even, 7)
    coarse_sweep(even, odd, 8)
    coarse_sweep(odd, even, 9)

    for c, d in cuts(10, WINDOW - 10, CHUNK // 2):
        rows = at(0, c, d)
        moved = get(mid_left, rows) + times((coarse_gather(even, c, d),), lift_table)
        put(mid_ping, rows, moved * get(mask, rows))
    mid_sweep(mid_faces, mid_tables, mid_start, mid_ping, mid_pong, 11)
    mid_sweep(mid_faces, mid_tables, mid_start, mid_pong, mid_ping, 12)

    lifted = get(mid_ping, at(0, 12, WINDOW - 12))
    for x in range(EX):
        rows = at(x, 12, WINDOW - 12)
        put(pong, rows, get(pong, rows) + times((lifted,), up_ref[x]))
    fine_sweep(pong, ping, 13, WINDOW - 13, None)
    fine_sweep(ping, pong, 14, WINDOW - 14, None)
    fine_sweep(pong, ping, RADIUS, WINDOW - RADIUS, None)

    for x in range(EX):
        for z in range(OWN):
            for y in range(2):
                values = ping[x * WINDOW + RADIUS + z, y * HALF : (y + 1) * HALF, :]
                first = x * HALF * OWN * 2 + z * 2 + y
                out_ref[pl.ds(first, HALF, stride=2 * OWN), :] = values


def cycle(bounds, mine, other, tables, down, up):
    big = pltpu.VMEM((EX * WINDOW, EY, LANES), f32)
    small = pltpu.VMEM((WINDOW, EY, LANES), f32)
    vmem = pl.BlockSpec(memory_space=pltpu.VMEM)
    return pl.pallas_call(
        cycle_body,
        out_shape=jax.ShapeDtypeStruct((EX * HALF * 2 * OWN, LANES), f32),
        in_specs=[pl.BlockSpec(memory_space=pltpu.SMEM)] + [vmem] * 5,
        out_specs=vmem,
        scratch_shapes=[big] * 7 + [small] * 8,
        compiler_params=pltpu.CompilerParams(vmem_limit_bytes=20 * MIB),
        name="cycle",
    )(bounds, mine, other, tables, down, up)


def per_device(fine_source_field, scaling, block_fine, block_mid, block_coarse):
    count_z = scaling.shape[2]
    parts = lax.axis_size("gx") * lax.axis_size("gy")
    groups = lax.axis_size("gz")
    down, up, low, high = transfer_tables()
    group = lax.axis_index("gz")
    core = group % 2
    cores = core.astype(jnp.int32).reshape(1)

    own, edge = pack(cores, fine_source_field, scaling)
    ties = [(i, i + 1) for i in range(1, groups - 1, 2)]
    pairs = [(i, i ^ 1) for i in range(groups)]
    halo = settle(lax.ppermute(edge, "gz", ties + [(j, i) for i, j in ties]))
    sibling = lax.ppermute(own, "gz", pairs)
    chunks = window(cores, own, sibling, halo, parts)
    chunks, *matrices = lax.optimization_barrier((chunks, block_fine, block_mid, block_coarse))
    recv = lax.all_to_all(
        chunks.reshape(parts * WINDOW // 2, 2, LANES), ("gx", "gy"), 0, 0, tiled=True
    ).reshape(parts * WINDOW, LANES)
    recv, tables = lax.optimization_barrier((recv, inverses(*matrices, low, high)))
    wide = lax.axis_size("gx")
    ways = [
        (x * groups + i, x * groups + (i ^ 1))
        for x in range(wide)
        for i in range(groups)
        if i % 2 == (1 if 2 * x < wide else 0)
    ]
    other = lax.ppermute(recv, ("gx", "gz"), ways)

    part = lax.axis_index("gx") * lax.axis_size("gy") + lax.axis_index("gy")
    first = (group - core) * count_z + OWN * part - RADIUS
    bounds = jnp.stack(
        [jnp.maximum(0, -first), jnp.minimum(WINDOW, groups * count_z - first), core]
    )
    result = cycle(
        bounds.astype(jnp.int32), recv, other, tables, down, up
    )
    back = lax.all_to_all(
        result.reshape(parts, 2 * OWN, LANES), ("gx", "gy"), 0, 0, tiled=True
    ).reshape(parts * 2 * OWN, LANES)
    return unpack(cores, back, scaling, fine_source_field.shape)


def solution(mesh):
    in_specs = (P("gx", "gy", "gz"), P("gx", "gy", "gz"), P(), P(), P())
    out_specs = P("gx", "gy", "gz")
    return jax.shard_map(
        per_device, mesh=mesh, in_specs=in_specs, out_specs=out_specs, check_vma=False
    )
```

```python
import math

import jax
import jax.numpy as jnp
import numpy as np
from jax import lax
from jax.experimental import pallas as pl
from jax.experimental.pallas import tpu as pltpu
from jax.sharding import PartitionSpec as P

FINE = 5
MID = 3
COARSE = 2
CSWEEPS = 4
RADIUS = 15
HALO = 16
OWN = 4
WINDOW = OWN + 2 * RADIUS
SPLIT = WINDOW // 2
EX = 4
EY = 16
HALF = EY // 2
LANES = 128

f32 = jnp.float32
bf16 = jnp.bfloat16
HIGHEST = lax.Precision.HIGHEST
MIB = 1 << 20


def gll_points(points):
    if points == 5:
        return np.array([-1.0, -math.sqrt(3.0 / 7.0), 0.0, math.sqrt(3.0 / 7.0), 1.0])
    if points == 3:
        return np.array([-1.0, 0.0, 1.0])
    return np.array([-1.0, 1.0])


def lagrange(fine_points, coarse_points):
    fine_nodes = gll_points(fine_points)
    coarse_nodes = gll_points(coarse_points)
    table = np.ones((fine_points, coarse_points))
    for column in range(coarse_points):
        for other in range(coarse_points):
            if other != column:
                table[:, column] *= (fine_nodes - coarse_nodes[other]) / (
                    coarse_nodes[column] - coarse_nodes[other]
                )
    return table


def halves(table):
    table = np.asarray(table, np.float32)
    hi = table.astype(jnp.bfloat16)
    lo = (table - hi.astype(np.float32)).astype(jnp.bfloat16)
    return np.concatenate([hi, lo], axis=1)


def transfer_tables():
    fine_mid = np.kron(np.kron(lagrange(5, 3), lagrange(5, 3)), lagrange(5, 3))
    mid_coarse = np.kron(np.kron(lagrange(3, 2), lagrange(3, 2)), lagrange(3, 2))
    down, up = [], []
    for place in range(EX):
        table = np.zeros((LANES, LANES))
        table[:125, place * 32 : place * 32 + 27] = fine_mid
        down.append(halves(table))
        up.append(halves(table.T))
    middle = np.zeros((LANES, LANES), np.float32)
    for place in range(EX):
        middle[place * 32 : place * 32 + 27, place * 8 : place * 8 + 8] = mid_coarse
    low = [0.027 * middle]
    low += [0.5 * np.dot(move, middle) for move in exchanges(MID, True)]
    high = [np.roll(middle.T, 32 * copy, axis=0) for copy in range(3)]
    return np.stack(down), np.stack(up), np.stack(low), np.stack(high)


def iota(shape, dimension):
    return lax.broadcasted_iota(jnp.int32, shape, dimension)


def three_way(values):
    one = values.astype(bf16)
    rest = values - one.astype(f32)
    two = rest.astype(bf16)
    three = (rest - two.astype(f32)).astype(bf16)
    return jnp.concatenate([one, two, three], axis=0)


def place_of(lane, y):
    i, j, k = lane // (FINE * FINE), (lane // FINE) % FINE, lane % FINE
    return jnp.where(lane < FINE**3, k * LANES + i * 2 * FINE + y * FINE + j, -1)


def pack_body(core_ref, field_ref, scale_ref, own_ref, edge_ref, lines, turned, *, count_z):
    lines[...] = jnp.zeros_like(lines)
    for i in range(FINE):
        lines[i * 2 * FINE : (i + 1) * 2 * FINE, 0 : count_z * FINE] = field_ref[i]
    for part in range(lines.shape[1] // LANES):
        lanes = slice(part * LANES, (part + 1) * LANES)
        turned[lanes, :] = lines[:, lanes].T
    lane = iota((1, 2 * LANES), 1)
    place = place_of(lane % LANES, lane // LANES)
    table = jnp.where(iota((FINE * LANES, 2 * LANES), 0) == place, 1.0, 0.0).astype(bf16)
    values = [turned[pl.ds(k, count_z, stride=FINE), :] for k in range(FINE)]
    nodes = jnp.dot(
        three_way(jnp.concatenate(values, axis=1)), table, preferred_element_type=f32
    )
    nodes = nodes[0:count_z] + nodes[count_z : 2 * count_z] + nodes[2 * count_z : 3 * count_z]
    scale = scale_ref[0].T
    for y in range(2):
        own_ref[y] = nodes[:, y * LANES : (y + 1) * LANES] / scale[:, y : y + 1]
    start = pl.multiple_of(core_ref[0] * (count_z - HALO), HALO)
    for y in range(2):
        edge_ref[y] = own_ref[y, pl.ds(start, HALO), :]


def pack(core, field, scaling):
    count_z = scaling.shape[2]
    width = -(-count_z * FINE // LANES) * LANES

    def body(*refs):
        pack_body(*refs, count_z=count_z)

    vmem = pl.BlockSpec(memory_space=pltpu.VMEM)
    return pl.pallas_call(
        body,
        out_shape=(
            jax.ShapeDtypeStruct((2, count_z, LANES), f32),
            jax.ShapeDtypeStruct((2, HALO, LANES), f32),
        ),
        in_specs=[pl.BlockSpec(memory_space=pltpu.SMEM), vmem, vmem],
        out_specs=(vmem, vmem),
        scratch_shapes=[pltpu.VMEM((LANES, width), f32), pltpu.VMEM((width, LANES), f32)],
        compiler_params=pltpu.CompilerParams(vmem_limit_bytes=8 * MIB),
        name="pack",
    )(core, field, scaling)


def settle(halo):
    def body(in_ref, out_ref):
        out_ref[...] = in_ref[...]

    return pl.pallas_call(
        body,
        out_shape=jax.ShapeDtypeStruct(halo.shape, f32),
        cost_estimate=pl.CostEstimate(
            flops=2_000_000_000, bytes_accessed=20_000_000, transcendentals=0
        ),
        compiler_params=pltpu.CompilerParams(vmem_limit_bytes=8 * MIB),
        name="settle",
    )(halo)


def window_body(core_ref, own_ref, sibling_ref, halo_ref, out_ref, line, *, parts):
    count_z = own_ref.shape[1]
    for core in range(2):
        places = (HALO, HALO + count_z, 0) if core == 0 else (count_z, 0, 2 * count_z)

        @pl.when(core_ref[0] == core)
        def _(core=core, places=places):
            for ref, place in zip((own_ref, sibling_ref, halo_ref), places):
                line[:, place : place + ref.shape[1], :] = ref[...]
            first = HALO - RADIUS if core == 0 else SPLIT - RADIUS
            for part in range(parts):
                for y in range(2):
                    start = first + OWN * part
                    row = part * WINDOW + y * SPLIT
                    out_ref[row : row + SPLIT, :] = line[y, start : start + SPLIT, :]


def window(core, own, sibling, halo, parts):
    def body(*refs):
        window_body(*refs, parts=parts)

    vmem = pl.BlockSpec(memory_space=pltpu.VMEM)
    return pl.pallas_call(
        body,
        out_shape=jax.ShapeDtypeStruct((parts * WINDOW, LANES), f32),
        in_specs=[pl.BlockSpec(memory_space=pltpu.SMEM), vmem, vmem, vmem],
        out_specs=vmem,
        scratch_shapes=[pltpu.VMEM((2, 2 * own.shape[1] + HALO, LANES), f32)],
        compiler_params=pltpu.CompilerParams(vmem_limit_bytes=8 * MIB),
        name="window",
    )(core, own, sibling, halo)


def unpack_body(core_ref, back_ref, scale_ref, out_ref, turned, *, count_z):
    scale = scale_ref[0].T
    base = core_ref[0] * (2 * count_z)
    rows = [
        back_ref[pl.ds(base + y, count_z, stride=2), :] / scale[:, y : y + 1] for y in range(2)
    ]
    table = jnp.concatenate(
        [
            jnp.where(
                iota((LANES, FINE * LANES), 1) == place_of(iota((LANES, 1), 0), y), 1.0, 0.0
            )
            for y in range(2)
        ],
        axis=0,
    ).astype(bf16)
    spread = jnp.dot(
        three_way(jnp.concatenate(rows, axis=1)), table, preferred_element_type=f32
    )
    spread = spread[0:count_z] + spread[count_z : 2 * count_z] + spread[2 * count_z : 3 * count_z]
    for k in range(FINE):
        turned[pl.ds(k, count_z, stride=FINE), :] = spread[:, k * LANES : (k + 1) * LANES]
    lines = [
        turned[part * LANES : (part + 1) * LANES, :].T for part in range(turned.shape[0] // LANES)
    ]
    lines = jnp.concatenate(lines, axis=1)
    for i in range(FINE):
        out_ref[i] = lines[i * 2 * FINE : (i + 1) * 2 * FINE, 0 : count_z * FINE]


def unpack(core, back, scaling, shape):
    count_z = scaling.shape[2]
    width = -(-count_z * FINE // LANES) * LANES

    def body(*refs):
        unpack_body(*refs, count_z=count_z)

    vmem = pl.BlockSpec(memory_space=pltpu.VMEM)
    return pl.pallas_call(
        body,
        out_shape=jax.ShapeDtypeStruct(shape, f32),
        in_specs=[pl.BlockSpec(memory_space=pltpu.SMEM), vmem, vmem],
        out_specs=vmem,
        scratch_shapes=[pltpu.VMEM((width, LANES), f32)],
        compiler_params=pltpu.CompilerParams(vmem_limit_bytes=8 * MIB),
        name="unpack",
    )(core, back, scaling)


def shifted_block(ref, pad, points):
    nodes = points**3
    pad[...] = jnp.zeros((LANES, LANES), f32)
    pad[0:nodes, 0:nodes] = ref[...]
    lane, row = iota((LANES, LANES), 1), iota((LANES, LANES), 0)
    count = jnp.zeros((LANES, LANES), f32)
    for stride in (points * points, points, 1):
        index = (lane // stride) % points
        count = count + jnp.where((index == 0) | (index == points - 1), 0.5, 0.0)
    diagonal = jnp.where(lane < nodes, count, 1.0)
    return pad[...] + jnp.where(lane == row, diagonal, 0.0)


def invert(matrix, panels):
    lane, row = iota((LANES, LANES), 1), iota((LANES, LANES), 0)
    lane1, lane16, row16 = iota((1, LANES), 1), iota((16, LANES), 1), iota((16, LANES), 0)
    for panel in range(panels):
        top = panel * 16
        rows = matrix[top : top + 16, :]
        for step in range(0, 16, 2):
            pivot = top + step
            left = jnp.broadcast_to(rows[:, pivot : pivot + 1], (16, LANES))
            right = jnp.broadcast_to(rows[:, pivot + 1 : pivot + 2], (16, LANES))
            a, b = left[step : step + 1], right[step : step + 1]
            c, d = left[step + 1 : step + 2], right[step + 1 : step + 2]
            scale = 1.0 / (a * d - b * c)
            here = (lane1 == pivot) | (lane1 == pivot + 1)
            one = jnp.where(here, jnp.where(lane1 == pivot, 1.0, 0.0), rows[step : step + 1])
            two = jnp.where(here, jnp.where(lane1 == pivot, 0.0, 1.0), rows[step + 1 : step + 2])
            one, two = (d * one - b * two) * scale, (a * two - c * one) * scale
            others = jnp.where((lane16 == pivot) | (lane16 == pivot + 1), 0.0, rows)
            others = others - left * one - right * two
            rows = jnp.where(row16 == step, one, jnp.where(row16 == step + 1, two, others))
        stacked = jnp.concatenate([rows] * 8, axis=0)
        inside = (lane >= top) & (lane < top + 16)
        update = jnp.dot(
            jnp.where(inside, matrix, 0.0), stacked, precision=HIGHEST, preferred_element_type=f32
        )
        matrix = jnp.where(
            (row >= top) & (row < top + 16), stacked, jnp.where(inside, 0.0, matrix) - update
        )
    return matrix


def exact(left, right):
    return jnp.dot(left, right, precision=HIGHEST, preferred_element_type=f32)


def repeated(matrix, width):
    lane, row = iota((LANES, LANES), 1), iota((LANES, LANES), 0)
    used = (lane < EX * width) & (row < EX * width)
    pick = jnp.where((row % width == lane) & (lane < width), 1.0, 0.0)
    put = jnp.where((lane % width == row) & (row < width), 1.0, 0.0)
    wide = exact(exact(pick, matrix), put)
    return jnp.where(used & (row // width == lane // width), wide, 0.0)


def moves(points, width):
    lane, row = iota((1, LANES), 1), iota((LANES, LANES), 0)
    local, place = lane % width, lane // width
    tables = []
    for dimension, stride in enumerate((points * points, points, 1)):
        index = (local // stride) % points
        first = (index == 0) & (local < points**3)
        last = (index == points - 1) & (local < points**3)
        reach = (points - 1) * stride
        if dimension == 0 and width < LANES:
            first, last = first & (place > 0), last & (place < EX - 1)
            reach = reach - width
        source = jnp.where(first, lane + reach, jnp.where(last, lane - reach, -LANES))
        tables.append((row, source))
    return tables


def inverses_body(fine_ref, mid_ref, coarse_ref, low_ref, high_ref, out_ref, pad):
    lane, row = iota((LANES, LANES), 1), iota((LANES, LANES), 0)
    coarse = invert(shifted_block(coarse_ref, pad, COARSE), 1)
    mid = invert(shifted_block(mid_ref, pad, MID), 2)
    fine = invert(shifted_block(fine_ref, pad, FINE), 8)
    levels = ((fine, FINE, LANES), (repeated(mid, 32), MID, 32))
    for level, (inverse, points, width) in enumerate(levels):
        inverse = 0.35 * inverse
        out_ref[4 * level] = two_way(inverse)
        moved = []
        for dimension, (own, source) in enumerate(moves(points, width)):
            moved.append(exact(jnp.where(own == source, 1.0, 0.0), inverse))
            out_ref[4 * level + 1 + dimension] = two_way(moved[dimension])
    lifted = 0.3 * high_ref[0]
    for dimension in range(3):
        lifted = lifted + exact(high_ref[dimension], moved[dimension])
    out_ref[8] = two_way(lifted)
    copies = jnp.where((lane % 32 == row) & (lane < 96), 1.0, 0.0)
    inverse = exact(0.35 * repeated(coarse, 8), copies)
    gather = jnp.zeros((LANES, LANES), f32)
    for dimension, (own, source) in enumerate(moves(COARSE, 8)):
        gather = gather + jnp.where((own == source + 32 * dimension) & (lane < 32), 1.0, 0.0)
    out_ref[9] = two_way(exact(gather, inverse))
    for part in range(4):
        out_ref[10 + part] = two_way(exact(low_ref[part], 2.0 * inverse))


def inverses(block_fine, block_mid, block_coarse, low, high):
    return pl.pallas_call(
        inverses_body,
        out_shape=jax.ShapeDtypeStruct((14, LANES, 2 * LANES), bf16),
        scratch_shapes=[pltpu.VMEM((LANES, LANES), f32)],
        compiler_params=pltpu.CompilerParams(vmem_limit_bytes=8 * MIB),
        cost_estimate=pl.CostEstimate(
            flops=2_000_000_000, bytes_accessed=20_000_000, transcendentals=0
        ),
        name="inverses",
    )(block_fine, block_mid, block_coarse, low, high)


def two_way(values):
    hi = values.astype(bf16)
    lo = (values - hi.astype(f32)).astype(bf16)
    return jnp.concatenate([hi, lo], axis=1)


def times(values, *tables):
    values = jnp.concatenate([two_way(value) for value in values], axis=1)
    stack = []
    for table in tables:
        high = table[:, 0:LANES]
        stack += [table, jnp.concatenate([high, jnp.zeros_like(high)], axis=1)]
    result = jnp.dot(values, jnp.concatenate(stack, axis=0), preferred_element_type=f32)
    return result[:, 0:LANES] + result[:, LANES : 2 * LANES]


def exchanges(points, in_lanes):
    nodes = points**3
    tables = []
    for dimension, stride in enumerate((points * points, points, 1)):
        table = np.zeros((LANES, LANES), np.float32)
        for place in range(EX if in_lanes else 1):
            for node in range(nodes):
                index = (node // stride) % points
                for end, step in ((0, -1), (points - 1, 1)):
                    if index != end:
                        continue
                    source = place * 32 + node - step * (points - 1) * stride
                    if dimension == 0 and in_lanes:
                        if not 0 <= place + step < EX:
                            continue
                        source += step * 32
                    table[source, place * 32 + node] = 1.0
        tables.append(table)
    return tables


class Faces:
    def __init__(self, points, in_lanes):
        lane, row = iota((EY, LANES), 1), iota((EY, LANES), 0)
        local = lane % 32 if in_lanes else lane
        self.masks = []
        for dimension, stride in enumerate((points * points, points, 1)):
            index = (local // stride) % points
            first, last = index == 0, index == points - 1
            if dimension == 1:
                self.masks.append((last & (row > 0), first & (row < EY - 1)))
            else:
                self.masks.append((last, first))

    def moved(self, dimension, faces):
        reach = (FINE - 1) * FINE ** (2 - dimension)
        lane = iota((1, LANES), 1)
        index = (lane // FINE ** (2 - dimension)) % FINE
        node = lane < FINE**3
        order = jnp.where((index == 0) & node, lane + reach, LANES - 1)
        order = jnp.where((index == FINE - 1) & node, lane - reach, order)
        turned = jnp.take_along_axis(
            faces, jnp.broadcast_to(order, faces.shape), axis=1, mode="promise_in_bounds"
        )
        return jnp.where(order < LANES - 1, turned, 0.0)

    def select(self, dimension, before, after):
        from_before, from_after = self.masks[dimension]
        if before is None:
            before, after = 0.0, flat_slabs(after)
        elif after is None:
            before, after = flat_slabs(before), 0.0
        else:
            before, after = flat_slabs(before), flat_slabs(after)
        if dimension == 1:
            after = jnp.where(from_after[None], after, 0.0)
        return flat(jnp.where(from_before[None], before, after))


def coarse_rows():
    lane, row = iota((EY, LANES), 1), iota((EY, LANES), 0)
    copy, j, k = lane // 32, (lane // 2) % 2, lane % 2
    masks = (
        copy == 0,
        (copy == 1) & (j == 1) & (row > 0),
        (copy == 1) & (j == 0) & (row < EY - 1),
        (copy == 2) & (k == 1),
        (copy == 2) & (k == 0),
    )

    def build(*parts):
        result = 0.0
        for mask, part in zip(masks, parts):
            result = jnp.where(mask[None], flat_slabs(part), result)
        return flat(result)

    return build


def flat_slabs(values):
    return values.reshape(-1, EY, LANES)


CHUNK = 16


def cuts(start, stop, chunk=CHUNK):
    count = -(-(stop - start) // chunk)
    edges = [start + (stop - start) * piece // count for piece in range(count + 1)]
    return list(zip(edges[:-1], edges[1:]))


def flat(values):
    return values.reshape(-1, LANES)


def beside(ref, rows):
    before = jnp.concatenate([ref[rows, HALF - 1 : EY - 1, :], ref[rows, 0:HALF, :]], axis=1)
    after = jnp.concatenate([ref[rows, HALF:EY, :], ref[rows, 1 : HALF + 1, :]], axis=1)
    return flat(before), flat(after)


def cycle_body(
    bounds_ref,
    mine_ref,
    other_ref,
    tables_ref,
    down_ref,
    up_ref,
    out_ref,
    start,
    ping,
    pong,
    left,
    left_x,
    left_y,
    left_z,
    mid_start,
    mid_ping,
    mid_pong,
    mid_left,
    mid_left_x,
    mid_left_y,
    mid_left_z,
    mask,
):
    lefts = (left_x, left_y, left_z)
    mid_lefts = (mid_left_x, mid_left_y, mid_left_z)
    fine_faces = Faces(FINE, False)
    mid_faces = Faces(MID, True)
    coarse_row = coarse_rows()
    fine_table, *fine_tables = [tables_ref[i] for i in range(4)]
    mid_table, *mid_tables = [tables_ref[i] for i in range(4, 8)]
    lift_table, coarse_table, *low_tables = [tables_ref[i] for i in range(8, 14)]

    slab = iota((WINDOW, EY, LANES), 0)
    mask[...] = jnp.where((slab >= bounds_ref[0]) & (slab < bounds_ref[1]), 1.0, 0.0)
    upper_is_mine = bounds_ref[2] == 1

    def at(x, a, b):
        return slice(x * WINDOW + a, x * WINDOW + b)

    def get(ref, rows):
        return flat(ref[rows, :, :])

    def put(ref, rows, values):
        ref[rows, :, :] = values.reshape(-1, EY, LANES)

    def fine_gather(ref, x, a, b):
        return (
            fine_faces.select(
                0,
                get(ref, at(x - 1, a, b)) if x > 0 else None,
                get(ref, at(x + 1, a, b)) if x < EX - 1 else None,
            ),
            fine_faces.select(1, *beside(ref, at(x, a, b))),
            fine_faces.select(2, get(ref, at(x, a - 1, b - 1)), get(ref, at(x, a + 1, b + 1))),
        )

    def fine_sweep(source, target, a, b, keep):
        for x in range(EX):
            for c, d in cuts(a, b):
                rows = at(x, c, d)
                faces = fine_gather(source, x, c, d)
                if keep is not None:
                    for ref, face in zip(lefts, faces):
                        if keep[0]:
                            put(ref, rows, keep[1] * face)
                        else:
                            put(ref, rows, get(ref, rows) + keep[1] * face)
                moved = 0.3 * get(source, rows) + get(start, rows) + times(faces, *fine_tables)
                put(target, rows, moved * get(mask, at(0, c, d)))

    for x in range(EX):
        for c, d in cuts(0, WINDOW):
            values = []
            for z in range(c, d):
                for y in range(2):
                    first = x * WINDOW + y * SPLIT + z % SPLIT
                    place = pl.ds(first, HALF, stride=EX * WINDOW)
                    mine, other = mine_ref[place, :], other_ref[place, :]
                    if z < SPLIT:
                        mine, other = other, mine
                    values.append(jnp.where(upper_is_mine, mine, other))
            values = jnp.concatenate(values, axis=0)
            rows = at(x, c, d)
            put(left, rows, values)
            put(start, rows, 2.0 * times((values,), fine_table))

    fine_sweep(start, ping, 1, WINDOW - 1, (True, -0.21))
    fine_sweep(ping, pong, 2, WINDOW - 2, (False, -0.7))

    def mid_gather(faces, ref, a, b):
        here = get(ref, at(0, a, b))
        return (
            here,
            faces.select(1, *beside(ref, at(0, a, b))),
            faces.select(2, get(ref, at(0, a - 1, b - 1)), get(ref, at(0, a + 1, b + 1))),
        )

    for c, d in cuts(3, WINDOW - 3):
        values = []
        for x in range(EX):
            rest = 0.027 * get(left, at(x, c, d))
            for dimension, face in enumerate(fine_gather(pong, x, c, d)):
                face = 0.5 * (get(lefts[dimension], at(x, c, d)) + face)
                rest = rest + fine_faces.moved(dimension, face)
            values.append(rest)
        tables = [down_ref[x] for x in range(EX)]
        rows = at(0, c, d)
        total = times(values, *tables) * get(mask, rows)
        put(mid_left, rows, total)
        put(mid_start, rows, 2.0 * times((total,), mid_table))

    def mid_sweep(faces, tables, base, source, target, margin, keep=None):
        for c, d in cuts(margin, WINDOW - margin, CHUNK // 2):
            rows = at(0, c, d)
            values = mid_gather(faces, source, c, d)
            if keep is not None:
                for ref, face in zip(mid_lefts, values):
                    if keep[0]:
                        put(ref, rows, keep[1] * face)
                    else:
                        put(ref, rows, get(ref, rows) + keep[1] * face)
            moved = 0.3 * get(source, rows) + get(base, rows) + times(values, *tables)
            put(target, rows, moved * get(mask, rows))

    mid_sweep(mid_faces, mid_tables, mid_start, mid_start, mid_ping, 4, (True, -0.21))
    mid_sweep(mid_faces, mid_tables, mid_start, mid_ping, mid_pong, 5, (False, -0.7))

    base = ping.at[0:WINDOW]
    even = ping.at[WINDOW : 2 * WINDOW]
    odd = ping.at[2 * WINDOW : 3 * WINDOW]
    for c, d in cuts(6, WINDOW - 6):
        rows = at(0, c, d)
        faces = mid_gather(mid_faces, mid_pong, c, d)
        values = [get(mid_left, rows)]
        for ref, face in zip(mid_lefts, faces):
            values.append(get(ref, rows) + face)
        put(base, rows, times(values, *low_tables) * get(mask, rows))

    for c, d in cuts(10, WINDOW - 10, CHUNK // 2):
        rows = at(0, c, d)
        moved = times(mid_gather(mid_faces, mid_pong, c, d), *mid_tables)
        put(mid_left, rows, 0.3 * get(mid_pong, rows) + get(mid_start, rows) + moved)

    def coarse_gather(ref, a, b):
        rows = at(0, a, b)
        near = beside(ref, rows)
        return coarse_row(
            get(ref, rows), *near, get(ref, at(0, a - 1, b - 1)), get(ref, at(0, a + 1, b + 1))
        )

    def coarse_sweep(source, target, margin):
        for c, d in cuts(margin, WINDOW - margin, CHUNK // 2):
            rows = at(0, c, d)
            moved = times((coarse_gather(source, c, d),), coarse_table)
            moved = 0.3 * get(source, rows) + get(base, rows) + moved
            put(target, rows, moved * get(mask, rows))

    coarse_sweep(base, even, 7)
    coarse_sweep(even, odd, 8)
    coarse_sweep(odd, even, 9)

    for c, d in cuts(10, WINDOW - 10, CHUNK // 2):
        rows = at(0, c, d)
        moved = get(mid_left, rows) + times((coarse_gather(even, c, d),), lift_table)
        put(mid_ping, rows, moved * get(mask, rows))
    mid_sweep(mid_faces, mid_tables, mid_start, mid_ping, mid_pong, 11)
    mid_sweep(mid_faces, mid_tables, mid_start, mid_pong, mid_ping, 12)

    lifted = get(mid_ping, at(0, 12, WINDOW - 12))
    for x in range(EX):
        rows = at(x, 12, WINDOW - 12)
        put(pong, rows, get(pong, rows) + times((lifted,), up_ref[x]))
    fine_sweep(pong, ping, 13, WINDOW - 13, None)
    fine_sweep(ping, pong, 14, WINDOW - 14, None)
    fine_sweep(pong, ping, RADIUS, WINDOW - RADIUS, None)

    for x in range(EX):
        for z in range(OWN):
            for y in range(2):
                values = ping[x * WINDOW + RADIUS + z, y * HALF : (y + 1) * HALF, :]
                first = x * OWN * 2 + z * 2 + y
                out_ref[pl.ds(first, HALF, stride=EX * 2 * OWN), :] = values


def cycle(bounds, mine, other, tables, down, up):
    big = pltpu.VMEM((EX * WINDOW, EY, LANES), f32)
    small = pltpu.VMEM((WINDOW, EY, LANES), f32)
    vmem = pl.BlockSpec(memory_space=pltpu.VMEM)
    return pl.pallas_call(
        cycle_body,
        out_shape=jax.ShapeDtypeStruct((EX * HALF * 2 * OWN, LANES), f32),
        in_specs=[pl.BlockSpec(memory_space=pltpu.SMEM)] + [vmem] * 5,
        out_specs=vmem,
        scratch_shapes=[big] * 7 + [small] * 8,
        compiler_params=pltpu.CompilerParams(vmem_limit_bytes=20 * MIB),
        name="cycle",
    )(bounds, mine, other, tables, down, up)


def per_device(fine_source_field, scaling, block_fine, block_mid, block_coarse):
    count_z = scaling.shape[2]
    parts = lax.axis_size("gx") * lax.axis_size("gy")
    groups = lax.axis_size("gz")
    down, up, low, high = transfer_tables()
    group = lax.axis_index("gz")
    core = group % 2
    cores = core.astype(jnp.int32).reshape(1)

    own, edge = pack(cores, fine_source_field, scaling)
    ties = [(i, i + 1) for i in range(1, groups - 1, 2)]
    pairs = [(i, i ^ 1) for i in range(groups)]
    halo = settle(lax.ppermute(edge, "gz", ties + [(j, i) for i, j in ties]))
    sibling = lax.ppermute(own, "gz", pairs)
    chunks = window(cores, own, sibling, halo, parts)
    chunks, *matrices = lax.optimization_barrier((chunks, block_fine, block_mid, block_coarse))
    recv = lax.all_to_all(
        chunks.reshape(parts * WINDOW // 2, 2, LANES), ("gy", "gx"), 0, 0, tiled=True
    ).reshape(parts * WINDOW, LANES)
    recv, tables = lax.optimization_barrier((recv, inverses(*matrices, low, high)))
    tall = lax.axis_size("gy")
    ways = [
        (y * groups + i, y * groups + (i ^ 1))
        for y in range(tall)
        for i in range(groups)
        if i % 2 == (1 if 2 * y < tall else 0)
    ]
    other = lax.ppermute(recv, ("gy", "gz"), ways)

    part = lax.axis_index("gy") * lax.axis_size("gx") + lax.axis_index("gx")
    first = (group - core) * count_z + OWN * part - RADIUS
    bounds = jnp.stack(
        [jnp.maximum(0, -first), jnp.minimum(WINDOW, groups * count_z - first), core]
    )
    result = cycle(
        bounds.astype(jnp.int32), recv, other, tables, down, up
    )
    back = lax.all_to_all(
        result.reshape(parts, 2 * OWN, LANES), ("gy", "gx"), 0, 0, tiled=True
    ).reshape(parts * 2 * OWN, LANES)
    return unpack(cores, back, scaling, fine_source_field.shape)


def solution(mesh):
    in_specs = (P("gx", "gy", "gz"), P("gx", "gy", "gz"), P(), P(), P())
    out_specs = P("gx", "gy", "gz")
    return jax.shard_map(
        per_device, mesh=mesh, in_specs=in_specs, out_specs=out_specs, check_vma=False
    )
```

```python
import math

import jax
import jax.numpy as jnp
import numpy as np
from jax import lax
from jax.experimental import pallas as pl
from jax.experimental.pallas import tpu as pltpu
from jax.sharding import PartitionSpec as P

FINE = 5
MID = 3
COARSE = 2
CSWEEPS = 4
RADIUS = 15
HALO = 16
OWN = 4
WINDOW = OWN + 2 * RADIUS
SPLIT = WINDOW // 2
EX = 4
EY = 16
HALF = EY // 2
LANES = 128

f32 = jnp.float32
bf16 = jnp.bfloat16
HIGHEST = lax.Precision.HIGHEST
MIB = 1 << 20


def gll_points(points):
    if points == 5:
        return np.array([-1.0, -math.sqrt(3.0 / 7.0), 0.0, math.sqrt(3.0 / 7.0), 1.0])
    if points == 3:
        return np.array([-1.0, 0.0, 1.0])
    return np.array([-1.0, 1.0])


def lagrange(fine_points, coarse_points):
    fine_nodes = gll_points(fine_points)
    coarse_nodes = gll_points(coarse_points)
    table = np.ones((fine_points, coarse_points))
    for column in range(coarse_points):
        for other in range(coarse_points):
            if other != column:
                table[:, column] *= (fine_nodes - coarse_nodes[other]) / (
                    coarse_nodes[column] - coarse_nodes[other]
                )
    return table


def halves(table):
    table = np.asarray(table, np.float32)
    hi = table.astype(jnp.bfloat16)
    lo = (table - hi.astype(np.float32)).astype(jnp.bfloat16)
    return np.concatenate([hi, lo], axis=1)


def transfer_tables():
    fine_mid = np.kron(np.kron(lagrange(5, 3), lagrange(5, 3)), lagrange(5, 3))
    mid_coarse = np.kron(np.kron(lagrange(3, 2), lagrange(3, 2)), lagrange(3, 2))
    down, up = [], []
    for place in range(EX):
        table = np.zeros((LANES, LANES))
        table[:125, place * 32 : place * 32 + 27] = fine_mid
        down.append(halves(table))
        up.append(halves(table.T))
    middle = np.zeros((LANES, LANES), np.float32)
    for place in range(EX):
        middle[place * 32 : place * 32 + 27, place * 8 : place * 8 + 8] = mid_coarse
    low = [0.027 * middle]
    low += [0.5 * np.dot(move, middle) for move in exchanges(MID, True)]
    high = [np.roll(middle.T, 32 * copy, axis=0) for copy in range(3)]
    return np.stack(down), np.stack(up), np.stack(low), np.stack(high)


def iota(shape, dimension):
    return lax.broadcasted_iota(jnp.int32, shape, dimension)


def three_way(values):
    one = values.astype(bf16)
    rest = values - one.astype(f32)
    two = rest.astype(bf16)
    three = (rest - two.astype(f32)).astype(bf16)
    return jnp.concatenate([one, two, three], axis=0)


def place_of(lane, y):
    i, j, k = lane // (FINE * FINE), (lane // FINE) % FINE, lane % FINE
    return jnp.where(lane < FINE**3, k * LANES + i * 2 * FINE + y * FINE + j, -1)


def pack_body(core_ref, field_ref, scale_ref, own_ref, edge_ref, lines, turned, *, count_z):
    lines[...] = jnp.zeros_like(lines)
    for i in range(FINE):
        lines[i * 2 * FINE : (i + 1) * 2 * FINE, 0 : count_z * FINE] = field_ref[i]
    for part in range(lines.shape[1] // LANES):
        lanes = slice(part * LANES, (part + 1) * LANES)
        turned[lanes, :] = lines[:, lanes].T
    lane = iota((1, 2 * LANES), 1)
    place = place_of(lane % LANES, lane // LANES)
    table = jnp.where(iota((FINE * LANES, 2 * LANES), 0) == place, 1.0, 0.0).astype(bf16)
    values = [turned[pl.ds(k, count_z, stride=FINE), :] for k in range(FINE)]
    nodes = jnp.dot(
        three_way(jnp.concatenate(values, axis=1)), table, preferred_element_type=f32
    )
    nodes = nodes[0:count_z] + nodes[count_z : 2 * count_z] + nodes[2 * count_z : 3 * count_z]
    scale = scale_ref[0].T
    for y in range(2):
        own_ref[y] = nodes[:, y * LANES : (y + 1) * LANES] / scale[:, y : y + 1]
    start = pl.multiple_of(core_ref[0] * (count_z - HALO), HALO)
    for y in range(2):
        edge_ref[y] = own_ref[y, pl.ds(start, HALO), :]


def pack(core, field, scaling):
    count_z = scaling.shape[2]
    width = -(-count_z * FINE // LANES) * LANES

    def body(*refs):
        pack_body(*refs, count_z=count_z)

    vmem = pl.BlockSpec(memory_space=pltpu.VMEM)
    return pl.pallas_call(
        body,
        out_shape=(
            jax.ShapeDtypeStruct((2, count_z, LANES), f32),
            jax.ShapeDtypeStruct((2, HALO, LANES), f32),
        ),
        in_specs=[pl.BlockSpec(memory_space=pltpu.SMEM), vmem, vmem],
        out_specs=(vmem, vmem),
        scratch_shapes=[pltpu.VMEM((LANES, width), f32), pltpu.VMEM((width, LANES), f32)],
        compiler_params=pltpu.CompilerParams(vmem_limit_bytes=8 * MIB),
        name="pack",
    )(core, field, scaling)


def settle(halo):
    def body(in_ref, out_ref):
        out_ref[...] = in_ref[...]

    return pl.pallas_call(
        body,
        out_shape=jax.ShapeDtypeStruct(halo.shape, f32),
        cost_estimate=pl.CostEstimate(
            flops=2_000_000_000, bytes_accessed=20_000_000, transcendentals=0
        ),
        compiler_params=pltpu.CompilerParams(vmem_limit_bytes=8 * MIB),
        name="settle",
    )(halo)


PIECES = 4


def window_body(
    core_ref, own_ref, sibling_ref, halo_ref, out_ref, line, block, sems, *, parts
):
    count_z = own_ref.shape[1]
    rows = parts // PIECES * WINDOW
    for core in range(2):
        places = (HALO, HALO + count_z, 0) if core == 0 else (count_z, 0, 2 * count_z)

        @pl.when(core_ref[0] == core)
        def _(core=core, places=places):
            for ref, place in zip((own_ref, sibling_ref, halo_ref), places):
                line[:, place : place + ref.shape[1], :] = ref[...]
            first = HALO - RADIUS if core == 0 else SPLIT - RADIUS
            copies = []
            for part in range(parts):
                for y in range(2):
                    start = first + OWN * part
                    row = part * WINDOW + y * SPLIT
                    block[row : row + SPLIT, :] = line[y, start : start + SPLIT, :]
                if (part + 1) % (parts // PIECES) == 0:
                    piece = part // (parts // PIECES)
                    place = slice(piece * rows, (piece + 1) * rows)
                    copies.append(
                        pltpu.make_async_copy(
                            block.at[place, :], out_ref.at[place, :], sems.at[piece]
                        )
                    )
                    copies[-1].start(priority=piece % 2)
            for copy in copies:
                copy.wait()


def window(core, own, sibling, halo, parts):
    def body(*refs):
        window_body(*refs, parts=parts)

    vmem = pl.BlockSpec(memory_space=pltpu.VMEM)
    return pl.pallas_call(
        body,
        out_shape=jax.ShapeDtypeStruct((parts * WINDOW, LANES), f32),
        in_specs=[pl.BlockSpec(memory_space=pltpu.SMEM), vmem, vmem, vmem],
        out_specs=pl.BlockSpec(memory_space=pl.ANY),
        scratch_shapes=[
            pltpu.VMEM((2, 2 * own.shape[1] + HALO, LANES), f32),
            pltpu.VMEM((parts * WINDOW, LANES), f32),
            pltpu.SemaphoreType.DMA((PIECES,)),
        ],
        compiler_params=pltpu.CompilerParams(vmem_limit_bytes=8 * MIB),
        name="window",
    )(core, own, sibling, halo)


def unpack_body(core_ref, back_ref, scale_ref, out_ref, turned, *, count_z):
    scale = scale_ref[0].T
    base = core_ref[0] * (2 * count_z)
    rows = [
        back_ref[pl.ds(base + y, count_z, stride=2), :] / scale[:, y : y + 1] for y in range(2)
    ]
    table = jnp.concatenate(
        [
            jnp.where(
                iota((LANES, FINE * LANES), 1) == place_of(iota((LANES, 1), 0), y), 1.0, 0.0
            )
            for y in range(2)
        ],
        axis=0,
    ).astype(bf16)
    spread = jnp.dot(
        three_way(jnp.concatenate(rows, axis=1)), table, preferred_element_type=f32
    )
    spread = spread[0:count_z] + spread[count_z : 2 * count_z] + spread[2 * count_z : 3 * count_z]
    for k in range(FINE):
        turned[pl.ds(k, count_z, stride=FINE), :] = spread[:, k * LANES : (k + 1) * LANES]
    lines = [
        turned[part * LANES : (part + 1) * LANES, :].T for part in range(turned.shape[0] // LANES)
    ]
    lines = jnp.concatenate(lines, axis=1)
    for i in range(FINE):
        out_ref[i] = lines[i * 2 * FINE : (i + 1) * 2 * FINE, 0 : count_z * FINE]


def unpack(core, back, scaling, shape):
    count_z = scaling.shape[2]
    width = -(-count_z * FINE // LANES) * LANES

    def body(*refs):
        unpack_body(*refs, count_z=count_z)

    vmem = pl.BlockSpec(memory_space=pltpu.VMEM)
    return pl.pallas_call(
        body,
        out_shape=jax.ShapeDtypeStruct(shape, f32),
        in_specs=[pl.BlockSpec(memory_space=pltpu.SMEM), vmem, vmem],
        out_specs=vmem,
        scratch_shapes=[pltpu.VMEM((width, LANES), f32)],
        compiler_params=pltpu.CompilerParams(vmem_limit_bytes=8 * MIB),
        name="unpack",
    )(core, back, scaling)


def shifted_block(ref, pad, points):
    nodes = points**3
    pad[...] = jnp.zeros((LANES, LANES), f32)
    pad[0:nodes, 0:nodes] = ref[...]
    lane, row = iota((LANES, LANES), 1), iota((LANES, LANES), 0)
    count = jnp.zeros((LANES, LANES), f32)
    for stride in (points * points, points, 1):
        index = (lane // stride) % points
        count = count + jnp.where((index == 0) | (index == points - 1), 0.5, 0.0)
    diagonal = jnp.where(lane < nodes, count, 1.0)
    return pad[...] + jnp.where(lane == row, diagonal, 0.0)


def invert(matrix, panels):
    lane, row = iota((LANES, LANES), 1), iota((LANES, LANES), 0)
    lane1, lane16, row16 = iota((1, LANES), 1), iota((16, LANES), 1), iota((16, LANES), 0)
    for panel in range(panels):
        top = panel * 16
        rows = matrix[top : top + 16, :]
        for step in range(0, 16, 2):
            pivot = top + step
            left = jnp.broadcast_to(rows[:, pivot : pivot + 1], (16, LANES))
            right = jnp.broadcast_to(rows[:, pivot + 1 : pivot + 2], (16, LANES))
            a, b = left[step : step + 1], right[step : step + 1]
            c, d = left[step + 1 : step + 2], right[step + 1 : step + 2]
            scale = 1.0 / (a * d - b * c)
            here = (lane1 == pivot) | (lane1 == pivot + 1)
            one = jnp.where(here, jnp.where(lane1 == pivot, 1.0, 0.0), rows[step : step + 1])
            two = jnp.where(here, jnp.where(lane1 == pivot, 0.0, 1.0), rows[step + 1 : step + 2])
            one, two = (d * one - b * two) * scale, (a * two - c * one) * scale
            others = jnp.where((lane16 == pivot) | (lane16 == pivot + 1), 0.0, rows)
            others = others - left * one - right * two
            rows = jnp.where(row16 == step, one, jnp.where(row16 == step + 1, two, others))
        stacked = jnp.concatenate([rows] * 8, axis=0)
        inside = (lane >= top) & (lane < top + 16)
        update = jnp.dot(
            jnp.where(inside, matrix, 0.0), stacked, precision=HIGHEST, preferred_element_type=f32
        )
        matrix = jnp.where(
            (row >= top) & (row < top + 16), stacked, jnp.where(inside, 0.0, matrix) - update
        )
    return matrix


def exact(left, right):
    return jnp.dot(left, right, precision=HIGHEST, preferred_element_type=f32)


def repeated(matrix, width):
    lane, row = iota((LANES, LANES), 1), iota((LANES, LANES), 0)
    used = (lane < EX * width) & (row < EX * width)
    pick = jnp.where((row % width == lane) & (lane < width), 1.0, 0.0)
    put = jnp.where((lane % width == row) & (row < width), 1.0, 0.0)
    wide = exact(exact(pick, matrix), put)
    return jnp.where(used & (row // width == lane // width), wide, 0.0)


def moves(points, width):
    lane, row = iota((1, LANES), 1), iota((LANES, LANES), 0)
    local, place = lane % width, lane // width
    tables = []
    for dimension, stride in enumerate((points * points, points, 1)):
        index = (local // stride) % points
        first = (index == 0) & (local < points**3)
        last = (index == points - 1) & (local < points**3)
        reach = (points - 1) * stride
        if dimension == 0 and width < LANES:
            first, last = first & (place > 0), last & (place < EX - 1)
            reach = reach - width
        source = jnp.where(first, lane + reach, jnp.where(last, lane - reach, -LANES))
        tables.append((row, source))
    return tables


def inverses_body(fine_ref, mid_ref, coarse_ref, low_ref, high_ref, out_ref, pad):
    lane, row = iota((LANES, LANES), 1), iota((LANES, LANES), 0)
    coarse = invert(shifted_block(coarse_ref, pad, COARSE), 1)
    mid = invert(shifted_block(mid_ref, pad, MID), 2)
    fine = invert(shifted_block(fine_ref, pad, FINE), 8)
    levels = ((fine, FINE, LANES), (repeated(mid, 32), MID, 32))
    for level, (inverse, points, width) in enumerate(levels):
        inverse = 0.35 * inverse
        out_ref[4 * level] = two_way(inverse)
        moved = []
        for dimension, (own, source) in enumerate(moves(points, width)):
            moved.append(exact(jnp.where(own == source, 1.0, 0.0), inverse))
            out_ref[4 * level + 1 + dimension] = two_way(moved[dimension])
    lifted = 0.3 * high_ref[0]
    for dimension in range(3):
        lifted = lifted + exact(high_ref[dimension], moved[dimension])
    out_ref[8] = two_way(lifted)
    copies = jnp.where((lane % 32 == row) & (lane < 96), 1.0, 0.0)
    inverse = exact(0.35 * repeated(coarse, 8), copies)
    gather = jnp.zeros((LANES, LANES), f32)
    for dimension, (own, source) in enumerate(moves(COARSE, 8)):
        gather = gather + jnp.where((own == source + 32 * dimension) & (lane < 32), 1.0, 0.0)
    out_ref[9] = two_way(exact(gather, inverse))
    for part in range(4):
        out_ref[10 + part] = two_way(exact(low_ref[part], 2.0 * inverse))


def inverses(block_fine, block_mid, block_coarse, low, high):
    return pl.pallas_call(
        inverses_body,
        out_shape=jax.ShapeDtypeStruct((14, LANES, 2 * LANES), bf16),
        scratch_shapes=[pltpu.VMEM((LANES, LANES), f32)],
        compiler_params=pltpu.CompilerParams(vmem_limit_bytes=8 * MIB),
        cost_estimate=pl.CostEstimate(
            flops=2_000_000_000, bytes_accessed=20_000_000, transcendentals=0
        ),
        name="inverses",
    )(block_fine, block_mid, block_coarse, low, high)


def two_way(values):
    hi = values.astype(bf16)
    lo = (values - hi.astype(f32)).astype(bf16)
    return jnp.concatenate([hi, lo], axis=1)


def times(values, *tables):
    values = jnp.concatenate([two_way(value) for value in values], axis=1)
    stack = []
    for table in tables:
        high = table[:, 0:LANES]
        stack += [table, jnp.concatenate([high, jnp.zeros_like(high)], axis=1)]
    result = jnp.dot(values, jnp.concatenate(stack, axis=0), preferred_element_type=f32)
    return result[:, 0:LANES] + result[:, LANES : 2 * LANES]


def exchanges(points, in_lanes):
    nodes = points**3
    tables = []
    for dimension, stride in enumerate((points * points, points, 1)):
        table = np.zeros((LANES, LANES), np.float32)
        for place in range(EX if in_lanes else 1):
            for node in range(nodes):
                index = (node // stride) % points
                for end, step in ((0, -1), (points - 1, 1)):
                    if index != end:
                        continue
                    source = place * 32 + node - step * (points - 1) * stride
                    if dimension == 0 and in_lanes:
                        if not 0 <= place + step < EX:
                            continue
                        source += step * 32
                    table[source, place * 32 + node] = 1.0
        tables.append(table)
    return tables


class Faces:
    def __init__(self, points, in_lanes):
        lane, row = iota((EY, LANES), 1), iota((EY, LANES), 0)
        local = lane % 32 if in_lanes else lane
        self.masks = []
        for dimension, stride in enumerate((points * points, points, 1)):
            index = (local // stride) % points
            first, last = index == 0, index == points - 1
            if dimension == 1:
                self.masks.append((last & (row > 0), first & (row < EY - 1)))
            else:
                self.masks.append((last, first))

    def moved(self, dimension, faces):
        reach = (FINE - 1) * FINE ** (2 - dimension)
        lane = iota((1, LANES), 1)
        index = (lane // FINE ** (2 - dimension)) % FINE
        node = lane < FINE**3
        order = jnp.where((index == 0) & node, lane + reach, LANES - 1)
        order = jnp.where((index == FINE - 1) & node, lane - reach, order)
        turned = jnp.take_along_axis(
            faces, jnp.broadcast_to(order, faces.shape), axis=1, mode="promise_in_bounds"
        )
        return jnp.where(order < LANES - 1, turned, 0.0)

    def select(self, dimension, before, after):
        from_before, from_after = self.masks[dimension]
        if before is None:
            before, after = 0.0, flat_slabs(after)
        elif after is None:
            before, after = flat_slabs(before), 0.0
        else:
            before, after = flat_slabs(before), flat_slabs(after)
        if dimension == 1:
            after = jnp.where(from_after[None], after, 0.0)
        return flat(jnp.where(from_before[None], before, after))


def coarse_rows():
    lane, row = iota((EY, LANES), 1), iota((EY, LANES), 0)
    copy, j, k = lane // 32, (lane // 2) % 2, lane % 2
    masks = (
        copy == 0,
        (copy == 1) & (j == 1) & (row > 0),
        (copy == 1) & (j == 0) & (row < EY - 1),
        (copy == 2) & (k == 1),
        (copy == 2) & (k == 0),
    )

    def build(*parts):
        result = 0.0
        for mask, part in zip(masks, parts):
            result = jnp.where(mask[None], flat_slabs(part), result)
        return flat(result)

    return build


def flat_slabs(values):
    return values.reshape(-1, EY, LANES)


CHUNK = 16


def cuts(start, stop, chunk=CHUNK):
    count = -(-(stop - start) // chunk)
    edges = [start + (stop - start) * piece // count for piece in range(count + 1)]
    return list(zip(edges[:-1], edges[1:]))


def flat(values):
    return values.reshape(-1, LANES)


def beside(ref, rows):
    before = jnp.concatenate([ref[rows, HALF - 1 : EY - 1, :], ref[rows, 0:HALF, :]], axis=1)
    after = jnp.concatenate([ref[rows, HALF:EY, :], ref[rows, 1 : HALF + 1, :]], axis=1)
    return flat(before), flat(after)


def cycle_body(
    bounds_ref,
    mine_ref,
    other_ref,
    tables_ref,
    down_ref,
    up_ref,
    out_ref,
    start,
    ping,
    pong,
    left,
    left_x,
    left_y,
    left_z,
    mid_start,
    mid_ping,
    mid_pong,
    mid_left,
    mid_left_x,
    mid_left_y,
    mid_left_z,
    mask,
):
    lefts = (left_x, left_y, left_z)
    mid_lefts = (mid_left_x, mid_left_y, mid_left_z)
    fine_faces = Faces(FINE, False)
    mid_faces = Faces(MID, True)
    coarse_row = coarse_rows()
    fine_table, *fine_tables = [tables_ref[i] for i in range(4)]
    mid_table, *mid_tables = [tables_ref[i] for i in range(4, 8)]
    lift_table, coarse_table, *low_tables = [tables_ref[i] for i in range(8, 14)]

    slab = iota((WINDOW, EY, LANES), 0)
    mask[...] = jnp.where((slab >= bounds_ref[0]) & (slab < bounds_ref[1]), 1.0, 0.0)
    upper_is_mine = bounds_ref[2] == 1

    def at(x, a, b):
        return slice(x * WINDOW + a, x * WINDOW + b)

    def get(ref, rows):
        return flat(ref[rows, :, :])

    def put(ref, rows, values):
        ref[rows, :, :] = values.reshape(-1, EY, LANES)

    def fine_gather(ref, x, a, b):
        return (
            fine_faces.select(
                0,
                get(ref, at(x - 1, a, b)) if x > 0 else None,
                get(ref, at(x + 1, a, b)) if x < EX - 1 else None,
            ),
            fine_faces.select(1, *beside(ref, at(x, a, b))),
            fine_faces.select(2, get(ref, at(x, a - 1, b - 1)), get(ref, at(x, a + 1, b + 1))),
        )

    def fine_sweep(source, target, a, b, keep):
        for x in range(EX):
            for c, d in cuts(a, b):
                rows = at(x, c, d)
                faces = fine_gather(source, x, c, d)
                if keep is not None:
                    for ref, face in zip(lefts, faces):
                        if keep[0]:
                            put(ref, rows, keep[1] * face)
                        else:
                            put(ref, rows, get(ref, rows) + keep[1] * face)
                moved = 0.3 * get(source, rows) + get(start, rows) + times(faces, *fine_tables)
                put(target, rows, moved * get(mask, at(0, c, d)))

    for x in range(EX):
        for c, d in cuts(0, WINDOW):
            values = []
            for z in range(c, d):
                for y in range(2):
                    first = x * HALF * WINDOW + y * SPLIT + z % SPLIT
                    place = pl.ds(first, HALF, stride=WINDOW)
                    mine, other = mine_ref[place, :], other_ref[place, :]
                    if z < SPLIT:
                        mine, other = other, mine
                    values.append(jnp.where(upper_is_mine, mine, other))
            values = jnp.concatenate(values, axis=0)
            rows = at(x, c, d)
            put(left, rows, values)
            put(start, rows, 2.0 * times((values,), fine_table))

    fine_sweep(start, ping, 1, WINDOW - 1, (True, -0.21))
    fine_sweep(ping, pong, 2, WINDOW - 2, (False, -0.7))

    def mid_gather(faces, ref, a, b):
        here = get(ref, at(0, a, b))
        return (
            here,
            faces.select(1, *beside(ref, at(0, a, b))),
            faces.select(2, get(ref, at(0, a - 1, b - 1)), get(ref, at(0, a + 1, b + 1))),
        )

    for c, d in cuts(3, WINDOW - 3):
        values = []
        for x in range(EX):
            rest = 0.027 * get(left, at(x, c, d))
            for dimension, face in enumerate(fine_gather(pong, x, c, d)):
                face = 0.5 * (get(lefts[dimension], at(x, c, d)) + face)
                rest = rest + fine_faces.moved(dimension, face)
            values.append(rest)
        tables = [down_ref[x] for x in range(EX)]
        rows = at(0, c, d)
        total = times(values, *tables) * get(mask, rows)
        put(mid_left, rows, total)
        put(mid_start, rows, 2.0 * times((total,), mid_table))

    def mid_sweep(faces, tables, base, source, target, margin, keep=None):
        for c, d in cuts(margin, WINDOW - margin, CHUNK // 2):
            rows = at(0, c, d)
            values = mid_gather(faces, source, c, d)
            if keep is not None:
                for ref, face in zip(mid_lefts, values):
                    if keep[0]:
                        put(ref, rows, keep[1] * face)
                    else:
                        put(ref, rows, get(ref, rows) + keep[1] * face)
            moved = 0.3 * get(source, rows) + get(base, rows) + times(values, *tables)
            put(target, rows, moved * get(mask, rows))

    mid_sweep(mid_faces, mid_tables, mid_start, mid_start, mid_ping, 4, (True, -0.21))
    mid_sweep(mid_faces, mid_tables, mid_start, mid_ping, mid_pong, 5, (False, -0.7))

    base = ping.at[0:WINDOW]
    even = ping.at[WINDOW : 2 * WINDOW]
    odd = ping.at[2 * WINDOW : 3 * WINDOW]
    for c, d in cuts(6, WINDOW - 6):
        rows = at(0, c, d)
        faces = mid_gather(mid_faces, mid_pong, c, d)
        values = [get(mid_left, rows)]
        for ref, face in zip(mid_lefts, faces):
            values.append(get(ref, rows) + face)
        put(base, rows, times(values, *low_tables) * get(mask, rows))

    for c, d in cuts(10, WINDOW - 10, CHUNK // 2):
        rows = at(0, c, d)
        moved = times(mid_gather(mid_faces, mid_pong, c, d), *mid_tables)
        put(mid_left, rows, 0.3 * get(mid_pong, rows) + get(mid_start, rows) + moved)

    def coarse_gather(ref, a, b):
        rows = at(0, a, b)
        near = beside(ref, rows)
        return coarse_row(
            get(ref, rows), *near, get(ref, at(0, a - 1, b - 1)), get(ref, at(0, a + 1, b + 1))
        )

    def coarse_sweep(source, target, margin):
        for c, d in cuts(margin, WINDOW - margin, CHUNK // 2):
            rows = at(0, c, d)
            moved = times((coarse_gather(source, c, d),), coarse_table)
            moved = 0.3 * get(source, rows) + get(base, rows) + moved
            put(target, rows, moved * get(mask, rows))

    coarse_sweep(base, even, 7)
    coarse_sweep(even, odd, 8)
    coarse_sweep(odd, even, 9)

    for c, d in cuts(10, WINDOW - 10, CHUNK // 2):
        rows = at(0, c, d)
        moved = get(mid_left, rows) + times((coarse_gather(even, c, d),), lift_table)
        put(mid_ping, rows, moved * get(mask, rows))
    mid_sweep(mid_faces, mid_tables, mid_start, mid_ping, mid_pong, 11)
    mid_sweep(mid_faces, mid_tables, mid_start, mid_pong, mid_ping, 12)

    lifted = get(mid_ping, at(0, 12, WINDOW - 12))
    for x in range(EX):
        rows = at(x, 12, WINDOW - 12)
        put(pong, rows, get(pong, rows) + times((lifted,), up_ref[x]))
    def pair_sweep(source, target, margin):
        a, b = margin, WINDOW - margin
        count = (b - a) * EY
        for x in range(0, EX, 2):
            faces = [fine_gather(source, x + i, a, b) for i in range(2)]
            faces = [jnp.concatenate(parts, axis=0) for parts in zip(*faces)]
            moved = times(faces, *fine_tables)
            for i in range(2):
                rows = at(x + i, a, b)
                part = 0.3 * get(source, rows) + get(start, rows)
                part = part + moved[i * count : (i + 1) * count]
                put(target, rows, part * get(mask, at(0, a, b)))

    pair_sweep(pong, ping, 13)
    pair_sweep(ping, pong, 14)
    pair_sweep(pong, ping, RADIUS)

    for x in range(EX):
        for z in range(OWN):
            for y in range(2):
                values = ping[x * WINDOW + RADIUS + z, y * HALF : (y + 1) * HALF, :]
                first = x * HALF * OWN * 2 + z * 2 + y
                out_ref[pl.ds(first, HALF, stride=2 * OWN), :] = values


def cycle(bounds, mine, other, tables, down, up):
    big = pltpu.VMEM((EX * WINDOW, EY, LANES), f32)
    small = pltpu.VMEM((WINDOW, EY, LANES), f32)
    vmem = pl.BlockSpec(memory_space=pltpu.VMEM)
    return pl.pallas_call(
        cycle_body,
        out_shape=jax.ShapeDtypeStruct((EX * HALF * 2 * OWN, LANES), f32),
        in_specs=[pl.BlockSpec(memory_space=pltpu.SMEM)] + [vmem] * 5,
        out_specs=vmem,
        scratch_shapes=[big] * 7 + [small] * 8,
        compiler_params=pltpu.CompilerParams(vmem_limit_bytes=20 * MIB),
        name="cycle",
    )(bounds, mine, other, tables, down, up)


def per_device(fine_source_field, scaling, block_fine, block_mid, block_coarse):
    count_z = scaling.shape[2]
    parts = lax.axis_size("gx") * lax.axis_size("gy")
    groups = lax.axis_size("gz")
    down, up, low, high = transfer_tables()
    group = lax.axis_index("gz")
    core = group % 2
    cores = core.astype(jnp.int32).reshape(1)

    own, edge = pack(cores, fine_source_field, scaling)
    ties = [(i, i + 1) for i in range(1, groups - 1, 2)]
    pairs = [(i, i ^ 1) for i in range(groups)]
    halo = settle(lax.ppermute(edge, "gz", ties + [(j, i) for i, j in ties]))
    sibling = lax.ppermute(own, "gz", pairs)
    chunks = window(cores, own, sibling, halo, parts)
    chunks, *matrices = lax.optimization_barrier((chunks, block_fine, block_mid, block_coarse))
    recv = lax.all_to_all(
        chunks.reshape(parts * WINDOW // 2, 2, LANES), ("gx", "gy"), 0, 0, tiled=True
    ).reshape(parts * WINDOW, LANES)
    recv, tables = lax.optimization_barrier((recv, inverses(*matrices, low, high)))
    wide = lax.axis_size("gx")
    ways = [
        (x * groups + i, x * groups + (i ^ 1))
        for x in range(wide)
        for i in range(groups)
        if i % 2 == (1 if 2 * x < wide else 0)
    ]
    other = lax.ppermute(recv, ("gx", "gz"), ways)

    part = lax.axis_index("gx") * lax.axis_size("gy") + lax.axis_index("gy")
    first = (group - core) * count_z + OWN * part - RADIUS
    bounds = jnp.stack(
        [jnp.maximum(0, -first), jnp.minimum(WINDOW, groups * count_z - first), core]
    )
    result = cycle(
        bounds.astype(jnp.int32), recv, other, tables, down, up
    )
    back = lax.all_to_all(
        result.reshape(parts, 2 * OWN, LANES), ("gx", "gy"), 0, 0, tiled=True
    ).reshape(parts * 2 * OWN, LANES)
    return unpack(cores, back, scaling, fine_source_field.shape)


def solution(mesh):
    in_specs = (P("gx", "gy", "gz"), P("gx", "gy", "gz"), P(), P(), P())
    out_specs = P("gx", "gy", "gz")
    return jax.shard_map(
        per_device, mesh=mesh, in_specs=in_specs, out_specs=out_specs, check_vma=False
    )
```

```python
import math

import jax
import jax.numpy as jnp
import numpy as np
from jax import lax
from jax.experimental import pallas as pl
from jax.experimental.pallas import tpu as pltpu
from jax.sharding import PartitionSpec as P

FINE = 5
MID = 3
COARSE = 2
CSWEEPS = 4
RADIUS = 15
HALO = 16
OWN = 4
WINDOW = OWN + 2 * RADIUS
SPLIT = WINDOW // 2
EX = 4
EY = 16
HALF = EY // 2
LANES = 128

f32 = jnp.float32
bf16 = jnp.bfloat16
HIGHEST = lax.Precision.HIGHEST
MIB = 1 << 20


def gll_points(points):
    if points == 5:
        return np.array([-1.0, -math.sqrt(3.0 / 7.0), 0.0, math.sqrt(3.0 / 7.0), 1.0])
    if points == 3:
        return np.array([-1.0, 0.0, 1.0])
    return np.array([-1.0, 1.0])


def lagrange(fine_points, coarse_points):
    fine_nodes = gll_points(fine_points)
    coarse_nodes = gll_points(coarse_points)
    table = np.ones((fine_points, coarse_points))
    for column in range(coarse_points):
        for other in range(coarse_points):
            if other != column:
                table[:, column] *= (fine_nodes - coarse_nodes[other]) / (
                    coarse_nodes[column] - coarse_nodes[other]
                )
    return table


def halves(table):
    table = np.asarray(table, np.float32)
    hi = table.astype(jnp.bfloat16)
    lo = (table - hi.astype(np.float32)).astype(jnp.bfloat16)
    return np.concatenate([hi, lo], axis=1)


def transfer_tables():
    fine_mid = np.kron(np.kron(lagrange(5, 3), lagrange(5, 3)), lagrange(5, 3))
    mid_coarse = np.kron(np.kron(lagrange(3, 2), lagrange(3, 2)), lagrange(3, 2))
    down, up = [], []
    for place in range(EX):
        table = np.zeros((LANES, LANES))
        table[:125, place * 32 : place * 32 + 27] = fine_mid
        down.append(halves(table))
        up.append(halves(table.T))
    middle = np.zeros((LANES, LANES), np.float32)
    for place in range(EX):
        middle[place * 32 : place * 32 + 27, place * 8 : place * 8 + 8] = mid_coarse
    low = [0.027 * middle]
    low += [0.5 * np.dot(move, middle) for move in exchanges(MID, True)]
    high = [np.roll(middle.T, 32 * copy, axis=0) for copy in range(3)]
    return np.stack(down), np.stack(up), np.stack(low), np.stack(high)


def iota(shape, dimension):
    return lax.broadcasted_iota(jnp.int32, shape, dimension)


def three_way(values):
    one = values.astype(bf16)
    rest = values - one.astype(f32)
    two = rest.astype(bf16)
    three = (rest - two.astype(f32)).astype(bf16)
    return jnp.concatenate([one, two, three], axis=0)


def place_of(lane, y):
    i, j, k = lane // (FINE * FINE), (lane // FINE) % FINE, lane % FINE
    return jnp.where(lane < FINE**3, k * LANES + i * 2 * FINE + y * FINE + j, -1)


def pack_body(core_ref, field_ref, scale_ref, own_ref, edge_ref, lines, turned, *, count_z):
    lines[...] = jnp.zeros_like(lines)
    for i in range(FINE):
        lines[i * 2 * FINE : (i + 1) * 2 * FINE, 0 : count_z * FINE] = field_ref[i]
    for part in range(lines.shape[1] // LANES):
        lanes = slice(part * LANES, (part + 1) * LANES)
        turned[lanes, :] = lines[:, lanes].T
    lane = iota((1, 2 * LANES), 1)
    place = place_of(lane % LANES, lane // LANES)
    table = jnp.where(iota((FINE * LANES, 2 * LANES), 0) == place, 1.0, 0.0).astype(bf16)
    values = [turned[pl.ds(k, count_z, stride=FINE), :] for k in range(FINE)]
    nodes = jnp.dot(
        three_way(jnp.concatenate(values, axis=1)), table, preferred_element_type=f32
    )
    nodes = nodes[0:count_z] + nodes[count_z : 2 * count_z] + nodes[2 * count_z : 3 * count_z]
    scale = scale_ref[0].T
    for y in range(2):
        own_ref[y] = nodes[:, y * LANES : (y + 1) * LANES] / scale[:, y : y + 1]
    start = pl.multiple_of(core_ref[0] * (count_z - HALO), HALO)
    for y in range(2):
        edge_ref[y] = own_ref[y, pl.ds(start, HALO), :]


def pack(core, field, scaling):
    count_z = scaling.shape[2]
    width = -(-count_z * FINE // LANES) * LANES

    def body(*refs):
        pack_body(*refs, count_z=count_z)

    vmem = pl.BlockSpec(memory_space=pltpu.VMEM)
    return pl.pallas_call(
        body,
        out_shape=(
            jax.ShapeDtypeStruct((2, count_z, LANES), f32),
            jax.ShapeDtypeStruct((2, HALO, LANES), f32),
        ),
        in_specs=[pl.BlockSpec(memory_space=pltpu.SMEM), vmem, vmem],
        out_specs=(vmem, vmem),
        scratch_shapes=[pltpu.VMEM((LANES, width), f32), pltpu.VMEM((width, LANES), f32)],
        compiler_params=pltpu.CompilerParams(vmem_limit_bytes=8 * MIB),
        name="pack",
    )(core, field, scaling)


def settle(halo):
    def body(in_ref, out_ref):
        out_ref[...] = in_ref[...]

    return pl.pallas_call(
        body,
        out_shape=jax.ShapeDtypeStruct(halo.shape, f32),
        cost_estimate=pl.CostEstimate(
            flops=2_000_000_000, bytes_accessed=20_000_000, transcendentals=0
        ),
        compiler_params=pltpu.CompilerParams(vmem_limit_bytes=8 * MIB),
        name="settle",
    )(halo)


def window_body(core_ref, own_ref, sibling_ref, halo_ref, out_ref, line, *, parts):
    count_z = own_ref.shape[1]
    for core in range(2):
        places = (HALO, HALO + count_z, 0) if core == 0 else (count_z, 0, 2 * count_z)

        @pl.when(core_ref[0] == core)
        def _(core=core, places=places):
            for ref, place in zip((own_ref, sibling_ref, halo_ref), places):
                line[:, place : place + ref.shape[1], :] = ref[...]
            first = HALO - RADIUS if core == 0 else SPLIT - RADIUS
            for part in range(parts):
                for y in range(2):
                    start = first + OWN * part
                    row = part * WINDOW + y * SPLIT
                    out_ref[row : row + SPLIT, :] = line[y, start : start + SPLIT, :]


def window(core, own, sibling, halo, parts):
    def body(*refs):
        window_body(*refs, parts=parts)

    vmem = pl.BlockSpec(memory_space=pltpu.VMEM)
    return pl.pallas_call(
        body,
        out_shape=jax.ShapeDtypeStruct((parts * WINDOW, LANES), f32),
        in_specs=[pl.BlockSpec(memory_space=pltpu.SMEM), vmem, vmem, vmem],
        out_specs=vmem,
        scratch_shapes=[pltpu.VMEM((2, 2 * own.shape[1] + HALO, LANES), f32)],
        compiler_params=pltpu.CompilerParams(vmem_limit_bytes=8 * MIB),
        name="window",
    )(core, own, sibling, halo)


def unpack_body(core_ref, back_ref, scale_ref, out_ref, turned, *, count_z):
    scale = scale_ref[0].T
    base = core_ref[0] * (2 * count_z)
    rows = [
        back_ref[pl.ds(base + y, count_z, stride=2), :] / scale[:, y : y + 1] for y in range(2)
    ]
    table = jnp.concatenate(
        [
            jnp.where(
                iota((LANES, FINE * LANES), 1) == place_of(iota((LANES, 1), 0), y), 1.0, 0.0
            )
            for y in range(2)
        ],
        axis=0,
    ).astype(bf16)
    spread = jnp.dot(
        three_way(jnp.concatenate(rows, axis=1)), table, preferred_element_type=f32
    )
    spread = spread[0:count_z] + spread[count_z : 2 * count_z] + spread[2 * count_z : 3 * count_z]
    for k in range(FINE):
        turned[pl.ds(k, count_z, stride=FINE), :] = spread[:, k * LANES : (k + 1) * LANES]
    lines = [
        turned[part * LANES : (part + 1) * LANES, :].T for part in range(turned.shape[0] // LANES)
    ]
    lines = jnp.concatenate(lines, axis=1)
    for i in range(FINE):
        out_ref[i] = lines[i * 2 * FINE : (i + 1) * 2 * FINE, 0 : count_z * FINE]


def unpack(core, back, scaling, shape):
    count_z = scaling.shape[2]
    width = -(-count_z * FINE // LANES) * LANES

    def body(*refs):
        unpack_body(*refs, count_z=count_z)

    vmem = pl.BlockSpec(memory_space=pltpu.VMEM)
    return pl.pallas_call(
        body,
        out_shape=jax.ShapeDtypeStruct(shape, f32),
        in_specs=[pl.BlockSpec(memory_space=pltpu.SMEM), vmem, vmem],
        out_specs=vmem,
        scratch_shapes=[pltpu.VMEM((width, LANES), f32)],
        compiler_params=pltpu.CompilerParams(vmem_limit_bytes=8 * MIB),
        name="unpack",
    )(core, back, scaling)


def shifted_block(ref, pad, points):
    nodes = points**3
    pad[...] = jnp.zeros((LANES, LANES), f32)
    pad[0:nodes, 0:nodes] = ref[...]
    lane, row = iota((LANES, LANES), 1), iota((LANES, LANES), 0)
    count = jnp.zeros((LANES, LANES), f32)
    for stride in (points * points, points, 1):
        index = (lane // stride) % points
        count = count + jnp.where((index == 0) | (index == points - 1), 0.5, 0.0)
    diagonal = jnp.where(lane < nodes, count, 1.0)
    return pad[...] + jnp.where(lane == row, diagonal, 0.0)


def invert(matrix, panels):
    lane, row = iota((LANES, LANES), 1), iota((LANES, LANES), 0)
    lane1, lane16, row16 = iota((1, LANES), 1), iota((16, LANES), 1), iota((16, LANES), 0)
    for panel in range(panels):
        top = panel * 16
        rows = matrix[top : top + 16, :]
        for step in range(0, 16, 2):
            pivot = top + step
            left = jnp.broadcast_to(rows[:, pivot : pivot + 1], (16, LANES))
            right = jnp.broadcast_to(rows[:, pivot + 1 : pivot + 2], (16, LANES))
            a, b = left[step : step + 1], right[step : step + 1]
            c, d = left[step + 1 : step + 2], right[step + 1 : step + 2]
            scale = 1.0 / (a * d - b * c)
            here = (lane1 == pivot) | (lane1 == pivot + 1)
            one = jnp.where(here, jnp.where(lane1 == pivot, 1.0, 0.0), rows[step : step + 1])
            two = jnp.where(here, jnp.where(lane1 == pivot, 0.0, 1.0), rows[step + 1 : step + 2])
            one, two = (d * one - b * two) * scale, (a * two - c * one) * scale
            others = jnp.where((lane16 == pivot) | (lane16 == pivot + 1), 0.0, rows)
            others = others - left * one - right * two
            rows = jnp.where(row16 == step, one, jnp.where(row16 == step + 1, two, others))
        stacked = jnp.concatenate([rows] * 8, axis=0)
        inside = (lane >= top) & (lane < top + 16)
        update = jnp.dot(
            jnp.where(inside, matrix, 0.0), stacked, precision=HIGHEST, preferred_element_type=f32
        )
        matrix = jnp.where(
            (row >= top) & (row < top + 16), stacked, jnp.where(inside, 0.0, matrix) - update
        )
    return matrix


def exact(left, right):
    return jnp.dot(left, right, precision=HIGHEST, preferred_element_type=f32)


def repeated(matrix, width):
    lane, row = iota((LANES, LANES), 1), iota((LANES, LANES), 0)
    used = (lane < EX * width) & (row < EX * width)
    pick = jnp.where((row % width == lane) & (lane < width), 1.0, 0.0)
    put = jnp.where((lane % width == row) & (row < width), 1.0, 0.0)
    wide = exact(exact(pick, matrix), put)
    return jnp.where(used & (row // width == lane // width), wide, 0.0)


def moves(points, width):
    lane, row = iota((1, LANES), 1), iota((LANES, LANES), 0)
    local, place = lane % width, lane // width
    tables = []
    for dimension, stride in enumerate((points * points, points, 1)):
        index = (local // stride) % points
        first = (index == 0) & (local < points**3)
        last = (index == points - 1) & (local < points**3)
        reach = (points - 1) * stride
        if dimension == 0 and width < LANES:
            first, last = first & (place > 0), last & (place < EX - 1)
            reach = reach - width
        source = jnp.where(first, lane + reach, jnp.where(last, lane - reach, -LANES))
        tables.append((row, source))
    return tables


def inverses_body(fine_ref, mid_ref, coarse_ref, low_ref, high_ref, out_ref, pad):
    lane, row = iota((LANES, LANES), 1), iota((LANES, LANES), 0)
    coarse = invert(shifted_block(coarse_ref, pad, COARSE), 1)
    mid = invert(shifted_block(mid_ref, pad, MID), 2)
    fine = invert(shifted_block(fine_ref, pad, FINE), 8)
    levels = ((fine, FINE, LANES), (repeated(mid, 32), MID, 32))
    for level, (inverse, points, width) in enumerate(levels):
        inverse = 0.35 * inverse
        out_ref[4 * level] = two_way(inverse)
        moved = []
        for dimension, (own, source) in enumerate(moves(points, width)):
            moved.append(exact(jnp.where(own == source, 1.0, 0.0), inverse))
            out_ref[4 * level + 1 + dimension] = two_way(moved[dimension])
    lifted = 0.3 * high_ref[0]
    for dimension in range(3):
        lifted = lifted + exact(high_ref[dimension], moved[dimension])
    out_ref[8] = two_way(lifted)
    copies = jnp.where((lane % 32 == row) & (lane < 96), 1.0, 0.0)
    inverse = exact(0.35 * repeated(coarse, 8), copies)
    gather = jnp.zeros((LANES, LANES), f32)
    for dimension, (own, source) in enumerate(moves(COARSE, 8)):
        gather = gather + jnp.where((own == source + 32 * dimension) & (lane < 32), 1.0, 0.0)
    out_ref[9] = two_way(exact(gather, inverse))
    for part in range(4):
        out_ref[10 + part] = two_way(exact(low_ref[part], 2.0 * inverse))


def inverses(block_fine, block_mid, block_coarse, low, high):
    return pl.pallas_call(
        inverses_body,
        out_shape=jax.ShapeDtypeStruct((14, LANES, 2 * LANES), bf16),
        scratch_shapes=[pltpu.VMEM((LANES, LANES), f32)],
        compiler_params=pltpu.CompilerParams(vmem_limit_bytes=8 * MIB),
        cost_estimate=pl.CostEstimate(
            flops=2_000_000_000, bytes_accessed=20_000_000, transcendentals=0
        ),
        name="inverses",
    )(block_fine, block_mid, block_coarse, low, high)


def two_way(values):
    hi = values.astype(bf16)
    lo = (values - hi.astype(f32)).astype(bf16)
    return jnp.concatenate([hi, lo], axis=1)


def times(values, *tables):
    values = jnp.concatenate([two_way(value) for value in values], axis=1)
    stack = []
    for table in tables:
        high = table[:, 0:LANES]
        stack += [table, jnp.concatenate([high, jnp.zeros_like(high)], axis=1)]
    result = jnp.dot(values, jnp.concatenate(stack, axis=0), preferred_element_type=f32)
    return result[:, 0:LANES] + result[:, LANES : 2 * LANES]


def exchanges(points, in_lanes):
    nodes = points**3
    tables = []
    for dimension, stride in enumerate((points * points, points, 1)):
        table = np.zeros((LANES, LANES), np.float32)
        for place in range(EX if in_lanes else 1):
            for node in range(nodes):
                index = (node // stride) % points
                for end, step in ((0, -1), (points - 1, 1)):
                    if index != end:
                        continue
                    source = place * 32 + node - step * (points - 1) * stride
                    if dimension == 0 and in_lanes:
                        if not 0 <= place + step < EX:
                            continue
                        source += step * 32
                    table[source, place * 32 + node] = 1.0
        tables.append(table)
    return tables


class Faces:
    def __init__(self, points, in_lanes):
        lane, row = iota((EY, LANES), 1), iota((EY, LANES), 0)
        local = lane % 32 if in_lanes else lane
        self.masks = []
        for dimension, stride in enumerate((points * points, points, 1)):
            index = (local // stride) % points
            first, last = index == 0, index == points - 1
            if dimension == 1:
                self.masks.append((last & (row > 0), first & (row < EY - 1)))
            else:
                self.masks.append((last, first))

    def moved(self, dimension, faces):
        reach = (FINE - 1) * FINE ** (2 - dimension)
        lane = iota((1, LANES), 1)
        index = (lane // FINE ** (2 - dimension)) % FINE
        node = lane < FINE**3
        order = jnp.where((index == 0) & node, lane + reach, LANES - 1)
        order = jnp.where((index == FINE - 1) & node, lane - reach, order)
        turned = jnp.take_along_axis(
            faces, jnp.broadcast_to(order, faces.shape), axis=1, mode="promise_in_bounds"
        )
        return jnp.where(order < LANES - 1, turned, 0.0)

    def select(self, dimension, before, after):
        from_before, from_after = self.masks[dimension]
        if before is None:
            before, after = 0.0, flat_slabs(after)
        elif after is None:
            before, after = flat_slabs(before), 0.0
        else:
            before, after = flat_slabs(before), flat_slabs(after)
        if dimension == 1:
            after = jnp.where(from_after[None], after, 0.0)
        return flat(jnp.where(from_before[None], before, after))


def coarse_rows():
    lane, row = iota((EY, LANES), 1), iota((EY, LANES), 0)
    copy, j, k = lane // 32, (lane // 2) % 2, lane % 2
    masks = (
        copy == 0,
        (copy == 1) & (j == 1) & (row > 0),
        (copy == 1) & (j == 0) & (row < EY - 1),
        (copy == 2) & (k == 1),
        (copy == 2) & (k == 0),
    )

    def build(*parts):
        result = 0.0
        for mask, part in zip(masks, parts):
            result = jnp.where(mask[None], flat_slabs(part), result)
        return flat(result)

    return build


def flat_slabs(values):
    return values.reshape(-1, EY, LANES)


CHUNK = 16


def cuts(start, stop, chunk=CHUNK):
    count = -(-(stop - start) // chunk)
    edges = [start + (stop - start) * piece // count for piece in range(count + 1)]
    return list(zip(edges[:-1], edges[1:]))


def flat(values):
    return values.reshape(-1, LANES)


def beside(ref, rows):
    before = jnp.concatenate([ref[rows, HALF - 1 : EY - 1, :], ref[rows, 0:HALF, :]], axis=1)
    after = jnp.concatenate([ref[rows, HALF:EY, :], ref[rows, 1 : HALF + 1, :]], axis=1)
    return flat(before), flat(after)


def cycle_body(
    bounds_ref,
    mine_ref,
    other_ref,
    tables_ref,
    down_ref,
    up_ref,
    out_ref,
    start,
    ping,
    pong,
    left,
    left_x,
    left_y,
    left_z,
    mid_start,
    mid_ping,
    mid_pong,
    mid_left,
    mid_left_x,
    mid_left_y,
    mid_left_z,
    mask,
):
    lefts = (left_x, left_y, left_z)
    mid_lefts = (mid_left_x, mid_left_y, mid_left_z)
    fine_faces = Faces(FINE, False)
    mid_faces = Faces(MID, True)
    coarse_row = coarse_rows()
    fine_table, *fine_tables = [tables_ref[i] for i in range(4)]
    mid_table, *mid_tables = [tables_ref[i] for i in range(4, 8)]
    lift_table, coarse_table, *low_tables = [tables_ref[i] for i in range(8, 14)]

    slab = iota((WINDOW, EY, LANES), 0)
    mask[...] = jnp.where((slab >= bounds_ref[0]) & (slab < bounds_ref[1]), 1.0, 0.0)
    upper_is_mine = bounds_ref[2] == 1

    def at(x, a, b):
        return slice(x * WINDOW + a, x * WINDOW + b)

    def get(ref, rows):
        return flat(ref[rows, :, :])

    def put(ref, rows, values):
        ref[rows, :, :] = values.reshape(-1, EY, LANES)

    def fine_gather(ref, x, a, b):
        return (
            fine_faces.select(
                0,
                get(ref, at(x - 1, a, b)) if x > 0 else None,
                get(ref, at(x + 1, a, b)) if x < EX - 1 else None,
            ),
            fine_faces.select(1, *beside(ref, at(x, a, b))),
            fine_faces.select(2, get(ref, at(x, a - 1, b - 1)), get(ref, at(x, a + 1, b + 1))),
        )

    def fine_sweep(source, target, a, b, keep):
        for x in range(EX):
            for c, d in cuts(a, b):
                rows = at(x, c, d)
                faces = fine_gather(source, x, c, d)
                if keep is not None:
                    for ref, face in zip(lefts, faces):
                        if keep[0]:
                            put(ref, rows, keep[1] * face)
                        else:
                            put(ref, rows, get(ref, rows) + keep[1] * face)
                moved = 0.3 * get(source, rows) + get(start, rows) + times(faces, *fine_tables)
                put(target, rows, moved * get(mask, at(0, c, d)))

    for x in range(EX):
        for c, d in cuts(0, WINDOW):
            values = []
            for z in range(c, d):
                for y in range(2):
                    first = x * HALF * WINDOW + y * SPLIT + z % SPLIT
                    place = pl.ds(first, HALF, stride=WINDOW)
                    mine, other = mine_ref[place, :], other_ref[place, :]
                    if z < SPLIT:
                        mine, other = other, mine
                    values.append(jnp.where(upper_is_mine, mine, other))
            values = jnp.concatenate(values, axis=0)
            rows = at(x, c, d)
            put(left, rows, values)
            put(start, rows, 2.0 * times((values,), fine_table))

    fine_sweep(start, ping, 1, WINDOW - 1, (True, -0.21))
    fine_sweep(ping, pong, 2, WINDOW - 2, (False, -0.7))

    def mid_gather(faces, ref, a, b):
        here = get(ref, at(0, a, b))
        return (
            here,
            faces.select(1, *beside(ref, at(0, a, b))),
            faces.select(2, get(ref, at(0, a - 1, b - 1)), get(ref, at(0, a + 1, b + 1))),
        )

    for c, d in cuts(3, WINDOW - 3):
        values = []
        for x in range(EX):
            rest = 0.027 * get(left, at(x, c, d))
            for dimension, face in enumerate(fine_gather(pong, x, c, d)):
                face = 0.5 * (get(lefts[dimension], at(x, c, d)) + face)
                rest = rest + fine_faces.moved(dimension, face)
            values.append(rest)
        tables = [down_ref[x] for x in range(EX)]
        rows = at(0, c, d)
        total = times(values, *tables) * get(mask, rows)
        put(mid_left, rows, total)
        put(mid_start, rows, 2.0 * times((total,), mid_table))

    def mid_sweep(faces, tables, base, source, target, margin, keep=None):
        for c, d in cuts(margin, WINDOW - margin, CHUNK // 2):
            rows = at(0, c, d)
            values = mid_gather(faces, source, c, d)
            if keep is not None:
                for ref, face in zip(mid_lefts, values):
                    if keep[0]:
                        put(ref, rows, keep[1] * face)
                    else:
                        put(ref, rows, get(ref, rows) + keep[1] * face)
            moved = 0.3 * get(source, rows) + get(base, rows) + times(values, *tables)
            put(target, rows, moved * get(mask, rows))

    mid_sweep(mid_faces, mid_tables, mid_start, mid_start, mid_ping, 4, (True, -0.21))
    mid_sweep(mid_faces, mid_tables, mid_start, mid_ping, mid_pong, 5, (False, -0.7))

    base = ping.at[0:WINDOW]
    even = ping.at[WINDOW : 2 * WINDOW]
    odd = ping.at[2 * WINDOW : 3 * WINDOW]
    for c, d in cuts(6, WINDOW - 6):
        rows = at(0, c, d)
        faces = mid_gather(mid_faces, mid_pong, c, d)
        values = [get(mid_left, rows)]
        for ref, face in zip(mid_lefts, faces):
            values.append(get(ref, rows) + face)
        put(base, rows, times(values, *low_tables) * get(mask, rows))

    for c, d in cuts(10, WINDOW - 10, CHUNK // 2):
        rows = at(0, c, d)
        moved = times(mid_gather(mid_faces, mid_pong, c, d), *mid_tables)
        put(mid_left, rows, 0.3 * get(mid_pong, rows) + get(mid_start, rows) + moved)

    def coarse_gather(ref, a, b):
        rows = at(0, a, b)
        near = beside(ref, rows)
        return coarse_row(
            get(ref, rows), *near, get(ref, at(0, a - 1, b - 1)), get(ref, at(0, a + 1, b + 1))
        )

    def coarse_sweep(source, target, margin):
        for c, d in cuts(margin, WINDOW - margin, CHUNK // 2):
            rows = at(0, c, d)
            moved = times((coarse_gather(source, c, d),), coarse_table)
            moved = 0.3 * get(source, rows) + get(base, rows) + moved
            put(target, rows, moved * get(mask, rows))

    coarse_sweep(base, even, 7)
    coarse_sweep(even, odd, 8)
    coarse_sweep(odd, even, 9)

    for c, d in cuts(10, WINDOW - 10, CHUNK // 2):
        rows = at(0, c, d)
        moved = get(mid_left, rows) + times((coarse_gather(even, c, d),), lift_table)
        put(mid_ping, rows, moved * get(mask, rows))
    mid_sweep(mid_faces, mid_tables, mid_start, mid_ping, mid_pong, 11)
    mid_sweep(mid_faces, mid_tables, mid_start, mid_pong, mid_ping, 12)

    lifted = get(mid_ping, at(0, 12, WINDOW - 12))
    for x in range(EX):
        rows = at(x, 12, WINDOW - 12)
        put(pong, rows, get(pong, rows) + times((lifted,), up_ref[x]))
    fine_sweep(pong, ping, 13, WINDOW - 13, None)
    fine_sweep(ping, pong, 14, WINDOW - 14, None)
    fine_sweep(pong, ping, RADIUS, WINDOW - RADIUS, None)

    for x in range(EX):
        for z in range(OWN):
            for y in range(2):
                values = ping[x * WINDOW + RADIUS + z, y * HALF : (y + 1) * HALF, :]
                first = x * HALF * OWN * 2 + z * 2 + y
                out_ref[pl.ds(first, HALF, stride=2 * OWN), :] = values


def cycle(bounds, mine, other, tables, down, up):
    big = pltpu.VMEM((EX * WINDOW, EY, LANES), f32)
    small = pltpu.VMEM((WINDOW, EY, LANES), f32)
    vmem = pl.BlockSpec(memory_space=pltpu.VMEM)
    def body(bounds_ref, *refs):
        @pl.when(bounds_ref[3] == 1)
        def _():
            cycle_body(bounds_ref, *refs)

        @pl.when(bounds_ref[3] == 0)
        def _():
            refs[5][...] = jnp.zeros_like(refs[5])

    return pl.pallas_call(
        body,
        out_shape=jax.ShapeDtypeStruct((EX * HALF * 2 * OWN, LANES), f32),
        in_specs=[pl.BlockSpec(memory_space=pltpu.SMEM)] + [vmem] * 5,
        out_specs=vmem,
        scratch_shapes=[big] * 7 + [small] * 8,
        compiler_params=pltpu.CompilerParams(vmem_limit_bytes=20 * MIB),
        name="cycle",
    )(bounds, mine, other, tables, down, up)


def per_device(fine_source_field, scaling, block_fine, block_mid, block_coarse):
    count_z = scaling.shape[2]
    parts = lax.axis_size("gx") * lax.axis_size("gy")
    groups = lax.axis_size("gz")
    down, up, low, high = transfer_tables()
    group = lax.axis_index("gz")
    core = group % 2
    cores = core.astype(jnp.int32).reshape(1)

    own, edge = pack(cores, fine_source_field, scaling)
    ties = [(i, i + 1) for i in range(1, groups - 1, 2)]
    pairs = [(i, i ^ 1) for i in range(groups)]
    halo = settle(lax.ppermute(edge, "gz", ties + [(j, i) for i, j in ties]))
    sibling = lax.ppermute(own, "gz", pairs)
    chunks = window(cores, own, sibling, halo, parts)
    chunks, *matrices = lax.optimization_barrier((chunks, block_fine, block_mid, block_coarse))
    recv = lax.all_to_all(
        chunks.reshape(parts * WINDOW // 2, 2, LANES), ("gx", "gy"), 0, 0, tiled=True
    ).reshape(parts * WINDOW, LANES)
    recv, tables = lax.optimization_barrier((recv, inverses(*matrices, low, high)))
    wide = lax.axis_size("gx")
    ways = [
        (x * groups + i, x * groups + (i ^ 1))
        for x in range(wide)
        for i in range(groups)
        if i % 2 == (1 if 2 * x < wide else 0)
    ]
    other = lax.ppermute(recv, ("gx", "gz"), ways)

    part = lax.axis_index("gx") * lax.axis_size("gy") + lax.axis_index("gy")
    first = (group - core) * count_z + OWN * part - RADIUS
    bounds = jnp.stack(
        [
            jnp.maximum(0, -first),
            jnp.minimum(WINDOW, groups * count_z - first),
            core,
            (core == part // (parts // 2)).astype(jnp.int32),
        ]
    )
    result = cycle(
        bounds.astype(jnp.int32), recv, other, tables, down, up
    )
    back = lax.all_to_all(
        result.reshape(parts, 2 * OWN, LANES), ("gx", "gy"), 0, 0, tiled=True
    ).reshape(parts * 2 * OWN, LANES)
    return unpack(cores, back, scaling, fine_source_field.shape)


def solution(mesh):
    in_specs = (P("gx", "gy", "gz"), P("gx", "gy", "gz"), P(), P(), P())
    out_specs = P("gx", "gy", "gz")
    return jax.shard_map(
        per_device, mesh=mesh, in_specs=in_specs, out_specs=out_specs, check_vma=False
    )
```
